32 devices in a mesh: dp: 4 (over x, core), atom: 8 (over z, y).
Axes of the slice: x: 2, y: 2, z: 4, core: 2. Of those that a mesh axis runs over, the one named last changes fastest.
Arguments:
- frac: float32 [3, 4096], P(None, ('dp', 'atom')), may hold values from 0 to 1, as said below
- species: int32 [4096], P(('dp', 'atom')), may hold values from 0 to 95
- neighbours: int32 [32, 4096], P(None, ('dp', 'atom')), may hold values from 0 to 191, as said below
- counts: int32 [4096], P(('dp', 'atom')), may hold values from 8 to 32, as said below
- shifts: int32 [3, 32, 4096], P(None, None, ('dp', 'atom')), may hold values from -1 to 1, as said below
- cell: float32 [4, 3, 3], P('dp'), may hold values from -0.4 to 211.2, as said below
- energy_ref: float32 [4], P('dp'), may hold values from -4 to 4
- embedding: float32 [96, 128], replicated, may hold values from -6 to 6
- radial_in: float32 [2, 64, 128], replicated, may hold values from -1.5 to 1.5
- radial_out: float32 [2, 128, 384], replicated, may hold values from -0.5 to 0.5
- scalar_mix: float32 [2, 128, 128], replicated, may hold values from -0.5 to 0.5
- vector_mix: float32 [2, 128, 128], replicated, may hold values from -0.5 to 0.5
- vector_gate: float32 [2, 128, 128], replicated, may hold values from -0.5 to 0.5
- readout_mid: float32 [128, 128], replicated, may hold values from -0.5 to 0.5
- readout_out: float32 [128], replicated, may hold values from -0.5 to 0.5
Outputs:
- energy: float32 [4], P('dp')
- forces: float32 [3, 4096], P(None, ('dp', 'atom'))
- stress: float32 [4, 3, 3], P('dp')
- embedding_grad: float32 [96, 128], replicated
- radial_in_grad: float32 [2, 64, 128], replicated
- radial_out_grad: float32 [2, 128, 384], replicated
- scalar_mix_grad: float32 [2, 128, 128], replicated
- vector_mix_grad: float32 [2, 128, 128], replicated
- vector_gate_grad: float32 [2, 128, 128], replicated
- readout_mid_grad: float32 [128, 128], replicated
- readout_out_grad: float32 [128], replicated
The draws below stay inside these ranges and needn't reach their ends.
Inputs may be any that keep to these rules, and one draw needn't show every extreme that they name: `frac`: each fractional coordinate of slab p's atoms along the first lattice vector lies in [p / 8, (p + 1) / 8); the other two lie in [0, 1). `neighbours`: A window row; atom i (local index within its slab) names rows i to i + 64 only. In every slab, slot 0 of the first atom names row 0 and slot 0 of the last atom names row 191. `counts`: in every slab the first atom has 32 used slots and the second 32 // 4. `shifts`: the first component is -1 exactly where slab 0 names a row below 32, +1 exactly where the last slab names a row from 160 on, else 0. `cell`: diagonal entries near 24 * 8, 12 and 12; off-diagonal entries small against them, so the determinant is positive.
All inputs are finite; a program needn't handle non-finite values.
Results may differ from the reference program's by a relative error of at most 0.0003.
Values sent between devices are 32-bit elements; how exact they have to be, the bound alone decides.
No kernel may reach another device: no remote copies, remote signals or barrier semaphores. Data moves between devices by JAX's collectives and lax.ppermute only.
A program may use at most 64 MiB of HBM per device.

```python
import math
import jax
import jax.numpy as jnp
import numpy as np
from jax import lax

C = 128
NB = 64
NSPEC = 96
K = 32
L = 2
BLOCK = 32
A_DEV = 128
HALO = 32
TOTAL = 4096
N_DP = 4
N_ATOM = 8


def grid_cells(key):
    cell_key = jax.random.fold_in(key, 5)
    return jax.random.randint(cell_key, (2, TOTAL), 0, 4).astype(jnp.int32)


def window_plan(key):
    cells = grid_cells(key)
    score_key = jax.random.fold_in(key, 7)
    span = 2 * HALO + 1
    index = jnp.arange(TOTAL, dtype=jnp.int32)
    local = index % A_DEV
    slab = index // A_DEV % N_ATOM
    cell_start = index // (A_DEV * N_ATOM) * (A_DEV * N_ATOM)
    offset = jnp.arange(span, dtype=jnp.int32) - HALO
    target = local[:, None] + offset[None, :]
    other_slab = (slab[:, None] + jnp.floor_divide(target, A_DEV)) % N_ATOM
    other = cell_start[:, None] + other_slab * A_DEV + jnp.remainder(target, A_DEV)
    delta = jnp.take(cells, other, axis=1) - cells[:, :, None]
    image = jnp.where(delta >= 2, -1, jnp.where(delta <= -2, 1, 0)).astype(jnp.int32)
    near = jnp.all(jnp.abs(delta + 4 * image) <= 1, axis=0).astype(jnp.int32)
    drawn = jax.random.randint(score_key, (TOTAL, span), 0, 65536).astype(jnp.int32)
    score = near * (1 << 27) + drawn * span + jnp.arange(span, dtype=jnp.int32)[None, :]
    picked = lax.top_k(score, K)[1].astype(jnp.int32)
    first_slot = jnp.where(local == 0, 0, jnp.where(local == A_DEV - 1, span - 1, picked[:, 0]))
    picked = jnp.concatenate([first_slot[:, None].astype(jnp.int32), picked[:, 1:]], axis=1)
    rows = (local[:, None] + picked).T.astype(jnp.int32)
    chosen = jnp.take_along_axis(image, picked[None, :, :], axis=2)
    return (rows, chosen.transpose(0, 2, 1).astype(jnp.int32))


def draw_frac(key, part):
    cells = grid_cells(key)
    key = jax.random.fold_in(key, 11)
    first_key, second_key = jax.random.split(key)
    index = jnp.arange(TOTAL, dtype=jnp.int32)
    slab = (index // A_DEV % N_ATOM).astype(jnp.float32)
    local = (index % A_DEV).astype(jnp.float32)
    jitter = jax.random.uniform(first_key, (TOTAL,), jnp.float32)
    first = (slab + (local + jitter) / A_DEV) / N_ATOM
    inside = jax.random.uniform(second_key, (2, TOTAL), jnp.float32, 0.25, 0.75)
    others = (cells.astype(jnp.float32) + inside) / 4.0
    return jnp.concatenate([first[None, :], others], axis=0).astype(jnp.float32)


def draw_neighbours(key, part):
    rows, chosen = window_plan(key)
    return rows


def draw_shifts(key, part):
    rows, chosen = window_plan(key)
    slab = jnp.arange(TOTAL, dtype=jnp.int32) // A_DEV % N_ATOM
    first = jnp.where((rows < HALO) & (slab[None, :] == 0), -1, jnp.where((rows >= A_DEV + HALO) & (slab[None, :] == N_ATOM - 1), 1, 0))
    return jnp.concatenate([first[None].astype(jnp.int32), chosen], axis=0).astype(jnp.int32)


def draw_counts(key, part):
    key = jax.random.fold_in(key, 41)
    drawn = jax.random.randint(key, (TOTAL,), K // 4, K + 1)
    local = jnp.arange(TOTAL, dtype=jnp.int32) % A_DEV
    return jnp.where(local == 0, K, jnp.where(local == 1, K // 4, drawn)).astype(jnp.int32)


def draw_cell(key, part):
    key = jax.random.fold_in(key, 51)
    first_key, second_key = jax.random.split(key)
    sides = jnp.array([24.0 * N_ATOM, 12.0, 12.0], jnp.float32)
    lengths = sides * (1.0 + 0.1 * jax.random.uniform(first_key, (N_DP, 3), jnp.float32))
    spread = 0.2
    tilt = spread * jax.random.uniform(second_key, (N_DP, 3, 3), jnp.float32, -1.0, 1.0)
    unit = jnp.eye(3, dtype=jnp.float32)
    return (unit[None] * lengths[:, :, None] + (1.0 - unit[None]) * tilt).astype(jnp.float32)


def place_ends(values, own_key, low, largest):
    index_at = [jax.random.randint(jax.random.fold_in(own_key, axis), (), 0, length) for axis, length in enumerate(values.shape)]
    main_axis = values.shape.index(max(values.shape))
    beside = index_at[:main_axis] + [(index_at[main_axis] + 1) % values.shape[main_axis]] + index_at[main_axis + 1:]
    return values.at[tuple(index_at)].set(low).at[tuple(beside)].set(largest)


def level_of(rng, dims, cuts, least, largest):
    factor_of, own = 1.0, jax.random.fold_in(rng, 6)
    for position, blocks in cuts:
        heights = jnp.exp(jax.random.uniform(jax.random.fold_in(own, position), (blocks,), jnp.float32, least / len(cuts), largest / len(cuts)))
        factor_of = factor_of * jnp.repeat(heights, dims[position] // blocks).reshape([-1 if axis == position else 1 for axis in range(len(dims))])
    return factor_of


def rank_table(count, skew):
    loads = [(1 << 20) // math.isqrt(grade ** skew) + 1 for grade in range(1, count + 1)]
    scale = 1 + sum(loads) // (1 << 30)
    return np.cumsum(np.array([max(1, weight // scale) for weight in loads]))


def ranked_ids(own_key, shape, count, slope):
    grid = rank_table(count, slope)
    lot = jax.random.randint(jax.random.fold_in(own_key, 1), shape, 0, int(grid[count - 1]))
    standing = jnp.searchsorted(jnp.asarray(grid, jnp.int32), lot, side="right")
    return jax.random.permutation(jax.random.fold_in(own_key, 2), count)[standing].astype(jnp.int32)


def bell_draw(key, dims, scale, most, cuts=(), held_as=jnp.bfloat16):
    values = jax.random.normal(key, dims, jnp.float32) * scale
    if len(cuts) > 0:
        values = level_of(key, dims, cuts, -0.22, 0.18) * values
    return jnp.clip(values, min=-most, max=most).astype(held_as)


def setup_inputs(seed: int = 0) -> dict:
    key_list = jax.random.split(jax.random.key(seed), 16)
    return {
        "frac": draw_frac(jax.random.fold_in(key_list[15], 71), 0),
        "species": place_ends(ranked_ids(key_list[1], (TOTAL,), NSPEC, 2), jax.random.fold_in(key_list[1], 3), 0, NSPEC - 1).astype(jnp.int32),
        "neighbours": draw_neighbours(jax.random.fold_in(key_list[15], 71), 0),
        "counts": draw_counts(jax.random.fold_in(key_list[15], 71), 0),
        "shifts": draw_shifts(jax.random.fold_in(key_list[15], 71), 0),
        "cell": draw_cell(jax.random.fold_in(key_list[15], 71), 0),
        "energy_ref": bell_draw(key_list[6], (N_DP,), 1.0, 4.0, ((0, 4),), jnp.float32),
        "embedding": bell_draw(key_list[7], (NSPEC, C), 1.0, 6.0, (), jnp.float32),
        "radial_in": bell_draw(key_list[8], (L, NB, C), (NB // 4) ** -0.5, 1.5, (), jnp.float32),
        "radial_out": bell_draw(key_list[9], (L, C, 3 * C), C ** -0.5, 0.5, (), jnp.float32),
        "scalar_mix": bell_draw(key_list[10], (L, C, C), C ** -0.5, 0.5, (), jnp.float32),
        "vector_mix": bell_draw(key_list[11], (L, C, C), C ** -0.5, 0.5, (), jnp.float32),
        "vector_gate": bell_draw(key_list[12], (L, C, C), C ** -0.5, 0.5, (), jnp.float32),
        "readout_mid": bell_draw(key_list[13], (C, C), C ** -0.5, 0.5, (), jnp.float32),
        "readout_out": bell_draw(key_list[14], (C,), C ** -0.5, 0.5, (), jnp.float32),
    }


HIGH = lax.Precision.HIGHEST

def edge_geometry(window_pos, neighbour_rows, image_shifts, lattice):
    atom_count = neighbour_rows.shape[1]
    halo_rows = (window_pos.shape[1] - atom_count) // 2
    far_end = jnp.take(window_pos, neighbour_rows, axis=1)
    near_end = window_pos[:, halo_rows:halo_rows + atom_count]
    image = jnp.einsum('akb,ac->ckb', image_shifts, lattice, precision=HIGH)
    return far_end - near_end[:, None, :] + image

def interact(layer_set, wide_rows, edge_set, neighbour_rows, slot_mask):
    radial_in, radial_out, scalar_mix, vector_mix, vector_gate = layer_set
    slot_count, atom_count = neighbour_rows.shape
    halo_rows = (wide_rows.shape[0] - atom_count) // 2
    block_count = atom_count // BLOCK
    width = wide_rows.shape[2]
    own_rows = wide_rows[halo_rows:halo_rows + atom_count]
    block_inputs = (neighbour_rows.reshape(slot_count, block_count, BLOCK).transpose(1, 0, 2), edge_set.reshape(3, slot_count, block_count, BLOCK).transpose(2, 0, 1, 3), slot_mask.reshape(slot_count, block_count, BLOCK).transpose(1, 0, 2), own_rows.reshape(block_count, BLOCK, own_rows.shape[1], width))
    scale = slot_count ** (-0.5)
    basis_count = radial_in.shape[0]
    centres = 8.0 * jnp.arange(basis_count, dtype=jnp.float32) / (basis_count - 1)
    sharpness = 0.5 * ((basis_count - 1) / 8.0) ** 2

    def one_block(inputs):
        rows, vectors, block_mask, own = inputs
        distance = jnp.sqrt(lax.optimization_barrier(jnp.sum(vectors * vectors, axis=0)) + 1.0)
        direction = vectors / distance
        radial_basis = jnp.exp(-sharpness * (distance[..., None] - centres) ** 2)
        hidden = jax.nn.silu(jnp.einsum('kbn,nc->kbc', radial_basis, radial_in, precision=HIGH))
        filters = jnp.einsum('kbc,cd->kbd', hidden, radial_out, precision=HIGH) * block_mask[..., None]
        filter_scalar = filters[..., :width]
        filter_vector = filters[..., width:2 * width]
        filter_direction = filters[..., 2 * width:]
        gathered = jnp.take(wide_rows, rows, axis=0)
        neighbour_scalar = gathered[:, :, 0, :]
        summed_scalar = lax.optimization_barrier(jnp.sum(filter_scalar * neighbour_scalar, axis=0)) * scale
        message = (filter_direction * neighbour_scalar)[:, :, None, :] * direction.transpose(1, 2, 0)[..., None]
        if gathered.shape[2] > 1:
            message = message + filter_vector[:, :, None, :] * gathered[:, :, 1:, :]
        summed_vector = lax.optimization_barrier(jnp.sum(message, axis=0)) * scale
        mixed_vector = jnp.einsum('bjc,cd->bjd', summed_vector, vector_mix, precision=HIGH)
        magnitude = jnp.sqrt(lax.optimization_barrier(jnp.sum(mixed_vector * mixed_vector, axis=1)) + 1.0) - 1.0
        new_scalar = own[:, 0, :] + jax.nn.silu(jnp.dot(summed_scalar, scalar_mix, precision=HIGH) + magnitude)
        gate = jax.nn.sigmoid(jnp.dot(summed_scalar, vector_gate, precision=HIGH))
        if own.shape[1] > 1:
            old_vector = own[:, 1:, :]
        else:
            old_vector = jnp.zeros(mixed_vector.shape, jnp.float32)
        new_vector = old_vector + mixed_vector * gate[:, None, :]
        return jnp.concatenate([new_scalar[:, None, :], new_vector], axis=1)
    result = lax.map(jax.checkpoint(one_block), block_inputs)
    return result.reshape(atom_count, 4, width)

def readout(readout_mid, readout_out, features):
    hidden = jax.nn.silu(jnp.dot(features[:, 0, :], readout_mid, precision=HIGH))
    return jnp.sum(jnp.dot(hidden, readout_out, precision=HIGH))

def determinant(lattice):
    return lattice[0, 0] * (lattice[1, 1] * lattice[2, 2] - lattice[1, 2] * lattice[2, 1]) - lattice[0, 1] * (lattice[1, 0] * lattice[2, 2] - lattice[1, 2] * lattice[2, 0]) + lattice[0, 2] * (lattice[1, 0] * lattice[2, 1] - lattice[1, 1] * lattice[2, 0])

def extend(slabs, axis):
    size = slabs.shape[axis]
    below = jnp.roll(slabs, 1, axis=0)
    above = jnp.roll(slabs, -1, axis=0)
    lower_rows = lax.slice_in_dim(below, size - HALO, size, axis=axis)
    upper_rows = lax.slice_in_dim(above, 0, HALO, axis=axis)
    return jnp.concatenate([lower_rows, slabs, upper_rows], axis=axis)

def reference(frac, species, neighbours, counts, shifts, cell, energy_ref, embedding, radial_in, radial_out, scalar_mix, vector_mix, vector_gate, readout_mid, readout_out):
    weight_set = (embedding, radial_in, radial_out, scalar_mix, vector_mix, vector_gate, readout_mid, readout_out)
    cell_atoms = A_DEV * N_ATOM
    group_inputs = (frac.reshape(3, N_DP, cell_atoms).transpose(1, 0, 2), species.reshape(N_DP, cell_atoms), neighbours.reshape(K, N_DP, cell_atoms).transpose(1, 0, 2), counts.reshape(N_DP, cell_atoms), shifts.astype(jnp.float32).reshape(3, K, N_DP, cell_atoms).transpose(2, 0, 1, 3), cell)

    def group_terms(inputs):
        frac_one, species_one, neighbour_one, count_one, shift_one, lattice = inputs
        positions = jnp.dot(lattice.T, frac_one, precision=HIGH)
        slot_mask = (lax.broadcasted_iota(jnp.int32, (K, cell_atoms), 0) < count_one[None, :]).astype(jnp.float32)
        one_hot = (species_one[:, None] == lax.broadcasted_iota(jnp.int32, (1, NSPEC), 1)).astype(jnp.float32)
        neighbour_slabs = neighbour_one.reshape(K, N_ATOM, A_DEV).transpose(1, 0, 2)
        mask_slabs = slot_mask.reshape(K, N_ATOM, A_DEV).transpose(1, 0, 2)
        shift_slabs = shift_one.reshape(3, K, N_ATOM, A_DEV).transpose(2, 0, 1, 3)

        def energy_fn(weights, positions, strain):
            slabs = positions.reshape(3, N_ATOM, A_DEV).transpose(1, 0, 2)
            wide_pos = extend(slabs, 2)
            vectors = jax.vmap(edge_geometry, in_axes=(0, 0, 0, None))(wide_pos, neighbour_slabs, shift_slabs, lattice)
            vectors = jnp.einsum('pakb,ac->pckb', vectors, jnp.eye(3, dtype=jnp.float32) + strain, precision=HIGH)
            features = jnp.dot(one_hot, weights[0], precision=HIGH).reshape(N_ATOM, A_DEV, 1, weights[0].shape[1])
            for layer_index in range(L):
                layer_set = tuple((w[layer_index] for w in weights[1:6]))
                wide_features = extend(features, 1)
                features = jax.vmap(interact, in_axes=(None, 0, 0, 0, 0))(layer_set, wide_features, vectors, neighbour_slabs, mask_slabs)
            parts = jax.vmap(readout, in_axes=(None, None, 0))(weights[6], weights[7], features)
            return jnp.sum(parts)
        total, pull_back = jax.vjp(energy_fn, weight_set, positions, jnp.zeros((3, 3), jnp.float32))
        grad_weights, grad_pos, grad_strain = pull_back(jnp.ones((), jnp.float32))
        return (total, -grad_pos, grad_strain / determinant(lattice), grad_weights)
    energies, force_groups, stress, grad_groups = lax.map(group_terms, group_inputs)
    loss_scale = 2.0 * (energies / cell_atoms - energy_ref) / cell_atoms
    grads = tuple((jnp.tensordot(loss_scale, g, axes=1, precision=HIGH) for g in grad_groups))
    forces = force_groups.transpose(1, 0, 2).reshape(3, N_DP * cell_atoms)
    return (energies, forces, stress, grads[0], grads[1], grads[2], grads[3], grads[4], grads[5], grads[6], grads[7])
```

```python
import functools

import jax
import jax.numpy as jnp
from jax import lax
from jax.experimental import pallas as pl
from jax.experimental.pallas import tpu as pltpu
from jax.sharding import PartitionSpec as P

F32 = jnp.float32
BF16 = jnp.bfloat16
LANES = 128
HALF = 64
FWD_ROWS = 2
BWD_ROWS = 2
VMEM_LIMIT = 50 * 1024 * 1024
G_ROWS = 992


def split(x):
    high = x.astype(BF16)
    return high, (x - high.astype(F32)).astype(BF16)


def mm(a, b):
    return lax.dot_general(a, b, (((1,), (0,)), ((), ())), preferred_element_type=F32)


def mm_nt(a, b):
    return lax.dot_general(a, b, (((1,), (1,)), ((), ())), preferred_element_type=F32)


def mm3(a, b):
    ah, al = split(a)
    bh, bl = split(b)
    return mm(ah, bh) + (mm(ah, bl) + mm(al, bh))


def mm3_nt(a, b):
    ah, al = split(a)
    bh, bl = split(b)
    return mm_nt(ah, bh) + (mm_nt(ah, bl) + mm_nt(al, bh))


def sigmoid(x):
    return 1.0 / (1.0 + jnp.exp(-x))


def lane_ids(rows):
    return lax.broadcasted_iota(jnp.int32, (rows, LANES), 1)


def twice(x, half):
    low = lane_ids(x.shape[0]) < HALF
    other = pltpu.roll(x, HALF, 1)
    return jnp.where(low, x, other) if half == 0 else jnp.where(low, other, x)


def folded(first, second):
    low = lane_ids(first.shape[0]) < HALF
    return jnp.where(low, first + pltpu.roll(first, HALF, 1), second + pltpu.roll(second, HALF, 1))


def windows(own, beside, halo):
    lane = lane_ids(own.shape[0])
    return jnp.where(lane < LANES - halo, own, beside), jnp.where(lane >= halo, own, beside)


def packed(parts, halo, tail):
    lane = lane_ids(parts[0].shape[0])
    out = None
    for q, x in enumerate(parts):
        turn = (halo * (q + 1) if tail else halo * q) % LANES
        x = pltpu.roll(x, turn, 1) if turn else x
        out = x if out is None else jnp.where(lane < halo * q, out, x)
    return out


def unpacked(pack, q, halo, tail):
    turn = (LANES - halo * (q + 1) if tail else LANES - halo * q) % LANES
    return pltpu.roll(pack, turn, 1) if turn else pack


def is_even(par_ref, shape):
    return (jnp.zeros(shape, jnp.int32) + par_ref[0]) == 0


def prepare_weights(rin_ref, rout_ref, ri4, ro3, groups):
    rh, rl = split(rin_ref[0])
    rows = jnp.concatenate([rh, rh, rl, rl], axis=0).astype(F32)
    ri4[...] = rows.T.astype(BF16)
    wh, wl = split(rout_ref[0])
    for place, g in enumerate(groups):
        cols = slice(g * LANES, (g + 1) * LANES)
        th = wh[:, cols].astype(F32).T.astype(BF16)
        tl = wl[:, cols].astype(F32).T.astype(BF16)
        out = slice(place * LANES, (place + 1) * LANES)
        ro3[out, 0:LANES] = th
        ro3[out, LANES : 2 * LANES] = th
        ro3[out, 2 * LANES : 3 * LANES] = tl


def prepare_back(rin_ref, rout_ref, rib, rob, groups):
    rh, rl = split(rin_ref[0])
    count = rh.shape[0]
    rib[0:count, 0:LANES] = rh
    rib[0:count, LANES:] = rh
    rib[count:, 0:LANES] = rl
    rib[count:, LANES:] = rl
    wh, wl = split(rout_ref[0])
    width = len(groups) * LANES
    for place, g in enumerate(groups):
        cols = slice(g * LANES, (g + 1) * LANES)
        for copy in range(2):
            out = slice(copy * width + place * LANES, copy * width + (place + 1) * LANES)
            rob[0:LANES, out] = wh[:, cols]
            rob[LANES:, out] = wl[:, cols]


def store_tables(tab, parts, besides, halo):
    for q, (own, beside) in enumerate(zip(parts, besides)):
        for h, table in enumerate(windows(own, beside, halo)):
            hi, lo = split(table)
            tab[h, q * LANES : (q + 1) * LANES, 0:LANES] = hi
            tab[h, q * LANES : (q + 1) * LANES, LANES:] = lo


def radial(rows, ri4, ro3, basis_count):
    sharpness = 0.5 * ((basis_count - 1) / 8.0) ** 2
    place = lax.broadcasted_iota(jnp.int32, (basis_count, LANES), 0).astype(F32)
    centres = 8.0 * place / (basis_count - 1)
    offsets = [g[3:4] - centres for g in rows]
    offset = jnp.concatenate(offsets, axis=1)
    basis = jnp.exp(-sharpness * offset * offset)
    bh, bl = split(basis)
    pre = mm(ri4[...], jnp.concatenate([bh, bl, bh, bl], axis=0))
    gate = sigmoid(pre)
    mask = jnp.concatenate([g[4:5] for g in rows], axis=1)
    hidden = pre * gate * mask
    hh, hl = split(hidden)
    filters = mm(ro3[...], jnp.concatenate([hh, hl, hh], axis=0))
    return offset, basis, bh, bl, pre, gate, mask, hidden, hh, hl, filters, sharpness


def one_hot_of(rows):
    place = lax.broadcasted_iota(jnp.int32, (LANES, LANES), 0).astype(F32)
    return jnp.concatenate(
        [jnp.where(place == g[5:6], 1.0, 0.0).astype(BF16) for g in rows], axis=1
    )


def part(x, group, q):
    return x[group * LANES : (group + 1) * LANES, q * LANES : (q + 1) * LANES]


def forward_edges(geom, tab, ri4, ro3, acc, basis_count, vectors):
    total = geom.shape[0]
    per_half = total // 2 // FWD_ROWS
    acc[...] = jnp.zeros(acc.shape, F32)
    wide = 2 if vectors else 1

    def step(t, carry):
        h = t // per_half
        rows = [geom[t * FWD_ROWS + q] for q in range(FWD_ROWS)]
        filters = radial(rows, ri4, ro3, basis_count)[10]
        hot = one_hot_of(rows)
        found = mm(tab[h], jnp.concatenate([hot, hot], axis=0))
        sums = [None] * 4
        for q, g in enumerate(rows):
            s = part(found, 0, q)
            terms = [part(filters, 0, q) * s]
            push = part(filters, wide, q) * s
            for c in range(3):
                term = push * g[c : c + 1]
                if vectors:
                    term = term + part(filters, 1, q) * part(found, 1 + c, q)
                terms.append(term)
            sums = [x if y is None else y + x for x, y in zip(terms, sums)]
        for n in range(4):
            acc[h, n] += sums[n]
        return carry

    lax.fori_loop(0, 2 * per_half, step, 0)


def aggregates(acc, scale):
    return [folded(acc[0, n], acc[1, n]) * scale for n in range(4)]


def node_forward(agg, sm, vm, vg):
    mixed = mm3(vm.T, jnp.concatenate(agg[1:], axis=1))
    w = [mixed[:, c * LANES : (c + 1) * LANES] for c in range(3)]
    size = jnp.sqrt(w[0] * w[0] + w[1] * w[1] + w[2] * w[2] + 1.0)
    u = mm3(sm.T, agg[0]) + (size - 1.0)
    gate = sigmoid(mm3(vg.T, agg[0]))
    return w, size, u, gate


def node_backward(agg, w, size, u, gate, sm, vm, vg, ds, dv, scale):
    act = sigmoid(u)
    du = ds * (act * (1.0 + u * (1.0 - act)))
    ratio = du / size
    dw = [w[c] * ratio + dv[c] * gate for c in range(3)]
    dq = (dv[0] * w[0] + dv[1] * w[1] + dv[2] * w[2]) * gate * (1.0 - gate)
    dw_all = jnp.concatenate(dw, axis=1)
    da_s = (mm3(sm, du) + mm3(vg, dq)) * scale
    da_v = mm3(vm, dw_all) * scale
    da = [da_s] + [da_v[:, c * LANES : (c + 1) * LANES] for c in range(3)]
    g_sm = mm3_nt(agg[0], du)
    g_vg = mm3_nt(agg[0], dq)
    g_vm = mm3_nt(jnp.concatenate(agg[1:], axis=1), dw_all)
    return da, g_sm, g_vm, g_vg


def backward_edges(geom, dgeom, tab, ri4, ro3, rib, rob, gacc, dro, dri, dtab, basis_count, vectors, finish):
    total = geom.shape[0]
    per_half = total // 2 // BWD_ROWS
    dro[...] = jnp.zeros(dro.shape, F32)
    dri[...] = jnp.zeros(dri.shape, F32)
    dtab[...] = jnp.zeros(dtab.shape, F32)
    wide = 2 if vectors else 1

    def step(t, carry):
        h = t // per_half
        rows = [geom[t * BWD_ROWS + q] for q in range(BWD_ROWS)]
        offset, basis, bh, bl, pre, gate, mask, hidden, hh, hl, filters, sharpness = radial(
            rows, ri4, ro3, basis_count
        )
        hot = one_hot_of(rows)
        found = mm(tab[h], jnp.concatenate([hot, hot], axis=0))
        d_filters, d_found, d_dirs = [], [], []
        gs = gacc[h, 0]
        gv = [gacc[h, 1 + c] for c in range(3)]
        for q, g in enumerate(rows):
            s = part(found, 0, q)
            along = gv[0] * g[0:1] + gv[1] * g[1:2] + gv[2] * g[2:3]
            f_s, f_d = part(filters, 0, q), part(filters, wide, q)
            groups = [gs * s]
            sources = [f_s * gs + f_d * along]
            if vectors:
                f_v = part(filters, 1, q)
                v = [part(found, 1 + c, q) for c in range(3)]
                groups.append(gv[0] * v[0] + gv[1] * v[1] + gv[2] * v[2])
                sources += [f_v * gv[c] for c in range(3)]
            groups.append(s * along)
            d_filters.append(jnp.concatenate(groups, axis=0))
            push = f_d * s
            d_dirs.append([jnp.sum(push * gv[c], axis=0, keepdims=True) for c in range(3)])
            d_found.append(jnp.concatenate(sources, axis=0))
        d_filter = jnp.concatenate(d_filters, axis=1)
        fh, fl = split(d_filter)
        both = jnp.concatenate([hh, hl], axis=0)
        dro[...] += mm_nt(jnp.concatenate([fh, fl], axis=1), jnp.concatenate([both, both], axis=1))
        spread = mm(rob[...], jnp.concatenate([fh, fl], axis=0))
        d_hidden = (spread[:LANES] + spread[LANES:]) * mask
        d_pre = d_hidden * (gate * (1.0 + pre * (1.0 - gate)))
        ph, plo = split(d_pre)
        bb = jnp.concatenate([bh, bl], axis=0)
        dri[...] += mm_nt(jnp.concatenate([ph, plo], axis=1), jnp.concatenate([bb, bb], axis=1))
        back = mm(rib[...], jnp.concatenate([ph, plo], axis=0))
        d_basis = back[:basis_count] + back[basis_count:]
        d_dist = jnp.sum(d_basis * basis * offset, axis=0, keepdims=True) * (-2.0 * sharpness)
        extra = []
        for q, g in enumerate(rows):
            extra.append(finish(t * BWD_ROWS + q, h, g, d_dirs[q], d_dist[:, q * LANES : (q + 1) * LANES]))
        if extra[0] is not None:
            d_found = [jnp.concatenate([a, b], axis=0) for a, b in zip(d_found, extra)]
        sh, sl = split(jnp.concatenate(d_found, axis=1))
        dtab[h] += mm_nt(jnp.concatenate([sh, sl], axis=1), jnp.concatenate([hot, hot], axis=1))
        return carry

    lax.fori_loop(0, 2 * per_half, step, 0)


def radial_grads(dro, dri, out, row_in, row_out, basis_count, groups):
    both = dri[...]
    turned = both + pltpu.roll(both, HALF, 1)
    out[row_in : row_in + basis_count] = turned.T[0:basis_count]
    for place, g in enumerate(groups):
        rows = slice(place * LANES, (place + 1) * LANES)
        grad = dro[rows, 0:LANES] + dro[rows, LANES:]
        out[row_out + g * LANES : row_out + (g + 1) * LANES] = grad.T


def species_hot(row, count):
    place = lax.broadcasted_iota(jnp.int32, (count, LANES), 0).astype(F32)
    return jnp.where(place == row, 1.0, 0.0).astype(BF16)


def first_features(emb_ref, hot):
    high, rest = split(emb_ref[...])
    low = (emb_ref[...] - high.astype(F32) - rest.astype(F32)).astype(BF16)
    dims = (((0,), (0,)), ((), ()))
    terms = [
        lax.dot_general(x.astype(F32).T.astype(BF16), hot, (((1,), (0,)), ((), ())), preferred_element_type=F32)
        for x in (high, rest, low)
    ]
    return terms[0] + (terms[1] + terms[2])


def from_sides(par_ref, a_ref, b_ref):
    even = is_even(par_ref, a_ref.shape)
    a, b = a_ref[...], b_ref[...]
    return jnp.where(even, a, b), jnp.where(even, b, a)


def species_tables(own_ref, up, down, emb_ref, halo):
    lane = lane_ids(1)
    count = emb_ref.shape[0]
    beside = jnp.where(lane >= LANES - halo, down[3:4], up[3:4])
    hot_own, hot_beside = species_hot(own_ref[3:4], count), species_hot(beside, count)
    return hot_own, hot_beside


def first_kernel(
    halo, par_ref, cell_ref, own_ref, a_ref, b_ref, nb_ref, count_ref, shift_ref, emb_ref, rin_ref, rout_ref,
    sm_ref, vm_ref, vg_ref,
    geom_ref, feat_ref, agg_ref, send_a, send_b,
    tab, ri4, ro3, acc,
):
    slots = nb_ref.shape[0]
    basis_count = rin_ref.shape[1]
    pairs = slots // 2
    up, down = from_sides(par_ref, a_ref, b_ref)
    lane = lane_ids(pairs)
    low = lane < HALF

    def halves(ref, *lead):
        even = ref[(*lead, pl.ds(0, pairs, stride=2), slice(None))]
        odd = ref[(*lead, pl.ds(1, pairs, stride=2), slice(None))]
        return jnp.where(low, even, pltpu.roll(odd, HALF, 1)), jnp.where(low, pltpu.roll(even, HALF, 1), odd)

    nb = halves(nb_ref)
    shift = [halves(shift_ref, a) for a in range(3)]
    row_slot = 2 * lax.broadcasted_iota(jnp.int32, (pairs, LANES), 0) + jnp.where(low, 0, 1)
    own = own_ref[...]
    lane8 = lane_ids(own.shape[0])
    places = (jnp.where(lane8 < LANES - halo, own, down), jnp.where(lane8 >= halo, own, up))
    for h in range(2):
        index = (nb[h] - halo) & (LANES - 1)
        near = twice(own, h)
        count = twice(count_ref[...], h)
        mask = jnp.where(row_slot < count, 1.0, 0.0).astype(F32)
        steps = [shift[a][h].astype(F32) for a in range(3)]
        r = []
        for c in range(3):
            table = jnp.broadcast_to(places[h][c : c + 1], (pairs, LANES))
            far = jnp.take_along_axis(table, index, axis=1, mode="promise_in_bounds")
            image = steps[0] * cell_ref[0, 0, c] + steps[1] * cell_ref[0, 1, c] + steps[2] * cell_ref[0, 2, c]
            r.append(far - near[c : c + 1] + image)
        dist = jnp.sqrt(r[0] * r[0] + r[1] * r[1] + r[2] * r[2] + 1.0)
        values = [x / dist for x in r] + [dist, mask, index.astype(F32)]
        for n, x in enumerate(values):
            for m in range(pairs):
                geom_ref[h * pairs + m, n : n + 1, :] = x[m : m + 1]
    hot_own, hot_beside = species_tables(own_ref, up, down, emb_ref, halo)
    s, beside = first_features(emb_ref, hot_own), first_features(emb_ref, hot_beside)
    store_tables(tab, [s], [beside], halo)
    prepare_weights(rin_ref, rout_ref, ri4, ro3, (0, 2))
    forward_edges(geom_ref, tab, ri4, ro3, acc, basis_count, False)
    agg = aggregates(acc, slots**-0.5)
    w, size, u, gate = node_forward(agg, sm_ref[0], vm_ref[0], vg_ref[0])
    features = [s + u * sigmoid(u)] + [w[c] * gate for c in range(3)]
    for n in range(4):
        agg_ref[n] = agg[n]
        feat_ref[n] = features[n]
    tail, head = packed(features, halo, True), packed(features, halo, False)
    even = is_even(par_ref, tail.shape)
    send_a[...] = jnp.where(even, tail, head)
    send_b[...] = jnp.where(even, head, tail)


def second_kernel(
    halo, par_ref, geom_ref, feat_ref, a_ref, b_ref, rin_ref, rout_ref, sm_ref, vm_ref, vg_ref, mid_ref, out_ref,
    energy_ref, cot_ref, send_a, send_b, dgeom_ref, grad_ref,
    tab, ri4, ro3, rib, rob, acc, gacc, dro, dri, dtab,
):
    basis_count = rin_ref.shape[1]
    slots = geom_ref.shape[0]
    scale = slots**-0.5
    up, down = from_sides(par_ref, a_ref, b_ref)
    lane = lane_ids(LANES)
    features = [feat_ref[n] for n in range(4)]
    besides = [
        jnp.where(lane >= LANES - halo, unpacked(down, q, halo, True), unpacked(up, q, halo, False)) for q in range(4)
    ]
    store_tables(tab, features, besides, halo)
    groups = (0, 1, 2)
    prepare_weights(rin_ref, rout_ref, ri4, ro3, groups)
    prepare_back(rin_ref, rout_ref, rib, rob, groups)
    forward_edges(geom_ref, tab, ri4, ro3, acc, basis_count, True)

    @pl.when(par_ref[0] >= 0)
    def _():
        agg = aggregates(acc, scale)
        sm, vm, vg = sm_ref[0], vm_ref[0], vg_ref[0]
        w, size, u, gate = node_forward(agg, sm, vm, vg)
        s = feat_ref[0] + u * sigmoid(u)
        mid = mid_ref[...]
        hidden = mm3(mid.T, s)
        act = sigmoid(hidden)
        shown = hidden * act
        weights = jnp.broadcast_to(out_ref[...], (8, LANES))
        per_atom = mm3(weights, shown)
        energy_ref[...] = jnp.broadcast_to(jnp.sum(per_atom, axis=1, keepdims=True), (8, LANES))
        weight_column = jnp.broadcast_to(out_ref[...], (LANES, LANES)).T
        d_hidden = weight_column * (act * (1.0 + hidden * (1.0 - act)))
        ds = mm3(mid, d_hidden)
        zero = jnp.zeros((LANES, LANES), F32)
        dv = [zero, zero, zero]
        da, g_sm, g_vm, g_vg = node_backward(agg, w, size, u, gate, sm, vm, vg, ds, dv, scale)
        for n in range(4):
            for h in range(2):
                gacc[h, n] = twice(da[n], h)
        for n, x in enumerate([ds] + dv):
            cot_ref[n] = x
        row = basis_count + 3 * LANES
        for grad in (g_sm, g_vm, g_vg, mm3_nt(s, d_hidden)):
            grad_ref[row : row + LANES] = grad
            row += LANES
        grad_ref[row : row + 8] = mm3_nt(jnp.ones((8, LANES), F32), shown)
        row += 8
        grad_ref[row:] = jnp.zeros((grad_ref.shape[0] - row, LANES), F32)

    def finish(row, h, g, d_dir, d_dist):
        for c in range(3):
            dgeom_ref[row, c : c + 1, :] = d_dir[c]
        dgeom_ref[row, 3:4, :] = d_dist
        return None

    backward_edges(
        geom_ref, dgeom_ref, tab, ri4, ro3, rib, rob, gacc, dro, dri, dtab, basis_count, True, finish
    )
    radial_grads(dro, dri, grad_ref, 0, basis_count, basis_count, groups)
    firsts = [dtab[0, q * LANES : (q + 1) * LANES] for q in range(4)]
    seconds = [dtab[1, q * LANES : (q + 1) * LANES] for q in range(4)]
    for q in range(4):
        cot_ref[q] += (
            jnp.where(lane < LANES - halo, firsts[q], 0.0) + jnp.where(lane >= halo, seconds[q], 0.0)
        )
    to_prev, to_next = packed(firsts, halo, True), packed(seconds, halo, False)
    even = is_even(par_ref, to_prev.shape)
    send_a[...] = jnp.where(even, to_next, to_prev)
    send_b[...] = jnp.where(even, to_prev, to_next)


def third_kernel(
    halo, par_ref, geom_ref, dgeom_ref, agg_ref, cot_ref, a_ref, b_ref, own_ref, pa_ref, pb_ref, emb_ref, rin_ref,
    rout_ref, sm_ref, vm_ref, vg_ref,
    force_ref, send_a, send_b, grad_ref,
    tab, ri4, ro3, rib, rob, gacc, dro, dri, dtab, pull, virial,
):
    basis_count = rin_ref.shape[1]
    slots = geom_ref.shape[0]
    scale = slots**-0.5
    lane = lane_ids(LANES)
    up, down = from_sides(par_ref, a_ref, b_ref)
    cot = []
    for q in range(4):
        cot.append(
            cot_ref[q]
            + jnp.where(lane >= LANES - halo, unpacked(up, q, halo, True), 0.0)
            + jnp.where(lane < halo, unpacked(down, q, halo, False), 0.0)
        )
    place_up, place_down = from_sides(par_ref, pa_ref, pb_ref)
    hot_own, hot_beside = species_tables(own_ref, place_up, place_down, emb_ref, halo)
    s, beside = first_features(emb_ref, hot_own), first_features(emb_ref, hot_beside)
    store_tables(tab, [s], [beside], halo)
    groups = (0, 2)
    prepare_weights(rin_ref, rout_ref, ri4, ro3, groups)
    prepare_back(rin_ref, rout_ref, rib, rob, groups)
    count = emb_ref.shape[0]

    @pl.when(par_ref[0] >= 0)
    def _():
        agg = [agg_ref[n] for n in range(4)]
        sm, vm, vg = sm_ref[0], vm_ref[0], vg_ref[0]
        w, size, u, gate = node_forward(agg, sm, vm, vg)
        da, g_sm, g_vm, g_vg = node_backward(agg, w, size, u, gate, sm, vm, vg, cot[0], cot[1:], scale)
        for n in range(4):
            for h in range(2):
                gacc[h, n] = twice(da[n], h)
        row = count + basis_count + 3 * LANES
        for g in (g_sm, g_vm, g_vg):
            grad_ref[row : row + LANES] = g
            row += LANES

    pull[...] = jnp.zeros(pull.shape, F32)
    virial[...] = jnp.zeros(virial.shape, F32)

    def finish(row, h, g, d_dir, d_dist):
        more = dgeom_ref[row]
        dist = g[3:4]
        toward = [g[c : c + 1] for c in range(3)]
        turn = [d_dir[c] + more[c : c + 1] for c in range(3)]
        inner = turn[0] * toward[0] + turn[1] * toward[1] + turn[2] * toward[2]
        stretch = d_dist + more[3:4]
        inverse = 1.0 / dist
        dr = [(turn[c] - toward[c] * inner) * inverse + stretch * toward[c] for c in range(3)]
        r = [toward[c] * dist for c in range(3)]
        lines = jnp.concatenate(dr + [jnp.zeros((13, LANES), F32)], axis=0)
        pull[h] += lines
        products = [r[a] * dr[c] for a in range(3) for c in range(3)]
        virial[...] += jnp.concatenate(products + [jnp.zeros((7, LANES), F32)], axis=0)
        return lines

    backward_edges(
        geom_ref, None, tab, ri4, ro3, rib, rob, gacc, dro, dri, dtab, basis_count, False, finish
    )
    first, second = dtab[0, 0:LANES], dtab[1, 0:LANES]
    own_cot = cot[0] + jnp.where(lane < LANES - halo, first, 0.0) + jnp.where(lane >= halo, second, 0.0)
    side_cot = jnp.where(lane >= LANES - halo, first, 0.0) + jnp.where(lane < halo, second, 0.0)
    grad = 0.0
    for hot, value in ((hot_own, own_cot), (hot_beside, side_cot)):
        hi, lo = split(value)
        grad = grad + (mm_nt(hot, hi) + mm_nt(hot, lo))
    grad_ref[0:count] = grad
    row = count
    radial_grads(dro, dri, grad_ref, row, row + basis_count, basis_count, groups)
    grad_ref[row + basis_count + LANES : row + basis_count + 2 * LANES] = jnp.zeros((LANES, LANES), F32)
    row += basis_count + 6 * LANES
    grad_ref[row:] = jnp.zeros((grad_ref.shape[0] - row, LANES), F32)
    total = jnp.broadcast_to(jnp.sum(virial[...], axis=1, keepdims=True), virial.shape)
    grad_ref[pl.ds(pl.multiple_of(row + 16 * par_ref[1], 16), 16)] = total
    lane16 = lane_ids(16)
    first, second = dtab[0, LANES:], dtab[1, LANES:]
    force_ref[...] = (
        jnp.where(lane16 < LANES - halo, first, 0.0)
        + jnp.where(lane16 >= halo, second, 0.0)
        - folded(pull[0], pull[1])
    )
    even = is_even(par_ref, first.shape)
    send_a[...] = jnp.where(even, second, first)
    send_b[...] = jnp.where(even, first, second)


def sides(a, b, axis):
    size = lax.axis_size(axis)
    pairs_a = [(i, i ^ 1) for i in range(size)]
    pairs_b = [(i, (i + 1) % size if i % 2 else (i - 1) % size) for i in range(size)]
    return lax.ppermute(a, axis, pairs_a), lax.ppermute(b, axis, pairs_b)


def swap(x, axis, bit):
    return lax.ppermute(x, axis, [(i, i ^ bit) for i in range(lax.axis_size(axis))])


def layer_spec(x, layer):
    rest = x.shape[1:]
    return pl.BlockSpec((1,) + rest, lambda i: (layer,) + (0,) * len(rest))


def vmem():
    return pl.BlockSpec(memory_space=pltpu.VMEM)


def smem():
    return pl.BlockSpec(memory_space=pltpu.SMEM)


def f32(*shape):
    return jax.ShapeDtypeStruct(shape, F32)


def params():
    return pltpu.CompilerParams(vmem_limit_bytes=VMEM_LIMIT)


def local(
    frac, species, neighbours, counts, shifts, cell, energy_ref, embedding, radial_in, radial_out, scalar_mix,
    vector_mix, vector_gate, readout_mid, readout_out,
):
    atom_count = frac.shape[1]
    halo = atom_count // 4
    slots = neighbours.shape[0]
    basis_count = radial_in.shape[1]
    me = lax.axis_index("atom")
    group = lax.axis_index("dp")
    lattice = cell[0]
    pos = lattice[0][:, None] * frac[0] + lattice[1][:, None] * frac[1] + lattice[2][:, None] * frac[2]
    own = jnp.concatenate([pos, species.astype(F32)[None], jnp.zeros((4, atom_count), F32)], axis=0)
    side_a, side_b = sides(own, own, "atom")
    par = jnp.stack([me % 2, group]).astype(jnp.int32)
    layer = (radial_in, radial_out, scalar_mix, vector_mix, vector_gate)
    block = f32(LANES, LANES)
    geom, feat, agg, feat_a, feat_b = pl.pallas_call(
        functools.partial(first_kernel, halo),
        grid=(1,),
        out_shape=(f32(slots, 8, LANES), f32(4, LANES, LANES), f32(4, LANES, LANES), block, block),
        in_specs=[smem(), smem()] + [vmem()] * 7 + [layer_spec(x, 0) for x in layer],
        out_specs=[vmem()] * 5,
        scratch_shapes=[
            pltpu.VMEM((2, LANES, 2 * LANES), BF16),
            pltpu.VMEM((LANES, 4 * basis_count), BF16),
            pltpu.VMEM((2 * LANES, 3 * LANES), BF16),
            pltpu.VMEM((2, 4, LANES, LANES), F32),
        ],
        compiler_params=params(),
        name="layer_one",
    )(par, cell, own, side_a, side_b, neighbours, counts[None], shifts, embedding, *layer)
    feat_a, feat_b = sides(feat_a, feat_b, "atom")
    energy_part, cot, cot_a, cot_b, dgeom, grads_two = pl.pallas_call(
        functools.partial(second_kernel, halo),
        grid=(1,),
        out_shape=(f32(8, LANES), f32(4, LANES, LANES), block, block, f32(slots, 8, LANES), f32(G_ROWS, LANES)),
        in_specs=[smem()] + [vmem()] * 4 + [layer_spec(x, 1) for x in layer] + [vmem()] * 2,
        out_specs=[vmem()] * 6,
        scratch_shapes=[
            pltpu.VMEM((2, 4 * LANES, 2 * LANES), BF16),
            pltpu.VMEM((LANES, 4 * basis_count), BF16),
            pltpu.VMEM((3 * LANES, 3 * LANES), BF16),
            pltpu.VMEM((2 * basis_count, 2 * LANES), BF16),
            pltpu.VMEM((2 * LANES, 6 * LANES), BF16),
            pltpu.VMEM((2, 4, LANES, LANES), F32),
            pltpu.VMEM((2, 4, LANES, LANES), F32),
            pltpu.VMEM((3 * LANES, 2 * LANES), F32),
            pltpu.VMEM((LANES, 2 * basis_count), F32),
            pltpu.VMEM((2, 4 * LANES, LANES), F32),
        ],
        compiler_params=params(),
        name="layer_two",
    )(par, geom, feat, feat_a, feat_b, *layer, readout_mid, readout_out[None])
    cot_a, cot_b = sides(cot_a, cot_b, "atom")
    force, force_a, force_b, grads_one = pl.pallas_call(
        functools.partial(third_kernel, halo),
        grid=(1,),
        out_shape=(f32(16, LANES), f32(16, LANES), f32(16, LANES), f32(G_ROWS, LANES)),
        in_specs=[smem()] + [vmem()] * 10 + [layer_spec(x, 0) for x in layer],
        out_specs=[vmem()] * 4,
        scratch_shapes=[
            pltpu.VMEM((2, LANES, 2 * LANES), BF16),
            pltpu.VMEM((LANES, 4 * basis_count), BF16),
            pltpu.VMEM((2 * LANES, 3 * LANES), BF16),
            pltpu.VMEM((2 * basis_count, 2 * LANES), BF16),
            pltpu.VMEM((2 * LANES, 4 * LANES), BF16),
            pltpu.VMEM((2, 4, LANES, LANES), F32),
            pltpu.VMEM((2 * LANES, 2 * LANES), F32),
            pltpu.VMEM((LANES, 2 * basis_count), F32),
            pltpu.VMEM((2, LANES + 16, LANES), F32),
            pltpu.VMEM((2, 16, LANES), F32),
            pltpu.VMEM((16, LANES), F32),
        ],
        compiler_params=params(),
        name="layer_one_back",
    )(par, geom, dgeom, agg, cot, cot_a, cot_b, own, side_a, side_b, embedding, *layer)
    bits = [1 << n for n in range((lax.axis_size("atom") - 1).bit_length())]
    energy = energy_part
    for bit in bits:
        energy = energy + swap(energy, "atom", bit)
    energy_total = energy[0, 0]
    cell_atoms = atom_count * lax.axis_size("atom")
    loss_scale = 2.0 * (energy_total / cell_atoms - energy_ref[0]) / cell_atoms
    force_a, force_b = sides(force_a, force_b, "atom")
    even = me % 2 == 0
    from_next, from_prev = jnp.where(even, force_a, force_b), jnp.where(even, force_b, force_a)
    lane = lax.broadcasted_iota(jnp.int32, (1, atom_count), 1)
    forces = -(
        force
        + jnp.where(lane >= atom_count - halo, from_next, 0.0)
        + jnp.where(lane < halo, from_prev, 0.0)
    )[:3]
    virial_row = embedding.shape[0] + basis_count + 6 * LANES
    is_virial = lax.broadcasted_iota(jnp.int32, (G_ROWS, 1), 0) >= virial_row
    one = grads_one * jnp.where(is_virial, 1.0, loss_scale)
    two = grads_two * loss_scale
    core = group % 2 == 1
    x = jnp.where(core, one, two) + swap(jnp.where(core, two, one), "dp", 1)
    high = group // 2 == 1
    low_part, high_part = x[: G_ROWS // 2], x[G_ROWS // 2 :]
    x = jnp.where(high, high_part, low_part) + swap(jnp.where(high, low_part, high_part), "dp", 2)
    for bit in bits:
        x = x + swap(x, "atom", bit)
    other = swap(x, "dp", 2)
    x = jnp.where(high, jnp.concatenate([other, x]), jnp.concatenate([x, other]))
    other = swap(x, "dp", 1)
    two, one = jnp.where(core, other, x), jnp.where(core, x, other)
    count = embedding.shape[0]
    virial = lax.dynamic_slice_in_dim(one, virial_row + 16 * group, 9, 0)[:, 0].reshape(3, 3)
    det = (
        lattice[0, 0] * (lattice[1, 1] * lattice[2, 2] - lattice[1, 2] * lattice[2, 1])
        - lattice[0, 1] * (lattice[1, 0] * lattice[2, 2] - lattice[1, 2] * lattice[2, 0])
        + lattice[0, 2] * (lattice[1, 0] * lattice[2, 1] - lattice[1, 1] * lattice[2, 0])
    )

    def cut(x, row, groups):
        return jnp.concatenate([x[row + g * LANES : row + (g + 1) * LANES] for g in range(groups)], axis=1)

    row_one, row_two = count + basis_count, basis_count
    mixes = [
        jnp.stack(
            [
                one[row_one + (3 + n) * LANES : row_one + (4 + n) * LANES],
                two[row_two + (3 + n) * LANES : row_two + (4 + n) * LANES],
            ]
        )
        for n in range(3)
    ]
    row = row_two + 6 * LANES
    return (
        energy_total.reshape(1),
        forces,
        (virial / det)[None],
        one[:count],
        jnp.stack([one[count:row_one], two[:row_two]]),
        jnp.stack([cut(one, row_one, 3), cut(two, row_two, 3)]),
        *mixes,
        two[row : row + LANES],
        two[row + LANES],
    )


def solution(mesh):
    both = ("dp", "atom")
    return jax.shard_map(
        local,
        mesh=mesh,
        in_specs=(
            P(None, both), P(both), P(None, both), P(both), P(None, None, both), P("dp", None, None), P("dp"),
        ) + (P(),) * 8,
        out_specs=(P("dp"), P(None, both), P("dp", None, None)) + (P(),) * 8,
        check_vma=False,
    )
```

```python
import functools

import jax
import jax.numpy as jnp
from jax import lax
from jax.experimental import pallas as pl
from jax.experimental.pallas import tpu as pltpu
from jax.sharding import PartitionSpec as P

F32 = jnp.float32
BF16 = jnp.bfloat16
LANES = 128
HALF = 64
FWD_ROWS = 16
BWD_ROWS = 16
VMEM_LIMIT = 50 * 1024 * 1024
G_ROWS = 928
MID_ROWS = 88


def split(x):
    high = x.astype(BF16)
    return high, (x - high.astype(F32)).astype(BF16)


def mm(a, b):
    return lax.dot_general(a, b, (((1,), (0,)), ((), ())), preferred_element_type=F32)


def mm_nt(a, b):
    return lax.dot_general(a, b, (((1,), (1,)), ((), ())), preferred_element_type=F32)


def mm3(a, b):
    ah, al = split(a)
    bh, bl = split(b)
    return mm(ah, bh) + (mm(ah, bl) + mm(al, bh))


def mm3_nt(a, b):
    ah, al = split(a)
    bh, bl = split(b)
    return mm_nt(ah, bh) + (mm_nt(ah, bl) + mm_nt(al, bh))


def sigmoid(x):
    return 0.5 * jnp.tanh(0.5 * x) + 0.5


def lane_ids(rows):
    return lax.broadcasted_iota(jnp.int32, (rows, LANES), 1)


def twice(x, half):
    low = lane_ids(x.shape[0]) < HALF
    other = pltpu.roll(x, HALF, 1)
    return jnp.where(low, x, other) if half == 0 else jnp.where(low, other, x)


def folded(first, second):
    low = lane_ids(first.shape[0]) < HALF
    return jnp.where(low, first + pltpu.roll(first, HALF, 1), second + pltpu.roll(second, HALF, 1))


def windows(own, beside, halo):
    lane = lane_ids(own.shape[0])
    return jnp.where(lane < LANES - halo, own, beside), jnp.where(lane >= halo, own, beside)


def packed(parts, halo, tail):
    lane = lane_ids(parts[0].shape[0])
    out = None
    for q, x in enumerate(parts):
        turn = (halo * (q + 1) if tail else halo * q) % LANES
        x = pltpu.roll(x, turn, 1) if turn else x
        out = x if out is None else jnp.where(lane < halo * q, out, x)
    return out


def unpacked(pack, q, halo, tail):
    turn = (LANES - halo * (q + 1) if tail else LANES - halo * q) % LANES
    return pltpu.roll(pack, turn, 1) if turn else pack


def is_even(par_ref, shape):
    return (jnp.zeros(shape, jnp.int32) + par_ref[0]) == 0


def prepare_weights(rin_ref, rout_ref, ri4, ro3, groups):
    rh, rl = split(rin_ref[0])
    rows = jnp.concatenate([rh, rh, rl, rl], axis=0).astype(F32)
    ri4[...] = rows.T.astype(BF16)
    wh, wl = split(rout_ref[0])
    for place, g in enumerate(groups):
        cols = slice(g * LANES, (g + 1) * LANES)
        th = wh[:, cols].astype(F32).T.astype(BF16)
        tl = wl[:, cols].astype(F32).T.astype(BF16)
        out = slice(place * LANES, (place + 1) * LANES)
        ro3[out, 0:LANES] = th
        ro3[out, LANES : 2 * LANES] = th
        ro3[out, 2 * LANES : 3 * LANES] = tl


def prepare_back(rin_ref, rout_ref, rib, rob, groups):
    rh, rl = split(rin_ref[0])
    count = rh.shape[0]
    rib[0:count, 0:LANES] = rh
    rib[0:count, LANES:] = rh
    rib[count:, 0:LANES] = rl
    rib[count:, LANES:] = rl
    wh, wl = split(rout_ref[0])
    width = len(groups) * LANES
    for place, g in enumerate(groups):
        cols = slice(g * LANES, (g + 1) * LANES)
        for copy in range(2):
            out = slice(copy * width + place * LANES, copy * width + (place + 1) * LANES)
            rob[0:LANES, out] = wh[:, cols]
            rob[LANES:, out] = wl[:, cols]


def store_tables(tab, parts, besides, halo):
    for q, (own, beside) in enumerate(zip(parts, besides)):
        for h, table in enumerate(windows(own, beside, halo)):
            hi, lo = split(table)
            tab[h, q * LANES : (q + 1) * LANES, 0:LANES] = hi
            tab[h, q * LANES : (q + 1) * LANES, LANES:] = lo


def radial(rows, ri4, ro3, basis_count):
    sharpness = 0.5 * ((basis_count - 1) / 8.0) ** 2
    place = lax.broadcasted_iota(jnp.int32, (basis_count, LANES), 0).astype(F32)
    centres = 8.0 * place / (basis_count - 1)
    offsets = [g[3:4] - centres for g in rows]
    offset = jnp.concatenate(offsets, axis=1)
    basis = jnp.exp(-sharpness * offset * offset)
    bh, bl = split(basis)
    pre = mm(ri4[...], jnp.concatenate([bh, bl, bh, bl], axis=0))
    gate = sigmoid(pre)
    mask = jnp.concatenate([g[4:5] for g in rows], axis=1)
    hidden = pre * gate * mask
    hh, hl = split(hidden)
    filters = mm(ro3[...], jnp.concatenate([hh, hl, hh], axis=0))
    return offset, basis, bh, bl, pre, gate, mask, hidden, hh, hl, filters, sharpness


def one_hot_of(rows):
    place = lax.broadcasted_iota(jnp.int32, (LANES, LANES), 0).astype(F32)
    return jnp.concatenate(
        [jnp.where(place == g[5:6], 1.0, 0.0).astype(BF16) for g in rows], axis=1
    )


def part(x, group, q):
    return x[group * LANES : (group + 1) * LANES, q * LANES : (q + 1) * LANES]


def forward_edges(geom, tab, ri4, ro3, acc, basis_count, vectors):
    total = geom.shape[0]
    per_half = total // 2 // FWD_ROWS
    acc[...] = jnp.zeros(acc.shape, F32)
    wide = 2 if vectors else 1

    def step(t, carry):
        h = t // per_half
        rows = [geom[t * FWD_ROWS + q] for q in range(FWD_ROWS)]
        filters = radial(rows, ri4, ro3, basis_count)[10]
        hot = one_hot_of(rows)
        found = mm(tab[h], jnp.concatenate([hot, hot], axis=0))
        sums = [None] * 4
        for q, g in enumerate(rows):
            s = part(found, 0, q)
            terms = [part(filters, 0, q) * s]
            push = part(filters, wide, q) * s
            for c in range(3):
                term = push * g[c : c + 1]
                if vectors:
                    term = term + part(filters, 1, q) * part(found, 1 + c, q)
                terms.append(term)
            sums = [x if y is None else y + x for x, y in zip(terms, sums)]
        for n in range(4):
            acc[h, n] += sums[n]
        return carry

    lax.fori_loop(0, 2 * per_half, step, 0)


def aggregates(acc, scale):
    return [folded(acc[0, n], acc[1, n]) * scale for n in range(4)]


def node_forward(agg, sm, vm, vg):
    mixed = mm3(vm.T, jnp.concatenate(agg[1:], axis=1))
    w = [mixed[:, c * LANES : (c + 1) * LANES] for c in range(3)]
    size = jnp.sqrt(w[0] * w[0] + w[1] * w[1] + w[2] * w[2] + 1.0)
    u = mm3(sm.T, agg[0]) + (size - 1.0)
    gate = sigmoid(mm3(vg.T, agg[0]))
    return w, size, u, gate


def node_backward(agg, w, size, u, gate, sm, vm, vg, ds, dv, scale):
    act = sigmoid(u)
    du = ds * (act * (1.0 + u * (1.0 - act)))
    ratio = du / size
    dw = [w[c] * ratio + dv[c] * gate for c in range(3)]
    dq = (dv[0] * w[0] + dv[1] * w[1] + dv[2] * w[2]) * gate * (1.0 - gate)
    dw_all = jnp.concatenate(dw, axis=1)
    da_s = (mm3(sm, du) + mm3(vg, dq)) * scale
    da_v = mm3(vm, dw_all) * scale
    da = [da_s] + [da_v[:, c * LANES : (c + 1) * LANES] for c in range(3)]
    g_sm = mm3_nt(agg[0], du)
    g_vg = mm3_nt(agg[0], dq)
    g_vm = mm3_nt(jnp.concatenate(agg[1:], axis=1), dw_all)
    return da, g_sm, g_vm, g_vg


def backward_edges(geom, dgeom, tab, ri4, ro3, rib, rob, gacc, dro, dri, dtab, basis_count, vectors, finish):
    total = geom.shape[0]
    per_half = total // 2 // BWD_ROWS
    dro[...] = jnp.zeros(dro.shape, F32)
    dri[...] = jnp.zeros(dri.shape, F32)
    dtab[...] = jnp.zeros(dtab.shape, F32)
    wide = 2 if vectors else 1

    def step(t, carry):
        h = t // per_half
        rows = [geom[t * BWD_ROWS + q] for q in range(BWD_ROWS)]
        offset, basis, bh, bl, pre, gate, mask, hidden, hh, hl, filters, sharpness = radial(
            rows, ri4, ro3, basis_count
        )
        hot = one_hot_of(rows)
        found = mm(tab[h], jnp.concatenate([hot, hot], axis=0))
        d_filters, d_found, d_dirs = [], [], []
        gs = gacc[h, 0]
        gv = [gacc[h, 1 + c] for c in range(3)]
        for q, g in enumerate(rows):
            s = part(found, 0, q)
            along = gv[0] * g[0:1] + gv[1] * g[1:2] + gv[2] * g[2:3]
            f_s, f_d = part(filters, 0, q), part(filters, wide, q)
            groups = [gs * s]
            sources = [f_s * gs + f_d * along]
            if vectors:
                f_v = part(filters, 1, q)
                v = [part(found, 1 + c, q) for c in range(3)]
                groups.append(gv[0] * v[0] + gv[1] * v[1] + gv[2] * v[2])
                sources += [f_v * gv[c] for c in range(3)]
            groups.append(s * along)
            d_filters.append(jnp.concatenate(groups, axis=0))
            push = f_d * s
            d_dirs.append([jnp.sum(push * gv[c], axis=0, keepdims=True) for c in range(3)])
            d_found.append(jnp.concatenate(sources, axis=0))
        d_filter = jnp.concatenate(d_filters, axis=1)
        fh, fl = split(d_filter)
        both = jnp.concatenate([hh, hl], axis=0)
        dro[...] += mm_nt(jnp.concatenate([fh, fl], axis=1), jnp.concatenate([both, both], axis=1))
        spread = mm(rob[...], jnp.concatenate([fh, fl], axis=0))
        d_hidden = (spread[:LANES] + spread[LANES:]) * mask
        d_pre = d_hidden * (gate * (1.0 + pre * (1.0 - gate)))
        ph, plo = split(d_pre)
        bb = jnp.concatenate([bh, bl], axis=0)
        dri[...] += mm_nt(jnp.concatenate([ph, plo], axis=1), jnp.concatenate([bb, bb], axis=1))
        back = mm(rib[...], jnp.concatenate([ph, plo], axis=0))
        d_basis = back[:basis_count] + back[basis_count:]
        d_dist = jnp.sum(d_basis * basis * offset, axis=0, keepdims=True) * (-2.0 * sharpness)
        extra = []
        for q, g in enumerate(rows):
            extra.append(finish(t * BWD_ROWS + q, h, g, d_dirs[q], d_dist[:, q * LANES : (q + 1) * LANES]))
        if extra[0] is not None:
            d_found = [jnp.concatenate([a, b], axis=0) for a, b in zip(d_found, extra)]
        sh, sl = split(jnp.concatenate(d_found, axis=1))
        dtab[h] += mm_nt(jnp.concatenate([sh, sl], axis=1), jnp.concatenate([hot, hot], axis=1))
        return carry

    lax.fori_loop(0, 2 * per_half, step, 0)


def radial_grads(dro, dri, out, row_in, row_out, basis_count, groups):
    both = dri[...]
    turned = both + pltpu.roll(both, HALF, 1)
    out[row_in : row_in + basis_count] = turned.T[0:basis_count]
    for place in range(groups):
        rows = slice(place * LANES, (place + 1) * LANES)
        grad = dro[rows, 0:LANES] + dro[rows, LANES:]
        out[row_out + place * LANES : row_out + (place + 1) * LANES] = grad.T


def species_hot(row, count):
    place = lax.broadcasted_iota(jnp.int32, (count, LANES), 0).astype(F32)
    return jnp.where(place == row, 1.0, 0.0).astype(BF16)


def first_features(emb_ref, hot):
    high, rest = split(emb_ref[...])
    low = (emb_ref[...] - high.astype(F32) - rest.astype(F32)).astype(BF16)
    dims = (((0,), (0,)), ((), ()))
    terms = [
        lax.dot_general(x.astype(F32).T.astype(BF16), hot, (((1,), (0,)), ((), ())), preferred_element_type=F32)
        for x in (high, rest, low)
    ]
    return terms[0] + (terms[1] + terms[2])


def from_sides(par_ref, a_ref, b_ref):
    even = is_even(par_ref, a_ref.shape)
    a, b = a_ref[...], b_ref[...]
    return jnp.where(even, a, b), jnp.where(even, b, a)


def species_tables(own_ref, up, down, emb_ref, halo):
    lane = lane_ids(1)
    count = emb_ref.shape[0]
    beside = jnp.where(lane >= LANES - halo, down[3:4], up[3:4])
    hot_own, hot_beside = species_hot(own_ref[3:4], count), species_hot(beside, count)
    return hot_own, hot_beside


def place_kernel(cell_ref, frac_ref, species_ref, own_ref):
    own_ref[...] = jnp.zeros(own_ref.shape, F32)
    for c in range(3):
        own_ref[c : c + 1] = (
            frac_ref[0:1] * cell_ref[0, 0, c] + frac_ref[1:2] * cell_ref[0, 1, c] + frac_ref[2:3] * cell_ref[0, 2, c]
        )
    own_ref[3:4] = species_ref[...].astype(F32)


def first_kernel(
    halo, par_ref, cell_ref, own_ref, a_ref, b_ref, nb_ref, count_ref, shift_ref, emb_ref, rin_ref, rout_ref,
    sm_ref, vm_ref, vg_ref,
    geom_ref, feat_ref, agg_ref, send_a, send_b,
    tab, ri4, ro3, acc,
):
    slots = nb_ref.shape[0]
    basis_count = rin_ref.shape[1]
    pairs = slots // 2
    up, down = from_sides(par_ref, a_ref, b_ref)
    lane = lane_ids(pairs)
    low = lane < HALF

    def halves(ref, *lead):
        even = ref[(*lead, pl.ds(0, pairs, stride=2), slice(None))]
        odd = ref[(*lead, pl.ds(1, pairs, stride=2), slice(None))]
        return jnp.where(low, even, pltpu.roll(odd, HALF, 1)), jnp.where(low, pltpu.roll(even, HALF, 1), odd)

    nb = halves(nb_ref)
    shift = [halves(shift_ref, a) for a in range(3)]
    row_slot = 2 * lax.broadcasted_iota(jnp.int32, (pairs, LANES), 0) + jnp.where(low, 0, 1)
    own = own_ref[...]
    lane8 = lane_ids(own.shape[0])
    places = (jnp.where(lane8 < LANES - halo, own, down), jnp.where(lane8 >= halo, own, up))
    for h in range(2):
        index = (nb[h] - halo) & (LANES - 1)
        near = twice(own, h)
        count = twice(count_ref[...], h)
        mask = jnp.where(row_slot < count, 1.0, 0.0).astype(F32)
        steps = [shift[a][h].astype(F32) for a in range(3)]
        r = []
        for c in range(3):
            table = jnp.broadcast_to(places[h][c : c + 1], (pairs, LANES))
            far = jnp.take_along_axis(table, index, axis=1, mode="promise_in_bounds")
            image = steps[0] * cell_ref[0, 0, c] + steps[1] * cell_ref[0, 1, c] + steps[2] * cell_ref[0, 2, c]
            r.append(far - near[c : c + 1] + image)
        dist = jnp.sqrt(r[0] * r[0] + r[1] * r[1] + r[2] * r[2] + 1.0)
        values = [x / dist for x in r] + [dist, mask, index.astype(F32)]
        for n, x in enumerate(values):
            for m in range(pairs):
                geom_ref[h * pairs + m, n : n + 1, :] = x[m : m + 1]
    hot_own, hot_beside = species_tables(own_ref, up, down, emb_ref, halo)
    s, beside = first_features(emb_ref, hot_own), first_features(emb_ref, hot_beside)
    store_tables(tab, [s], [beside], halo)
    prepare_weights(rin_ref, rout_ref, ri4, ro3, (0, 2))
    forward_edges(geom_ref, tab, ri4, ro3, acc, basis_count, False)
    agg = aggregates(acc, slots**-0.5)
    w, size, u, gate = node_forward(agg, sm_ref[0], vm_ref[0], vg_ref[0])
    features = [s + u * sigmoid(u)] + [w[c] * gate for c in range(3)]
    for n in range(4):
        agg_ref[n] = agg[n]
        feat_ref[n] = features[n]
    tail, head = packed(features, halo, True), packed(features, halo, False)
    even = is_even(par_ref, tail.shape)
    send_a[...] = jnp.where(even, tail, head)
    send_b[...] = jnp.where(even, head, tail)


def second_kernel(
    halo, par_ref, geom_ref, feat_ref, a_ref, b_ref, rin_ref, rout_ref, sm_ref, vm_ref, vg_ref, mid_ref, out_ref,
    cot_ref, send_a, send_b, dgeom_ref, grad_ref, mid_tail,
    tab, ri4, ro3, rib, rob, acc, gacc, dro, dri, dtab,
):
    basis_count = rin_ref.shape[1]
    slots = geom_ref.shape[0]
    scale = slots**-0.5
    up, down = from_sides(par_ref, a_ref, b_ref)
    lane = lane_ids(LANES)
    features = [feat_ref[n] for n in range(4)]
    besides = [
        jnp.where(lane >= LANES - halo, unpacked(down, q, halo, True), unpacked(up, q, halo, False)) for q in range(4)
    ]
    store_tables(tab, features, besides, halo)
    groups = (0, 1, 2)
    prepare_weights(rin_ref, rout_ref, ri4, ro3, groups)
    prepare_back(rin_ref, rout_ref, rib, rob, groups)
    forward_edges(geom_ref, tab, ri4, ro3, acc, basis_count, True)

    @pl.when(par_ref[0] >= 0)
    def _():
        agg = aggregates(acc, scale)
        sm, vm, vg = sm_ref[0], vm_ref[0], vg_ref[0]
        w, size, u, gate = node_forward(agg, sm, vm, vg)
        s = feat_ref[0] + u * sigmoid(u)
        mid = mid_ref[...]
        hidden = mm3(mid.T, s)
        act = sigmoid(hidden)
        shown = hidden * act
        weights = jnp.broadcast_to(out_ref[...], (8, LANES))
        per_atom = mm3(weights, shown)
        send_a[LANES:] = jnp.broadcast_to(jnp.sum(per_atom, axis=1, keepdims=True), (8, LANES))
        weight_column = jnp.broadcast_to(out_ref[...], (LANES, LANES)).T
        d_hidden = weight_column * (act * (1.0 + hidden * (1.0 - act)))
        ds = mm3(mid, d_hidden)
        zero = jnp.zeros((LANES, LANES), F32)
        dv = [zero, zero, zero]
        da, g_sm, g_vm, g_vg = node_backward(agg, w, size, u, gate, sm, vm, vg, ds, dv, scale)
        for n in range(4):
            for h in range(2):
                gacc[h, n] = twice(da[n], h)
        for n, x in enumerate([ds] + dv):
            cot_ref[n] = x
        row = basis_count + 3 * LANES
        for grad in (g_sm, g_vm, g_vg):
            grad_ref[row : row + LANES] = grad
            row += LANES
        grad_ref[row : row + 8] = mm3_nt(jnp.ones((8, LANES), F32), shown)
        g_mid = mm3_nt(s, d_hidden)
        grad_ref[row + 8 :] = g_mid[:MID_ROWS]
        mid_tail[...] = g_mid[MID_ROWS:]

    def finish(row, h, g, d_dir, d_dist):
        for c in range(3):
            dgeom_ref[row, c : c + 1, :] = d_dir[c]
        dgeom_ref[row, 3:4, :] = d_dist
        return None

    backward_edges(
        geom_ref, dgeom_ref, tab, ri4, ro3, rib, rob, gacc, dro, dri, dtab, basis_count, True, finish
    )
    radial_grads(dro, dri, grad_ref, 0, basis_count, basis_count, len(groups))
    firsts = [dtab[0, q * LANES : (q + 1) * LANES] for q in range(4)]
    seconds = [dtab[1, q * LANES : (q + 1) * LANES] for q in range(4)]
    for q in range(4):
        cot_ref[q] += (
            jnp.where(lane < LANES - halo, firsts[q], 0.0) + jnp.where(lane >= halo, seconds[q], 0.0)
        )
    to_prev, to_next = packed(firsts, halo, True), packed(seconds, halo, False)
    even = is_even(par_ref, to_prev.shape)
    send_a[:LANES] = jnp.where(even, to_next, to_prev)
    send_b[...] = jnp.where(even, to_prev, to_next)


def third_kernel(
    halo, par_ref, geom_ref, dgeom_ref, agg_ref, cot_ref, a_ref, b_ref, own_ref, pa_ref, pb_ref, mid_tail, emb_ref,
    rin_ref, rout_ref, sm_ref, vm_ref, vg_ref,
    force_ref, send_a, send_b, grad_ref,
    tab, ri4, ro3, rib, rob, gacc, dro, dri, dtab, pull, virial,
):
    basis_count = rin_ref.shape[1]
    slots = geom_ref.shape[0]
    scale = slots**-0.5
    lane = lane_ids(LANES)
    up, down = from_sides(par_ref, a_ref.at[:LANES], b_ref)
    cot = []
    for q in range(4):
        cot.append(
            cot_ref[q]
            + jnp.where(lane >= LANES - halo, unpacked(up, q, halo, True), 0.0)
            + jnp.where(lane < halo, unpacked(down, q, halo, False), 0.0)
        )
    place_up, place_down = from_sides(par_ref, pa_ref, pb_ref)
    hot_own, hot_beside = species_tables(own_ref, place_up, place_down, emb_ref, halo)
    s, beside = first_features(emb_ref, hot_own), first_features(emb_ref, hot_beside)
    store_tables(tab, [s], [beside], halo)
    groups = (0, 2)
    prepare_weights(rin_ref, rout_ref, ri4, ro3, groups)
    prepare_back(rin_ref, rout_ref, rib, rob, groups)
    count = emb_ref.shape[0]

    @pl.when(par_ref[0] >= 0)
    def _():
        agg = [agg_ref[n] for n in range(4)]
        sm, vm, vg = sm_ref[0], vm_ref[0], vg_ref[0]
        w, size, u, gate = node_forward(agg, sm, vm, vg)
        da, g_sm, g_vm, g_vg = node_backward(agg, w, size, u, gate, sm, vm, vg, cot[0], cot[1:], scale)
        for n in range(4):
            for h in range(2):
                gacc[h, n] = twice(da[n], h)
        row = count + basis_count + 2 * LANES
        for g in (g_sm, g_vm, g_vg):
            grad_ref[row : row + LANES] = g
            row += LANES

    pull[...] = jnp.zeros(pull.shape, F32)
    virial[...] = jnp.zeros(virial.shape, F32)

    def finish(row, h, g, d_dir, d_dist):
        more = dgeom_ref[row]
        dist = g[3:4]
        toward = [g[c : c + 1] for c in range(3)]
        turn = [d_dir[c] + more[c : c + 1] for c in range(3)]
        inner = turn[0] * toward[0] + turn[1] * toward[1] + turn[2] * toward[2]
        stretch = d_dist + more[3:4]
        inverse = 1.0 / dist
        dr = [(turn[c] - toward[c] * inner) * inverse + stretch * toward[c] for c in range(3)]
        r = [toward[c] * dist for c in range(3)]
        lines = jnp.concatenate(dr + [jnp.zeros((13, LANES), F32)], axis=0)
        pull[h] += lines
        products = [r[a] * dr[c] for a in range(3) for c in range(3)]
        virial[...] += jnp.concatenate(products + [jnp.zeros((7, LANES), F32)], axis=0)
        return lines

    backward_edges(
        geom_ref, None, tab, ri4, ro3, rib, rob, gacc, dro, dri, dtab, basis_count, False, finish
    )
    first, second = dtab[0, 0:LANES], dtab[1, 0:LANES]
    own_cot = cot[0] + jnp.where(lane < LANES - halo, first, 0.0) + jnp.where(lane >= halo, second, 0.0)
    side_cot = jnp.where(lane >= LANES - halo, first, 0.0) + jnp.where(lane < halo, second, 0.0)
    grad = 0.0
    for hot, value in ((hot_own, own_cot), (hot_beside, side_cot)):
        hi, lo = split(value)
        grad = grad + (mm_nt(hot, hi) + mm_nt(hot, lo))
    grad_ref[0:count] = grad
    row = count
    radial_grads(dro, dri, grad_ref, row, row + basis_count, basis_count, len(groups))
    row += basis_count + 5 * LANES
    grad_ref[row:] = jnp.zeros((grad_ref.shape[0] - row, LANES), F32)
    grad_ref[row + 64 : row + 64 + mid_tail.shape[0]] = mid_tail[...]
    total = jnp.broadcast_to(jnp.sum(virial[...], axis=1, keepdims=True), virial.shape)
    grad_ref[pl.ds(pl.multiple_of(row + 16 * par_ref[1], 16), 16)] = total
    lane16 = lane_ids(16)
    first, second = dtab[0, LANES:], dtab[1, LANES:]
    force_ref[...] = (
        jnp.where(lane16 < LANES - halo, first, 0.0)
        + jnp.where(lane16 >= halo, second, 0.0)
        - folded(pull[0], pull[1])
    )
    even = is_even(par_ref, first.shape)
    send_a[...] = jnp.where(even, second, first)
    send_b[...] = jnp.where(even, first, second)


def final_kernel(
    halo, par_ref, cell_ref, sum_energy, force_ref, a_ref, b_ref, mine, other,
    energy_ref, forces_ref, stress_ref, emb_ref, rin_ref, rout_ref, sm_ref, vm_ref, vg_ref, mid_ref, out_ref,
):
    energy_ref[0, 0] = jnp.max(sum_energy[0:1])
    lane = lane_ids(16)
    up, down = from_sides(par_ref, a_ref, b_ref)
    force = force_ref[...] + jnp.where(lane >= LANES - halo, up, 0.0) + jnp.where(lane < halo, down, 0.0)
    forces_ref[...] = -force[0:3]
    count, basis_count = emb_ref.shape[0], rin_ref.shape[1]
    m = [[cell_ref[0, a, c] for c in range(3)] for a in range(3)]
    det = (
        m[0][0] * (m[1][1] * m[2][2] - m[1][2] * m[2][1])
        - m[0][1] * (m[1][0] * m[2][2] - m[1][2] * m[2][0])
        + m[0][2] * (m[1][0] * m[2][1] - m[1][1] * m[2][0])
    )

    def write(one, two):
        emb_ref[...] = one[0:count]
        row = count
        rin_ref[0] = one[row : row + basis_count]
        rin_ref[1] = two[0:basis_count]
        row += basis_count
        rout_ref[0, :, 0:LANES] = one[row : row + LANES]
        rout_ref[0, :, LANES : 2 * LANES] = jnp.zeros((LANES, LANES), F32)
        rout_ref[0, :, 2 * LANES :] = one[row + LANES : row + 2 * LANES]
        row += 2 * LANES
        line = basis_count
        for g in range(3):
            rout_ref[1, :, g * LANES : (g + 1) * LANES] = two[line : line + LANES]
            line += LANES
        for ref in (sm_ref, vm_ref, vg_ref):
            ref[0] = one[row : row + LANES]
            ref[1] = two[line : line + LANES]
            row += LANES
            line += LANES
        out_ref[...] = two[line : line + 1]
        mid_ref[0:MID_ROWS] = two[line + 8 : line + 8 + MID_ROWS]
        mid_ref[MID_ROWS:] = one[row + 64 : row + 64 + LANES - MID_ROWS]
        virial = one[pl.ds(pl.multiple_of(row + 16 * par_ref[1], 16), 16)]
        place = lane_ids(1)
        lines = [
            jnp.where(place == 0, virial[3 * a : 3 * a + 1], jnp.where(place == 1, virial[3 * a + 1 : 3 * a + 2], virial[3 * a + 2 : 3 * a + 3]))
            for a in range(3)
        ]
        stress = jnp.concatenate(lines, axis=0) / (jnp.zeros((3, LANES), F32) + det)
        stress_ref[0] = stress[:, 0:3]

    @pl.when(par_ref[1] % 2 == 0)
    def _():
        write(other, mine)

    @pl.when(par_ref[1] % 2 == 1)
    def _():
        write(mine, other)


def sides(a, b, axis):
    size = lax.axis_size(axis)
    pairs_a = [(i, i ^ 1) for i in range(size)]
    pairs_b = [(i, (i + 1) % size if i % 2 else (i - 1) % size) for i in range(size)]
    return lax.ppermute(a, axis, pairs_a), lax.ppermute(b, axis, pairs_b)


def swap(x, axis, bit):
    return lax.ppermute(x, axis, [(i, i ^ bit) for i in range(lax.axis_size(axis))])


def layer_spec(x, layer):
    rest = x.shape[1:]
    return pl.BlockSpec((1,) + rest, lambda i: (layer,) + (0,) * len(rest))


def vmem():
    return pl.BlockSpec(memory_space=pltpu.VMEM)


def smem():
    return pl.BlockSpec(memory_space=pltpu.SMEM)


def whole(x):
    return pl.BlockSpec(x.shape, lambda i: (0,) * len(x.shape))


def f32(*shape):
    return jax.ShapeDtypeStruct(shape, F32)


def call(kernel, name, outs, in_specs, out_specs, scratch, flops, *args):
    return pl.pallas_call(
        kernel,
        grid=(1,),
        out_shape=outs,
        in_specs=in_specs,
        out_specs=out_specs,
        scratch_shapes=scratch,
        compiler_params=pltpu.CompilerParams(vmem_limit_bytes=VMEM_LIMIT),
        cost_estimate=pl.CostEstimate(flops=flops, bytes_accessed=flops // 500, transcendentals=0),
        name=name,
    )(*args)


def exchange(x, moves):
    groups, slabs = lax.axis_size("dp"), lax.axis_size("atom")
    route = []
    for g in range(groups):
        for p in range(slabs):
            to_g, to_p = moves(g, p)
            route.append((g * slabs + p, to_g * slabs + to_p))
    return lax.ppermute(x, ("dp", "atom"), route)


def local(
    frac, species, neighbours, counts, shifts, cell, energy_ref, embedding, radial_in, radial_out, scalar_mix,
    vector_mix, vector_gate, readout_mid, readout_out,
):
    atom_count = frac.shape[1]
    halo = atom_count // 4
    slots = neighbours.shape[0]
    basis_count = radial_in.shape[1]
    me = lax.axis_index("atom")
    group = lax.axis_index("dp")
    species_row, counts_row, out_row = species[None], counts[None], readout_out[None]
    own = call(
        place_kernel, "place", f32(8, LANES), [smem(), whole(frac), whole(species_row)], vmem(), [], 10**6,
        cell, frac, species_row,
    )
    side_a, side_b = sides(own, own, "atom")
    par = jnp.stack([me % 2, group]).astype(jnp.int32)
    layer = (radial_in, radial_out, scalar_mix, vector_mix, vector_gate)
    block = f32(LANES, LANES)
    geom, feat, agg, feat_a, feat_b = call(
        functools.partial(first_kernel, halo),
        "layer_one",
        (f32(slots, 8, LANES), f32(4, LANES, LANES), f32(4, LANES, LANES), block, block),
        [smem(), smem()] + [vmem()] * 3 + [whole(x) for x in (neighbours, counts_row, shifts, embedding)]
        + [layer_spec(x, 0) for x in layer],
        [vmem()] * 5,
        [
            pltpu.VMEM((2, LANES, 2 * LANES), BF16),
            pltpu.VMEM((LANES, 4 * basis_count), BF16),
            pltpu.VMEM((2 * LANES, 3 * LANES), BF16),
            pltpu.VMEM((2, 4, LANES, LANES), F32),
        ],
        3 * 10**9,
        par, cell, own, side_a, side_b, neighbours, counts_row, shifts, embedding, *layer,
    )
    feat_a, feat_b = sides(feat_a, feat_b, "atom")
    cot, cot_a, cot_b, dgeom, grads_two, mid_tail = call(
        functools.partial(second_kernel, halo),
        "layer_two",
        (
            f32(4, LANES, LANES), f32(LANES + 8, LANES), block, f32(slots, 8, LANES), f32(G_ROWS, LANES),
            f32(LANES - MID_ROWS, LANES),
        ),
        [smem()] + [vmem()] * 4 + [layer_spec(x, 1) for x in layer] + [whole(readout_mid), whole(out_row)],
        [vmem()] * 6,
        [
            pltpu.VMEM((2, 4 * LANES, 2 * LANES), BF16),
            pltpu.VMEM((LANES, 4 * basis_count), BF16),
            pltpu.VMEM((3 * LANES, 3 * LANES), BF16),
            pltpu.VMEM((2 * basis_count, 2 * LANES), BF16),
            pltpu.VMEM((2 * LANES, 6 * LANES), BF16),
            pltpu.VMEM((2, 4, LANES, LANES), F32),
            pltpu.VMEM((2, 4, LANES, LANES), F32),
            pltpu.VMEM((3 * LANES, 2 * LANES), F32),
            pltpu.VMEM((LANES, 2 * basis_count), F32),
            pltpu.VMEM((2, 4 * LANES, LANES), F32),
        ],
        10**10,
        par, geom, feat, feat_a, feat_b, *layer, readout_mid, out_row,
    )
    energy = cot_a[LANES:]
    cot_a, cot_b = sides(cot_a, cot_b, "atom")
    energy = energy + cot_a[LANES:]
    bits = [1 << n for n in range(1, (lax.axis_size("atom") - 1).bit_length())]
    for bit in bits[:1]:
        energy = energy + swap(energy, "atom", bit)
    force, force_a, force_b, grads_one = call(
        functools.partial(third_kernel, halo),
        "layer_one_back",
        (f32(16, LANES), f32(16, LANES), f32(16, LANES), f32(G_ROWS, LANES)),
        [smem()] + [vmem()] * 11 + [layer_spec(x, 0) for x in layer],
        [vmem()] * 4,
        [
            pltpu.VMEM((2, LANES, 2 * LANES), BF16),
            pltpu.VMEM((LANES, 4 * basis_count), BF16),
            pltpu.VMEM((2 * LANES, 3 * LANES), BF16),
            pltpu.VMEM((2 * basis_count, 2 * LANES), BF16),
            pltpu.VMEM((2 * LANES, 4 * LANES), BF16),
            pltpu.VMEM((2, 4, LANES, LANES), F32),
            pltpu.VMEM((2 * LANES, 2 * LANES), F32),
            pltpu.VMEM((LANES, 2 * basis_count), F32),
            pltpu.VMEM((2, LANES + 16, LANES), F32),
            pltpu.VMEM((2, 16, LANES), F32),
            pltpu.VMEM((16, LANES), F32),
        ],
        6 * 10**9,
        par, geom, dgeom, agg, cot, cot_a, cot_b, own, side_a, side_b, mid_tail, embedding, *layer,
    )
    for bit in bits[1:]:
        energy = energy + swap(energy, "atom", bit)
    force_a, force_b = sides(force_a, force_b, "atom")
    cell_atoms = atom_count * lax.axis_size("atom")
    loss_scale = 2.0 * (energy[0, 0] / cell_atoms - energy_ref[0]) / cell_atoms
    virial_row = embedding.shape[0] + basis_count + 5 * LANES
    line = lax.broadcasted_iota(jnp.int32, (G_ROWS, 1), 0)
    one = grads_one * jnp.where((line >= virial_row) & (line < virial_row + 64), 1.0, loss_scale)
    two = grads_two * loss_scale
    core = group % 2 == 1
    x = jnp.where(core, one, two) + swap(jnp.where(core, two, one), "dp", 1)
    x, force_a, force_b = lax.optimization_barrier((x, force_a, force_b))
    far = [b for b in bits[1:]]
    across, along = group // 2 == 1, (me // 2) % 2 == 1
    upper = (jnp.where(core, along, across), jnp.where(core, across, along))

    def x_or_z(g, p, turned):
        return (g, p ^ 2) if (g % 2 == 1) != turned else (g ^ 2, p)

    for n in range(2):
        half = x.shape[0] // 2
        low_part, high_part = x[:half], x[half:]
        sent = jnp.where(upper[n], low_part, high_part)
        x = jnp.where(upper[n], high_part, low_part) + exchange(sent, lambda g, p: x_or_z(g, p, n == 1))
    order = [1] + far
    for n in range(len(order)):
        first, second = order[n], order[(n + 1) % len(order)]
        x = x + exchange(x, lambda g, p: (g, p ^ (second if g % 2 else first)))
    for n in (1, 0):
        received = exchange(x, lambda g, p: x_or_z(g, p, n == 1))
        x = jnp.where(upper[n], jnp.concatenate([received, x]), jnp.concatenate([x, received]))
    other = swap(x, "dp", 1)
    weights = (embedding,) + layer + (readout_mid, out_row)
    outs = (f32(1, 1), f32(3, atom_count), f32(1, 3, 3)) + tuple(f32(*x.shape) for x in weights)
    result = call(
        functools.partial(final_kernel, halo),
        "final",
        outs,
        [smem(), smem()] + [vmem()] * 6,
        [smem()] + [whole(x) for x in outs[1:]],
        [],
        10**8,
        par, cell, energy, force, force_a, force_b, x, other,
    )
    return (result[0].reshape(1),) + tuple(result[1:-1]) + (result[-1].reshape(LANES),)


def solution(mesh):
    both = ("dp", "atom")
    return jax.shard_map(
        local,
        mesh=mesh,
        in_specs=(
            P(None, both), P(both), P(None, both), P(both), P(None, None, both), P("dp", None, None), P("dp"),
        ) + (P(),) * 8,
        out_specs=(P("dp"), P(None, both), P("dp", None, None)) + (P(),) * 8,
        check_vma=False,
    )
```

```python
import functools

import jax
import jax.numpy as jnp
from jax import lax
from jax.experimental import pallas as pl
from jax.experimental.pallas import tpu as pltpu
from jax.sharding import PartitionSpec as P

F32 = jnp.float32
BF16 = jnp.bfloat16
LANES = 128
HALF = 64
ROWS = 16
VMEM_LIMIT = 20 * 1024 * 1024
G_ROWS = 928
MID_ROWS = 88


def split(x):
    high = x.astype(BF16)
    return high, (x - high.astype(F32)).astype(BF16)


def mm(a, b):
    return lax.dot_general(a, b, (((1,), (0,)), ((), ())), preferred_element_type=F32)


def mm_nt(a, b):
    return lax.dot_general(a, b, (((1,), (1,)), ((), ())), preferred_element_type=F32)


def mm3(a, b):
    ah, al = split(a)
    bh, bl = split(b)
    return mm(ah, bh) + (mm(ah, bl) + mm(al, bh))


def mm3_nt(a, b):
    ah, al = split(a)
    bh, bl = split(b)
    return mm_nt(ah, bh) + (mm_nt(ah, bl) + mm_nt(al, bh))


def sigmoid(x):
    return 0.5 * jnp.tanh(0.5 * x) + 0.5


def lane_ids(rows):
    return lax.broadcasted_iota(jnp.int32, (rows, LANES), 1)


def twice(x, half):
    low = lane_ids(x.shape[0]) < HALF
    other = pltpu.roll(x, HALF, 1)
    return jnp.where(low, x, other) if half == 0 else jnp.where(low, other, x)


def folded(first, second):
    low = lane_ids(first.shape[0]) < HALF
    return jnp.where(low, first + pltpu.roll(first, HALF, 1), second + pltpu.roll(second, HALF, 1))


def windows(own, beside, halo):
    lane = lane_ids(own.shape[0])
    return jnp.where(lane < LANES - halo, own, beside), jnp.where(lane >= halo, own, beside)


def packed(parts, halo, tail):
    lane = lane_ids(parts[0].shape[0])
    out = None
    for q, x in enumerate(parts):
        turn = (halo * (q + 1) if tail else halo * q) % LANES
        x = pltpu.roll(x, turn, 1) if turn else x
        out = x if out is None else jnp.where(lane < halo * q, out, x)
    return out


def unpacked(pack, q, halo, tail):
    turn = (LANES - halo * (q + 1) if tail else LANES - halo * q) % LANES
    return pltpu.roll(pack, turn, 1) if turn else pack


def is_even(par_ref, shape):
    return (jnp.zeros(shape, jnp.int32) + par_ref[0]) == 0


def prepare_weights(rin_ref, rout_ref, ri4, ro3, groups):
    rh, rl = split(rin_ref[0])
    rows = jnp.concatenate([rh, rh, rl, rl], axis=0).astype(F32)
    ri4[...] = rows.T.astype(BF16)
    wh, wl = split(rout_ref[0])
    for place, g in enumerate(groups):
        cols = slice(g * LANES, (g + 1) * LANES)
        th = wh[:, cols].astype(F32).T.astype(BF16)
        tl = wl[:, cols].astype(F32).T.astype(BF16)
        out = slice(place * LANES, (place + 1) * LANES)
        ro3[out, 0:LANES] = th
        ro3[out, LANES : 2 * LANES] = th
        ro3[out, 2 * LANES : 3 * LANES] = tl


def prepare_back(rin_ref, rout_ref, rib, rob, groups):
    rh, rl = split(rin_ref[0])
    count = rh.shape[0]
    rib[0:count, 0:LANES] = rh
    rib[0:count, LANES:] = rh
    rib[count:, 0:LANES] = rl
    rib[count:, LANES:] = rl
    wh, wl = split(rout_ref[0])
    width = len(groups) * LANES
    for place, g in enumerate(groups):
        cols = slice(g * LANES, (g + 1) * LANES)
        for copy in range(2):
            out = slice(copy * width + place * LANES, copy * width + (place + 1) * LANES)
            rob[0:LANES, out] = wh[:, cols]
            rob[LANES:, out] = wl[:, cols]


def store_tables(tab, parts, besides, halo):
    for q, (own, beside) in enumerate(zip(parts, besides)):
        for h, table in enumerate(windows(own, beside, halo)):
            hi, lo = split(table)
            tab[h, q * LANES : (q + 1) * LANES, 0:LANES] = hi
            tab[h, q * LANES : (q + 1) * LANES, LANES:] = lo


def centre_offsets(rows, basis_count):
    place = lax.broadcasted_iota(jnp.int32, (basis_count, LANES), 0).astype(F32)
    centres = 8.0 * place / (basis_count - 1)
    return jnp.concatenate([g[3:4] - centres for g in rows], axis=1)


def sharpness(basis_count):
    return 0.5 * ((basis_count - 1) / 8.0) ** 2


def edge_rows(geom, t):
    return [geom[t * ROWS + q] for q in range(ROWS)]


def radial(rows, t, ri4, ro3, kept, basis_count):
    filters_ref, hidden_ref, basis_ref, slope_ref = kept
    offset = centre_offsets(rows, basis_count)
    bh, bl = split(jnp.exp(-sharpness(basis_count) * offset * offset))
    basis_ref[t] = jnp.concatenate([bh, bl], axis=0)
    pre = mm(ri4[...], jnp.concatenate([bh, bl, bh, bl], axis=0))
    gate = sigmoid(pre)
    mask = jnp.concatenate([g[4:5] for g in rows], axis=1)
    slope_ref[t] = mask * (gate * (1.0 + pre * (1.0 - gate)))
    hh, hl = split(pre * gate * mask)
    hidden_ref[t] = jnp.concatenate([hh, hl], axis=0)
    filters = mm(ro3[...], jnp.concatenate([hh, hl, hh], axis=0))
    filters_ref[t] = filters
    return filters


def one_hot_of(rows):
    place = lax.broadcasted_iota(jnp.int32, (LANES, LANES), 0).astype(F32)
    return jnp.concatenate(
        [jnp.where(place == g[5:6], 1.0, 0.0).astype(BF16) for g in rows], axis=1
    )


def part(x, group, q):
    return x[group * LANES : (group + 1) * LANES, q * LANES : (q + 1) * LANES]


def radial_edges(geom, ri4, ro3, kept, basis_count):
    def step(t, carry):
        radial(edge_rows(geom, t), t, ri4, ro3, kept, basis_count)
        return carry

    lax.fori_loop(0, geom.shape[0] // ROWS, step, 0)


def forward_edges(geom, tab, acc, found_ref, filters_of, vectors):
    per_half = geom.shape[0] // 2 // ROWS
    acc[...] = jnp.zeros(acc.shape, F32)
    wide = 2 if vectors else 1

    def step(t, carry):
        h = t // per_half
        rows = edge_rows(geom, t)
        filters = filters_of(rows, t)
        hot = one_hot_of(rows)
        found = mm(tab[h], jnp.concatenate([hot, hot], axis=0))
        found_ref[t] = found
        sums = [None] * 4
        for q, g in enumerate(rows):
            s = part(found, 0, q)
            terms = [part(filters, 0, q) * s]
            push = part(filters, wide, q) * s
            for c in range(3):
                term = push * g[c : c + 1]
                if vectors:
                    term = term + part(filters, 1, q) * part(found, 1 + c, q)
                terms.append(term)
            sums = [x if y is None else y + x for x, y in zip(terms, sums)]
        for n in range(4):
            acc[h, n] += sums[n]
        return carry

    lax.fori_loop(0, 2 * per_half, step, 0)


def aggregates(acc, scale):
    return [folded(acc[0, n], acc[1, n]) * scale for n in range(4)]


def node_forward(agg, sm, vm, vg):
    mixed = mm3(vm.T, jnp.concatenate(agg[1:], axis=1))
    w = [mixed[:, c * LANES : (c + 1) * LANES] for c in range(3)]
    size = jnp.sqrt(w[0] * w[0] + w[1] * w[1] + w[2] * w[2] + 1.0)
    u = mm3(sm.T, agg[0]) + (size - 1.0)
    gate = sigmoid(mm3(vg.T, agg[0]))
    return w, size, u, gate


def node_backward(agg, w, size, u, gate, sm, vm, vg, ds, dv, scale):
    act = sigmoid(u)
    du = ds * (act * (1.0 + u * (1.0 - act)))
    ratio = du / size
    dw = [w[c] * ratio + dv[c] * gate for c in range(3)]
    dq = (dv[0] * w[0] + dv[1] * w[1] + dv[2] * w[2]) * gate * (1.0 - gate)
    dw_all = jnp.concatenate(dw, axis=1)
    da_s = (mm3(sm, du) + mm3(vg, dq)) * scale
    da_v = mm3(vm, dw_all) * scale
    da = [da_s] + [da_v[:, c * LANES : (c + 1) * LANES] for c in range(3)]
    g_sm = mm3_nt(agg[0], du)
    g_vg = mm3_nt(agg[0], dq)
    g_vm = mm3_nt(jnp.concatenate(agg[1:], axis=1), dw_all)
    return da, g_sm, g_vm, g_vg


def source_terms(rows, filters, found, gs, gv, vectors):
    wide = 2 if vectors else 1
    columns = []
    for q, g in enumerate(rows):
        along = gv[0] * g[0:1] + gv[1] * g[1:2] + gv[2] * g[2:3]
        sources = [part(filters, 0, q) * gs + part(filters, wide, q) * along]
        if vectors:
            f_v = part(filters, 1, q)
            sources += [f_v * gv[c] for c in range(3)]
        columns.append(jnp.concatenate(sources, axis=0))
    return columns


def scatter(columns, hot):
    sh, sl = split(jnp.concatenate(columns, axis=1))
    return mm_nt(jnp.concatenate([sh, sl], axis=1), jnp.concatenate([hot, hot], axis=1))


def step_derivatives(gacc, h):
    return gacc[h, 0], [gacc[h, 1 + c] for c in range(3)]


def filter_terms(rows, t, kept, found, gs, gv, rib, rob, dro, dri, basis_count, vectors):
    filters_ref, hidden_ref, basis_ref, slope_ref = kept
    wide = 2 if vectors else 1
    d_filters, d_dirs = [], []
    for q, g in enumerate(rows):
        s = part(found, 0, q)
        along = gv[0] * g[0:1] + gv[1] * g[1:2] + gv[2] * g[2:3]
        groups = [gs * s]
        if vectors:
            v = [part(found, 1 + c, q) for c in range(3)]
            groups.append(gv[0] * v[0] + gv[1] * v[1] + gv[2] * v[2])
        groups.append(s * along)
        d_filters.append(jnp.concatenate(groups, axis=0))
        push = part(filters_ref.at[t], wide, q) * s
        d_dirs.append([jnp.sum(push * gv[c], axis=0, keepdims=True) for c in range(3)])
    fh, fl = split(jnp.concatenate(d_filters, axis=1))
    both = hidden_ref[t]
    dro[...] += mm_nt(jnp.concatenate([fh, fl], axis=1), jnp.concatenate([both, both], axis=1))
    spread = mm(rob[...], jnp.concatenate([fh, fl], axis=0))
    d_pre = (spread[:LANES] + spread[LANES:]) * slope_ref[t]
    ph, plo = split(d_pre)
    bb = basis_ref[t]
    dri[...] += mm_nt(jnp.concatenate([ph, plo], axis=1), jnp.concatenate([bb, bb], axis=1))
    back = mm(rib[...], jnp.concatenate([ph, plo], axis=0))
    d_basis = back[:basis_count] + back[basis_count:]
    basis = bb[:basis_count].astype(F32) + bb[basis_count:].astype(F32)
    offset = centre_offsets(rows, basis_count)
    d_dist = jnp.sum(d_basis * basis * offset, axis=0, keepdims=True) * (-2.0 * sharpness(basis_count))
    return d_dirs, [d_dist[:, q * LANES : (q + 1) * LANES] for q in range(len(rows))]


def radial_grads(dro, dri, out, row_in, row_out, basis_count, groups):
    both = dri[...]
    turned = both + pltpu.roll(both, HALF, 1)
    out[row_in : row_in + basis_count] = turned.T[0:basis_count]
    for place in range(groups):
        rows = slice(place * LANES, (place + 1) * LANES)
        grad = dro[rows, 0:LANES] + dro[rows, LANES:]
        out[row_out + place * LANES : row_out + (place + 1) * LANES] = grad.T


def species_hot(row, count):
    place = lax.broadcasted_iota(jnp.int32, (count, LANES), 0).astype(F32)
    return jnp.where(place == row, 1.0, 0.0).astype(BF16)


def first_features(emb_ref, hot):
    high, rest = split(emb_ref[...])
    low = (emb_ref[...] - high.astype(F32) - rest.astype(F32)).astype(BF16)
    dims = (((0,), (0,)), ((), ()))
    terms = [
        lax.dot_general(x.astype(F32).T.astype(BF16), hot, (((1,), (0,)), ((), ())), preferred_element_type=F32)
        for x in (high, rest, low)
    ]
    return terms[0] + (terms[1] + terms[2])


def from_sides(par_ref, a_ref, b_ref):
    even = is_even(par_ref, a_ref.shape)
    a, b = a_ref[...], b_ref[...]
    return jnp.where(even, a, b), jnp.where(even, b, a)


def species_tables(own_ref, up, down, emb_ref, halo):
    lane = lane_ids(1)
    count = emb_ref.shape[0]
    beside = jnp.where(lane >= LANES - halo, down[3:4], up[3:4])
    hot_own, hot_beside = species_hot(own_ref[3:4], count), species_hot(beside, count)
    return hot_own, hot_beside


def place_kernel(cell_ref, frac_ref, species_ref, own_ref):
    own_ref[...] = jnp.zeros(own_ref.shape, F32)
    for c in range(3):
        own_ref[c : c + 1] = (
            frac_ref[0:1] * cell_ref[0, 0, c] + frac_ref[1:2] * cell_ref[0, 1, c] + frac_ref[2:3] * cell_ref[0, 2, c]
        )
    own_ref[3:4] = species_ref[...].astype(F32)


def first_kernel(
    halo, par_ref, cell_ref, own_ref, a_ref, b_ref, nb_ref, count_ref, shift_ref, emb_ref, rin_ref, rout_ref,
    sm_ref, vm_ref, vg_ref,
    geom_ref, feat_ref, agg_ref, send_a, send_b, filters_ref, hidden_ref, basis_ref, slope_ref, found_ref,
    tab, ri4, ro3, acc,
):
    slots = nb_ref.shape[0]
    basis_count = rin_ref.shape[1]
    pairs = slots // 2
    up, down = from_sides(par_ref, a_ref, b_ref)
    lane = lane_ids(pairs)
    low = lane < HALF

    def halves(ref, *lead):
        even = ref[(*lead, pl.ds(0, pairs, stride=2), slice(None))]
        odd = ref[(*lead, pl.ds(1, pairs, stride=2), slice(None))]
        return jnp.where(low, even, pltpu.roll(odd, HALF, 1)), jnp.where(low, pltpu.roll(even, HALF, 1), odd)

    nb = halves(nb_ref)
    shift = [halves(shift_ref, a) for a in range(3)]
    row_slot = 2 * lax.broadcasted_iota(jnp.int32, (pairs, LANES), 0) + jnp.where(low, 0, 1)
    own = own_ref[...]
    lane8 = lane_ids(own.shape[0])
    places = (jnp.where(lane8 < LANES - halo, own, down), jnp.where(lane8 >= halo, own, up))
    for h in range(2):
        index = (nb[h] - halo) & (LANES - 1)
        near = twice(own, h)
        count = twice(count_ref[...], h)
        mask = jnp.where(row_slot < count, 1.0, 0.0).astype(F32)
        steps = [shift[a][h].astype(F32) for a in range(3)]
        r = []
        for c in range(3):
            table = jnp.broadcast_to(places[h][c : c + 1], (pairs, LANES))
            far = jnp.take_along_axis(table, index, axis=1, mode="promise_in_bounds")
            image = steps[0] * cell_ref[0, 0, c] + steps[1] * cell_ref[0, 1, c] + steps[2] * cell_ref[0, 2, c]
            r.append(far - near[c : c + 1] + image)
        dist = jnp.sqrt(r[0] * r[0] + r[1] * r[1] + r[2] * r[2] + 1.0)
        values = [x / dist for x in r] + [dist, mask, index.astype(F32)]
        for n, x in enumerate(values):
            for m in range(pairs):
                geom_ref[h * pairs + m, n : n + 1, :] = x[m : m + 1]
    hot_own, hot_beside = species_tables(own_ref, up, down, emb_ref, halo)
    s, beside = first_features(emb_ref, hot_own), first_features(emb_ref, hot_beside)
    store_tables(tab, [s], [beside], halo)
    prepare_weights(rin_ref, rout_ref, ri4, ro3, (0, 2))
    kept = (filters_ref, hidden_ref, basis_ref, slope_ref)
    forward_edges(
        geom_ref, tab, acc, found_ref, lambda rows, t: radial(rows, t, ri4, ro3, kept, basis_count), False
    )
    agg = aggregates(acc, slots**-0.5)
    w, size, u, gate = node_forward(agg, sm_ref[0], vm_ref[0], vg_ref[0])
    features = [s + u * sigmoid(u)] + [w[c] * gate for c in range(3)]
    for n in range(4):
        agg_ref[n] = agg[n]
        feat_ref[n] = features[n]
    tail, head = packed(features, halo, True), packed(features, halo, False)
    even = is_even(par_ref, tail.shape)
    send_a[...] = jnp.where(even, tail, head)
    send_b[...] = jnp.where(even, head, tail)


def radial_kernel(geom_ref, rin_ref, rout_ref, filters_ref, hidden_ref, basis_ref, slope_ref, ri4, ro3):
    prepare_weights(rin_ref, rout_ref, ri4, ro3, (0, 1, 2))
    radial_edges(geom_ref, ri4, ro3, (filters_ref, hidden_ref, basis_ref, slope_ref), rin_ref.shape[1])


def second_kernel(
    halo, par_ref, geom_ref, feat_ref, a_ref, b_ref, filters_ref, sm_ref, vm_ref, vg_ref, mid_ref, out_ref,
    cot_ref, send_a, send_b, grad_ref, mid_tail, gacc, found_ref,
    tab, acc, dtab,
):
    slots = geom_ref.shape[0]
    scale = slots**-0.5
    up, down = from_sides(par_ref, a_ref, b_ref)
    lane = lane_ids(LANES)
    features = [feat_ref[n] for n in range(4)]
    besides = [
        jnp.where(lane >= LANES - halo, unpacked(down, q, halo, True), unpacked(up, q, halo, False)) for q in range(4)
    ]
    store_tables(tab, features, besides, halo)
    forward_edges(geom_ref, tab, acc, found_ref, lambda rows, t: filters_ref.at[t], True)

    @pl.when(par_ref[0] >= 0)
    def _():
        agg = aggregates(acc, scale)
        sm, vm, vg = sm_ref[0], vm_ref[0], vg_ref[0]
        w, size, u, gate = node_forward(agg, sm, vm, vg)
        s = feat_ref[0] + u * sigmoid(u)
        mid = mid_ref[...]
        hidden = mm3(mid.T, s)
        act = sigmoid(hidden)
        shown = hidden * act
        weights = jnp.broadcast_to(out_ref[...], (8, LANES))
        per_atom = mm3(weights, shown)
        send_a[LANES:] = jnp.broadcast_to(jnp.sum(per_atom, axis=1, keepdims=True), (8, LANES))
        weight_column = jnp.broadcast_to(out_ref[...], (LANES, LANES)).T
        d_hidden = weight_column * (act * (1.0 + hidden * (1.0 - act)))
        ds = mm3(mid, d_hidden)
        zero = jnp.zeros((LANES, LANES), F32)
        dv = [zero, zero, zero]
        da, g_sm, g_vm, g_vg = node_backward(agg, w, size, u, gate, sm, vm, vg, ds, dv, scale)
        for n in range(4):
            for h in range(2):
                gacc[h, n] = twice(da[n], h)
        for n, x in enumerate([ds] + dv):
            cot_ref[n] = x
        row = 0
        for grad in (g_sm, g_vm, g_vg):
            grad_ref[row : row + LANES] = grad
            row += LANES
        grad_ref[row : row + 8] = mm3_nt(jnp.ones((8, LANES), F32), shown)
        g_mid = mm3_nt(s, d_hidden)
        grad_ref[row + 8 :] = g_mid[:MID_ROWS]
        mid_tail[...] = g_mid[MID_ROWS:]

    per_half = slots // 2 // ROWS
    dtab[...] = jnp.zeros(dtab.shape, F32)

    def step(t, carry):
        h = t // per_half
        rows = edge_rows(geom_ref, t)
        gs, gv = step_derivatives(gacc, h)
        columns = source_terms(rows, filters_ref.at[t], found_ref.at[t], gs, gv, True)
        dtab[h] += scatter(columns, one_hot_of(rows))
        return carry

    lax.fori_loop(0, 2 * per_half, step, 0)
    firsts = [dtab[0, q * LANES : (q + 1) * LANES] for q in range(4)]
    seconds = [dtab[1, q * LANES : (q + 1) * LANES] for q in range(4)]
    for q in range(4):
        cot_ref[q] += (
            jnp.where(lane < LANES - halo, firsts[q], 0.0) + jnp.where(lane >= halo, seconds[q], 0.0)
        )
    to_prev, to_next = packed(firsts, halo, True), packed(seconds, halo, False)
    even = is_even(par_ref, to_prev.shape)
    send_a[:LANES] = jnp.where(even, to_next, to_prev)
    send_b[...] = jnp.where(even, to_prev, to_next)


def radial_back_kernel(
    geom_ref, filters_ref, hidden_ref, basis_ref, slope_ref, found_ref, gacc, mixed_ref, rin_ref, rout_ref,
    dgeom_ref, grad_ref,
    rib, rob, dro, dri,
):
    basis_count = rin_ref.shape[1]
    groups = (0, 1, 2)
    prepare_back(rin_ref, rout_ref, rib, rob, groups)
    kept = (filters_ref, hidden_ref, basis_ref, slope_ref)
    per_half = geom_ref.shape[0] // 2 // ROWS
    dro[...] = jnp.zeros(dro.shape, F32)
    dri[...] = jnp.zeros(dri.shape, F32)

    def step(t, carry):
        rows = edge_rows(geom_ref, t)
        gs, gv = step_derivatives(gacc, t // per_half)
        d_dirs, d_dists = filter_terms(
            rows, t, kept, found_ref.at[t], gs, gv, rib, rob, dro, dri, basis_count, True
        )
        for q in range(ROWS):
            for c in range(3):
                dgeom_ref[t * ROWS + q, c : c + 1, :] = d_dirs[q][c]
            dgeom_ref[t * ROWS + q, 3:4, :] = d_dists[q]
        return carry

    lax.fori_loop(0, 2 * per_half, step, 0)
    radial_grads(dro, dri, grad_ref, 0, basis_count, basis_count, len(groups))
    grad_ref[basis_count + 3 * LANES :] = mixed_ref[...]


def third_kernel(
    halo, par_ref, geom_ref, dgeom_ref, agg_ref, cot_ref, a_ref, b_ref, own_ref, pa_ref, pb_ref, mid_tail,
    filters_ref, hidden_ref, basis_ref, slope_ref, found_ref, emb_ref, rin_ref, rout_ref, sm_ref, vm_ref, vg_ref,
    force_ref, send_ref, grad_ref,
    rib, rob, gacc, dro, dri, dtab, pull, virial,
):
    basis_count = rin_ref.shape[1]
    slots = geom_ref.shape[0]
    scale = slots**-0.5
    lane = lane_ids(LANES)
    up, down = from_sides(par_ref, a_ref.at[:LANES], b_ref)
    cot = []
    for q in range(4):
        cot.append(
            cot_ref[q]
            + jnp.where(lane >= LANES - halo, unpacked(up, q, halo, True), 0.0)
            + jnp.where(lane < halo, unpacked(down, q, halo, False), 0.0)
        )
    place_up, place_down = from_sides(par_ref, pa_ref, pb_ref)
    hot_own, hot_beside = species_tables(own_ref, place_up, place_down, emb_ref, halo)
    groups = (0, 2)
    prepare_back(rin_ref, rout_ref, rib, rob, groups)
    count = emb_ref.shape[0]

    @pl.when(par_ref[0] >= 0)
    def _():
        agg = [agg_ref[n] for n in range(4)]
        sm, vm, vg = sm_ref[0], vm_ref[0], vg_ref[0]
        w, size, u, gate = node_forward(agg, sm, vm, vg)
        da, g_sm, g_vm, g_vg = node_backward(agg, w, size, u, gate, sm, vm, vg, cot[0], cot[1:], scale)
        for n in range(4):
            for h in range(2):
                gacc[h, n] = twice(da[n], h)
        row = count + basis_count + 2 * LANES
        for g in (g_sm, g_vm, g_vg):
            grad_ref[row : row + LANES] = g
            row += LANES

    pull[...] = jnp.zeros(pull.shape, F32)
    virial[...] = jnp.zeros(virial.shape, F32)

    def finish(row, g, d_dir, d_dist):
        more = dgeom_ref[row]
        dist = g[3:4]
        toward = [g[c : c + 1] for c in range(3)]
        turn = [d_dir[c] + more[c : c + 1] for c in range(3)]
        inner = turn[0] * toward[0] + turn[1] * toward[1] + turn[2] * toward[2]
        stretch = d_dist + more[3:4]
        inverse = 1.0 / dist
        dr = [(turn[c] - toward[c] * inner) * inverse + stretch * toward[c] for c in range(3)]
        r = [toward[c] * dist for c in range(3)]
        lines = jnp.concatenate(dr + [jnp.zeros((13, LANES), F32)], axis=0)
        products = [r[a] * dr[c] for a in range(3) for c in range(3)]
        return lines, jnp.concatenate(products + [jnp.zeros((7, LANES), F32)], axis=0)

    kept = (filters_ref, hidden_ref, basis_ref, slope_ref)
    per_half = slots // 2 // ROWS
    dro[...] = jnp.zeros(dro.shape, F32)
    dri[...] = jnp.zeros(dri.shape, F32)
    dtab[...] = jnp.zeros(dtab.shape, F32)

    def step(t, carry):
        h = t // per_half
        rows = edge_rows(geom_ref, t)
        gs, gv = step_derivatives(gacc, h)
        found = found_ref.at[t]
        d_dirs, d_dists = filter_terms(rows, t, kept, found, gs, gv, rib, rob, dro, dri, basis_count, False)
        columns = source_terms(rows, filters_ref.at[t], found, gs, gv, False)
        pairs = [finish(t * ROWS + q, g, d_dirs[q], d_dists[q]) for q, g in enumerate(rows)]
        pull[h] += sum(x for x, _ in pairs[1:]) + pairs[0][0]
        virial[...] += sum(x for _, x in pairs[1:]) + pairs[0][1]
        columns = [jnp.concatenate([x, y], axis=0) for x, (y, _) in zip(columns, pairs)]
        dtab[h] += scatter(columns, one_hot_of(rows))
        return carry

    lax.fori_loop(0, 2 * per_half, step, 0)
    first, second = dtab[0, 0:LANES], dtab[1, 0:LANES]
    own_cot = cot[0] + jnp.where(lane < LANES - halo, first, 0.0) + jnp.where(lane >= halo, second, 0.0)
    side_cot = jnp.where(lane >= LANES - halo, first, 0.0) + jnp.where(lane < halo, second, 0.0)
    grad = 0.0
    for hot, value in ((hot_own, own_cot), (hot_beside, side_cot)):
        hi, lo = split(value)
        grad = grad + (mm_nt(hot, hi) + mm_nt(hot, lo))
    grad_ref[0:count] = grad
    row = count
    radial_grads(dro, dri, grad_ref, row, row + basis_count, basis_count, len(groups))
    row += basis_count + 5 * LANES
    grad_ref[row:] = jnp.zeros((grad_ref.shape[0] - row, LANES), F32)
    grad_ref[row + 64 : row + 64 + mid_tail.shape[0]] = mid_tail[...]
    total = jnp.broadcast_to(jnp.sum(virial[...], axis=1, keepdims=True), virial.shape)
    grad_ref[pl.ds(pl.multiple_of(row + 16 * par_ref[1], 16), 16)] = total
    lane16 = lane_ids(16)
    first, second = dtab[0, LANES:], dtab[1, LANES:]
    force_ref[...] = (
        jnp.where(lane16 < LANES - halo, first, 0.0)
        + jnp.where(lane16 >= halo, second, 0.0)
        - folded(pull[0], pull[1])
    )
    even = is_even(par_ref, first.shape)
    send_ref[0:8] = jnp.where(even, second, first)[0:8]
    send_ref[8:16] = jnp.where(even, first, second)[0:8]


def final_kernel(
    halo, par_ref, cell_ref, sum_energy, force_ref, a_ref, b_ref, mine_turned, other_turned,
    energy_ref, forces_ref, stress_ref, emb_ref, rin_ref, rout_ref, sm_ref, vm_ref, vg_ref, mid_ref, out_ref,
    mine, other,
):
    energy_ref[0, 0] = jnp.max(sum_energy[0:1])
    rows = mine.shape[0] // 4
    for c in range(4):
        turned = pl.ds(pl.multiple_of((par_ref[2] ^ c) * rows, 8), rows)
        mine[c * rows : (c + 1) * rows] = mine_turned[turned]
        other[c * rows : (c + 1) * rows] = other_turned[turned]
    lane = lane_ids(8)
    up, down = from_sides(par_ref, a_ref, b_ref.at[pl.ds(pl.multiple_of(8 * par_ref[3], 8), 8)])
    force = force_ref[0:8] + jnp.where(lane >= LANES - halo, up, 0.0) + jnp.where(lane < halo, down, 0.0)
    forces_ref[...] = -force[0:3]
    count, basis_count = emb_ref.shape[0], rin_ref.shape[1]
    m = [[cell_ref[0, a, c] for c in range(3)] for a in range(3)]
    det = (
        m[0][0] * (m[1][1] * m[2][2] - m[1][2] * m[2][1])
        - m[0][1] * (m[1][0] * m[2][2] - m[1][2] * m[2][0])
        + m[0][2] * (m[1][0] * m[2][1] - m[1][1] * m[2][0])
    )

    def write(one, two):
        emb_ref[...] = one[0:count]
        row = count
        rin_ref[0] = one[row : row + basis_count]
        rin_ref[1] = two[0:basis_count]
        row += basis_count
        rout_ref[0, :, 0:LANES] = one[row : row + LANES]
        rout_ref[0, :, LANES : 2 * LANES] = jnp.zeros((LANES, LANES), F32)
        rout_ref[0, :, 2 * LANES :] = one[row + LANES : row + 2 * LANES]
        row += 2 * LANES
        line = basis_count
        for g in range(3):
            rout_ref[1, :, g * LANES : (g + 1) * LANES] = two[line : line + LANES]
            line += LANES
        for ref in (sm_ref, vm_ref, vg_ref):
            ref[0] = one[row : row + LANES]
            ref[1] = two[line : line + LANES]
            row += LANES
            line += LANES
        out_ref[...] = two[line : line + 1]
        mid_ref[0:MID_ROWS] = two[line + 8 : line + 8 + MID_ROWS]
        mid_ref[MID_ROWS:] = one[row + 64 : row + 64 + LANES - MID_ROWS]
        virial = one[pl.ds(pl.multiple_of(row + 16 * par_ref[1], 16), 16)]
        place = lane_ids(1)
        lines = [
            jnp.where(place == 0, virial[3 * a : 3 * a + 1], jnp.where(place == 1, virial[3 * a + 1 : 3 * a + 2], virial[3 * a + 2 : 3 * a + 3]))
            for a in range(3)
        ]
        stress = jnp.concatenate(lines, axis=0) / (jnp.zeros((3, LANES), F32) + det)
        stress_ref[0] = stress[:, 0:3]

    @pl.when(par_ref[1] % 2 == 0)
    def _():
        write(other, mine)

    @pl.when(par_ref[1] % 2 == 1)
    def _():
        write(mine, other)


def sides(a, b, axis):
    size = lax.axis_size(axis)
    pairs_a = [(i, i ^ 1) for i in range(size)]
    pairs_b = [(i, (i + 1) % size if i % 2 else (i - 1) % size) for i in range(size)]
    return lax.ppermute(a, axis, pairs_a), lax.ppermute(b, axis, pairs_b)


def swap(x, axis, bit):
    return lax.ppermute(x, axis, [(i, i ^ bit) for i in range(lax.axis_size(axis))])


def layer_spec(x, layer):
    rest = x.shape[1:]
    return pl.BlockSpec((1,) + rest, lambda i: (layer,) + (0,) * len(rest))


def vmem():
    return pl.BlockSpec(memory_space=pltpu.VMEM)


def smem():
    return pl.BlockSpec(memory_space=pltpu.SMEM)


def whole(x):
    return pl.BlockSpec(x.shape, lambda i: (0,) * len(x.shape))


def f32(*shape):
    return jax.ShapeDtypeStruct(shape, F32)


def call(kernel, name, outs, in_specs, out_specs, scratch, flops, *args):
    return pl.pallas_call(
        kernel,
        grid=(1,),
        out_shape=outs,
        in_specs=in_specs,
        out_specs=out_specs,
        scratch_shapes=scratch,
        compiler_params=pltpu.CompilerParams(vmem_limit_bytes=VMEM_LIMIT),
        cost_estimate=pl.CostEstimate(flops=flops, bytes_accessed=flops // 500, transcendentals=0),
        name=name,
    )(*args)


def exchange(x, moves):
    groups, slabs = lax.axis_size("dp"), lax.axis_size("atom")
    route = []
    for g in range(groups):
        for p in range(slabs):
            to_g, to_p = moves(g, p)
            route.append((g * slabs + p, to_g * slabs + to_p))
    return lax.ppermute(x, ("dp", "atom"), route)


def local(
    frac, species, neighbours, counts, shifts, cell, energy_ref, embedding, radial_in, radial_out, scalar_mix,
    vector_mix, vector_gate, readout_mid, readout_out,
):
    atom_count = frac.shape[1]
    halo = atom_count // 4
    slots = neighbours.shape[0]
    basis_count = radial_in.shape[1]
    me = lax.axis_index("atom")
    group = lax.axis_index("dp")
    species_row, counts_row, out_row = species[None], counts[None], readout_out[None]
    own = call(
        place_kernel, "place", f32(8, LANES), [smem(), whole(frac), whole(species_row)], vmem(), [], 10**10,
        cell, frac, species_row,
    )
    side_a, side_b = sides(own, own, "atom")
    plane = group // 2 * 2 + me % 2
    slabs = lax.axis_size("atom")
    levels = (slabs - 1).bit_length() - 1
    bits = [2 << n for n in range(levels)]
    opposite = jnp.where(me % 2 == 1, (me + 1) % slabs, (me + slabs - 1) % slabs)
    turned = (me ^ opposite ^ 1) >> 1
    turned = jnp.where(group % 2 == 1, (turned >> 1) | ((turned & 1) << (levels - 1)), turned)
    par = jnp.stack([me % 2, group, plane, turned]).astype(jnp.int32)
    layer = (radial_in, radial_out, scalar_mix, vector_mix, vector_gate)
    block = f32(LANES, LANES)
    edges, steps = ROWS * LANES, slots // ROWS

    def kept(groups):
        halves = tuple(jax.ShapeDtypeStruct((steps, n, edges), BF16) for n in (2 * LANES, 2 * basis_count))
        return (f32(steps, groups * LANES, edges),) + halves + (f32(steps, LANES, edges),)

    geom, feat, agg, feat_a, feat_b, *kept_one = call(
        functools.partial(first_kernel, halo),
        "layer_one",
        (f32(slots, 8, LANES), f32(4, LANES, LANES), f32(4, LANES, LANES), block, block) + kept(2)
        + (f32(steps, LANES, edges),),
        [smem(), smem()] + [vmem()] * 7 + [layer_spec(x, 0) for x in layer],
        [vmem()] * 10,
        [
            pltpu.VMEM((2, LANES, 2 * LANES), BF16),
            pltpu.VMEM((LANES, 4 * basis_count), BF16),
            pltpu.VMEM((2 * LANES, 3 * LANES), BF16),
            pltpu.VMEM((2, 4, LANES, LANES), F32),
        ],
        3 * 10**9,
        par, cell, own, side_a, side_b, neighbours, counts_row, shifts, embedding, *layer,
    )
    feat_a, feat_b = sides(feat_a, feat_b, "atom")
    kept_two = call(
        radial_kernel,
        "radial_two",
        kept(3),
        [vmem(), layer_spec(radial_in, 1), layer_spec(radial_out, 1)],
        [vmem()] * 4,
        [pltpu.VMEM((LANES, 4 * basis_count), BF16), pltpu.VMEM((3 * LANES, 3 * LANES), BF16)],
        3 * 10**9,
        geom, radial_in, radial_out,
    )
    tail_rows = LANES - MID_ROWS
    mixed_rows = 3 * LANES + 8 + MID_ROWS
    cot, cot_a, cot_b, mixed, mid_tail, gacc, found_two = call(
        functools.partial(second_kernel, halo),
        "layer_two",
        (
            f32(4, LANES, LANES), f32(LANES + 8, LANES), block, f32(mixed_rows, LANES), f32(tail_rows, LANES),
            f32(2, 4, LANES, LANES), f32(steps, 4 * LANES, edges),
        ),
        [smem()] + [vmem()] * 5 + [layer_spec(x, 1) for x in layer[2:]] + [whole(readout_mid), whole(out_row)],
        [vmem()] * 7,
        [
            pltpu.VMEM((2, 4 * LANES, 2 * LANES), BF16),
            pltpu.VMEM((2, 4, LANES, LANES), F32),
            pltpu.VMEM((2, 4 * LANES, LANES), F32),
        ],
        5 * 10**9,
        par, geom, feat, feat_a, feat_b, kept_two[0], *layer[2:], readout_mid, out_row,
    )
    energy = cot_a[LANES:]
    cot_a, cot_b = sides(cot_a, cot_b, "atom")
    dgeom, grads_two = call(
        radial_back_kernel,
        "radial_two_back",
        (f32(slots, 8, LANES), f32(G_ROWS, LANES)),
        [vmem()] * 8 + [layer_spec(radial_in, 1), layer_spec(radial_out, 1)],
        [vmem()] * 2,
        [
            pltpu.VMEM((2 * basis_count, 2 * LANES), BF16),
            pltpu.VMEM((2 * LANES, 6 * LANES), BF16),
            pltpu.VMEM((3 * LANES, 2 * LANES), F32),
            pltpu.VMEM((LANES, 2 * basis_count), F32),
        ],
        5 * 10**9,
        geom, *kept_two, found_two, gacc, mixed, radial_in, radial_out,
    )
    energy = energy + cot_a[LANES:]
    others = [swap(energy, "atom", k) for k in range(2, min(slabs, 8), 2)]
    for other in others:
        energy = energy + other
    force, force_sent, grads_one = call(
        functools.partial(third_kernel, halo),
        "layer_one_back",
        (f32(16, LANES), f32(16, LANES), f32(G_ROWS, LANES)),
        [smem()] + [vmem()] * 16 + [layer_spec(x, 0) for x in layer],
        [vmem()] * 3,
        [
            pltpu.VMEM((2 * basis_count, 2 * LANES), BF16),
            pltpu.VMEM((2 * LANES, 4 * LANES), BF16),
            pltpu.VMEM((2, 4, LANES, LANES), F32),
            pltpu.VMEM((2 * LANES, 2 * LANES), F32),
            pltpu.VMEM((LANES, 2 * basis_count), F32),
            pltpu.VMEM((2, LANES + 16, LANES), F32),
            pltpu.VMEM((2, 16, LANES), F32),
            pltpu.VMEM((16, LANES), F32),
        ],
        6 * 10**9,
        par, geom, dgeom, agg, cot, cot_a, cot_b, own, side_a, side_b, mid_tail, *kept_one, embedding,
        *layer,
    )
    for bit in bits[2:]:
        energy = energy + swap(energy, "atom", bit)
    cell_atoms = atom_count * slabs
    loss_scale = 2.0 * (energy[0:1] / cell_atoms - energy_ref[0]) / cell_atoms
    virial_row = embedding.shape[0] + basis_count + 5 * LANES
    line = lax.broadcasted_iota(jnp.int32, (G_ROWS, 1), 0)
    one = grads_one * jnp.where((line >= virial_row) & (line < virial_row + 64), 1.0, loss_scale)
    two = grads_two * loss_scale
    core = group % 2 == 1
    x = jnp.where(core, one, two) + swap(jnp.where(core, two, one), "dp", 1)
    quarter = G_ROWS // 4

    def piece(k):
        return lax.dynamic_slice_in_dim(x, (plane ^ k) * quarter, quarter, 0)

    def plane_move(k):
        return lambda g, p: (g ^ (2 * (k >> 1)), p ^ (k & 1))

    joined = exchange(jnp.concatenate([piece(1), force_sent]), plane_move(1))
    second, third = exchange(piece(2), plane_move(2)), exchange(piece(3), plane_move(3))
    force_a, force_b = joined[quarter : quarter + 8], joined[quarter + 8 :]
    y = piece(0) + joined[:quarter] + second + third
    for n in range(levels):
        one_bit, two_bit = bits[n], bits[(n + 1) % levels]
        joined = exchange(jnp.concatenate([y, force_b]), lambda g, p: (g, p ^ (two_bit if g % 2 else one_bit)))
        y = y + joined[:quarter]
        force_b = jnp.concatenate([force_b, joined[quarter:]])
    x = jnp.concatenate([y] + [exchange(y, plane_move(k)) for k in (1, 2, 3)])
    other = swap(x, "dp", 1)
    weights = (embedding,) + layer + (readout_mid, out_row)
    outs = (f32(1, 1), f32(3, atom_count), f32(1, 3, 3)) + tuple(f32(*x.shape) for x in weights)
    result = call(
        functools.partial(final_kernel, halo),
        "final",
        outs,
        [smem(), smem()] + [vmem()] * 6,
        [smem()] + [whole(x) for x in outs[1:]],
        [pltpu.VMEM((G_ROWS, LANES), F32)] * 2,
        10**8,
        par, cell, energy, force, force_a, force_b, x, other,
    )
    return (result[0].reshape(1),) + tuple(result[1:-1]) + (result[-1].reshape(LANES),)


def solution(mesh):
    both = ("dp", "atom")
    return jax.shard_map(
        local,
        mesh=mesh,
        in_specs=(
            P(None, both), P(both), P(None, both), P(both), P(None, None, both), P("dp", None, None), P("dp"),
        ) + (P(),) * 8,
        out_specs=(P("dp"), P(None, both), P("dp", None, None)) + (P(),) * 8,
        check_vma=False,
    )
```

```python
import functools

import jax
import jax.numpy as jnp
from jax import lax
from jax.experimental import pallas as pl
from jax.experimental.pallas import tpu as pltpu
from jax.sharding import PartitionSpec as P

F32 = jnp.float32
BF16 = jnp.bfloat16
LANES = 128
HALF = 64
ROWS = 16
VMEM_LIMIT = 20 * 1024 * 1024
G_ROWS = 928
MID_ROWS = 88


def split(x):
    high = x.astype(BF16)
    return high, (x - high.astype(F32)).astype(BF16)


def mm(a, b):
    return lax.dot_general(a, b, (((1,), (0,)), ((), ())), preferred_element_type=F32)


def mm_nt(a, b):
    return lax.dot_general(a, b, (((1,), (1,)), ((), ())), preferred_element_type=F32)


def mm3(a, b):
    ah, al = split(a)
    bh, bl = split(b)
    return mm(ah, bh) + (mm(ah, bl) + mm(al, bh))


def mm3_nt(a, b):
    ah, al = split(a)
    bh, bl = split(b)
    return mm_nt(ah, bh) + (mm_nt(ah, bl) + mm_nt(al, bh))


def sigmoid(x):
    return 0.5 * jnp.tanh(0.5 * x) + 0.5


def lane_ids(rows):
    return lax.broadcasted_iota(jnp.int32, (rows, LANES), 1)


def twice(x, half):
    low = lane_ids(x.shape[0]) < HALF
    other = pltpu.roll(x, HALF, 1)
    return jnp.where(low, x, other) if half == 0 else jnp.where(low, other, x)


def folded(first, second):
    low = lane_ids(first.shape[0]) < HALF
    return jnp.where(low, first + pltpu.roll(first, HALF, 1), second + pltpu.roll(second, HALF, 1))


def windows(own, beside, halo):
    lane = lane_ids(own.shape[0])
    return jnp.where(lane < LANES - halo, own, beside), jnp.where(lane >= halo, own, beside)


def packed(parts, halo, tail):
    lane = lane_ids(parts[0].shape[0])
    out = None
    for q, x in enumerate(parts):
        turn = (halo * (q + 1) if tail else halo * q) % LANES
        x = pltpu.roll(x, turn, 1) if turn else x
        out = x if out is None else jnp.where(lane < halo * q, out, x)
    return out


def unpacked(pack, q, halo, tail):
    turn = (LANES - halo * (q + 1) if tail else LANES - halo * q) % LANES
    return pltpu.roll(pack, turn, 1) if turn else pack


def is_even(par_ref, shape):
    return (jnp.zeros(shape, jnp.int32) + par_ref[0]) == 0


def prepare_weights(rin_ref, rout_ref, ri4, ro3, groups):
    rh, rl = split(rin_ref[0])
    rows = jnp.concatenate([rh, rh, rl, rl], axis=0).astype(F32)
    ri4[...] = rows.T.astype(BF16)
    wh, wl = split(rout_ref[0])
    for place, g in enumerate(groups):
        cols = slice(g * LANES, (g + 1) * LANES)
        th = wh[:, cols].astype(F32).T.astype(BF16)
        tl = wl[:, cols].astype(F32).T.astype(BF16)
        out = slice(place * LANES, (place + 1) * LANES)
        ro3[out, 0:LANES] = th
        ro3[out, LANES : 2 * LANES] = th
        ro3[out, 2 * LANES : 3 * LANES] = tl


def prepare_back(rin_ref, rout_ref, rib, rob, groups):
    rh, rl = split(rin_ref[0])
    count = rh.shape[0]
    rib[0:count, 0:LANES] = rh
    rib[0:count, LANES:] = rh
    rib[count:, 0:LANES] = rl
    rib[count:, LANES:] = rl
    wh, wl = split(rout_ref[0])
    width = len(groups) * LANES
    for place, g in enumerate(groups):
        cols = slice(g * LANES, (g + 1) * LANES)
        for copy in range(2):
            out = slice(copy * width + place * LANES, copy * width + (place + 1) * LANES)
            rob[0:LANES, out] = wh[:, cols]
            rob[LANES:, out] = wl[:, cols]


def store_tables(tab, parts, besides, halo):
    for q, (own, beside) in enumerate(zip(parts, besides)):
        for h, table in enumerate(windows(own, beside, halo)):
            hi, lo = split(table)
            tab[h, q * LANES : (q + 1) * LANES, 0:LANES] = hi
            tab[h, q * LANES : (q + 1) * LANES, LANES:] = lo


def centre_offsets(rows, basis_count):
    place = lax.broadcasted_iota(jnp.int32, (basis_count, LANES), 0).astype(F32)
    centres = 8.0 * place / (basis_count - 1)
    return jnp.concatenate([g[3:4] - centres for g in rows], axis=1)


def sharpness(basis_count):
    return 0.5 * ((basis_count - 1) / 8.0) ** 2


def edge_rows(geom, t):
    return [geom[t * ROWS + q] for q in range(ROWS)]


def radial(rows, t, ri4, ro3, kept, basis_count):
    filters_ref, hidden_ref, basis_ref, slope_ref = kept
    offset = centre_offsets(rows, basis_count)
    bh, bl = split(jnp.exp(-sharpness(basis_count) * offset * offset))
    basis_ref[t] = jnp.concatenate([bh, bl], axis=0)
    pre = mm(ri4[...], jnp.concatenate([bh, bl, bh, bl], axis=0))
    gate = sigmoid(pre)
    mask = jnp.concatenate([g[4:5] for g in rows], axis=1)
    slope_ref[t] = mask * (gate * (1.0 + pre * (1.0 - gate)))
    hh, hl = split(pre * gate * mask)
    hidden_ref[t] = jnp.concatenate([hh, hl], axis=0)
    filters = mm(ro3[...], jnp.concatenate([hh, hl, hh], axis=0))
    filters_ref[t] = filters
    return filters


def one_hot_of(rows):
    place = lax.broadcasted_iota(jnp.int32, (LANES, LANES), 0).astype(F32)
    return jnp.concatenate(
        [jnp.where(place == g[5:6], 1.0, 0.0).astype(BF16) for g in rows], axis=1
    )


def part(x, group, q):
    return x[group * LANES : (group + 1) * LANES, q * LANES : (q + 1) * LANES]


def radial_edges(geom, ri4, ro3, kept, basis_count):
    def step(t, carry):
        radial(edge_rows(geom, t), t, ri4, ro3, kept, basis_count)
        return carry

    for t in range(geom.shape[0] // ROWS):
        step(t, 0)


def forward_edges(geom, tab, acc, found_ref, filters_of, vectors):
    per_half = geom.shape[0] // 2 // ROWS
    acc[...] = jnp.zeros(acc.shape, F32)
    wide = 2 if vectors else 1

    def step(t, carry):
        h = t // per_half
        rows = edge_rows(geom, t)
        filters = filters_of(rows, t)
        hot = one_hot_of(rows)
        found = mm(tab[h], jnp.concatenate([hot, hot], axis=0))
        found_ref[t] = found
        sums = [None] * 4
        for q, g in enumerate(rows):
            s = part(found, 0, q)
            terms = [part(filters, 0, q) * s]
            push = part(filters, wide, q) * s
            for c in range(3):
                term = push * g[c : c + 1]
                if vectors:
                    term = term + part(filters, 1, q) * part(found, 1 + c, q)
                terms.append(term)
            sums = [x if y is None else y + x for x, y in zip(terms, sums)]
        for n in range(4):
            acc[h, n] += sums[n]
        return carry

    for t in range(2 * per_half):
        step(t, 0)


def aggregates(acc, scale):
    return [folded(acc[0, n], acc[1, n]) * scale for n in range(4)]


def node_forward(agg, sm, vm, vg):
    mixed = mm3(vm.T, jnp.concatenate(agg[1:], axis=1))
    w = [mixed[:, c * LANES : (c + 1) * LANES] for c in range(3)]
    size = jnp.sqrt(w[0] * w[0] + w[1] * w[1] + w[2] * w[2] + 1.0)
    u = mm3(sm.T, agg[0]) + (size - 1.0)
    gate = sigmoid(mm3(vg.T, agg[0]))
    return w, size, u, gate


def node_backward(agg, w, size, u, gate, sm, vm, vg, ds, dv, scale):
    act = sigmoid(u)
    du = ds * (act * (1.0 + u * (1.0 - act)))
    ratio = du / size
    dw = [w[c] * ratio + dv[c] * gate for c in range(3)]
    dq = (dv[0] * w[0] + dv[1] * w[1] + dv[2] * w[2]) * gate * (1.0 - gate)
    dw_all = jnp.concatenate(dw, axis=1)
    da_s = (mm3(sm, du) + mm3(vg, dq)) * scale
    da_v = mm3(vm, dw_all) * scale
    da = [da_s] + [da_v[:, c * LANES : (c + 1) * LANES] for c in range(3)]
    g_sm = mm3_nt(agg[0], du)
    g_vg = mm3_nt(agg[0], dq)
    g_vm = mm3_nt(jnp.concatenate(agg[1:], axis=1), dw_all)
    return da, g_sm, g_vm, g_vg


def source_terms(rows, filters, found, gs, gv, vectors):
    wide = 2 if vectors else 1
    columns = []
    for q, g in enumerate(rows):
        along = gv[0] * g[0:1] + gv[1] * g[1:2] + gv[2] * g[2:3]
        sources = [part(filters, 0, q) * gs + part(filters, wide, q) * along]
        if vectors:
            f_v = part(filters, 1, q)
            sources += [f_v * gv[c] for c in range(3)]
        columns.append(jnp.concatenate(sources, axis=0))
    return columns


def scatter(columns, hot):
    sh, sl = split(jnp.concatenate(columns, axis=1))
    return mm_nt(jnp.concatenate([sh, sl], axis=1), jnp.concatenate([hot, hot], axis=1))


def step_derivatives(gacc, h):
    return gacc[h, 0], [gacc[h, 1 + c] for c in range(3)]


def filter_terms(rows, t, kept, found, gs, gv, rib, rob, dro, dri, basis_count, vectors):
    filters_ref, hidden_ref, basis_ref, slope_ref = kept
    wide = 2 if vectors else 1
    d_filters, d_dirs = [], []
    for q, g in enumerate(rows):
        s = part(found, 0, q)
        along = gv[0] * g[0:1] + gv[1] * g[1:2] + gv[2] * g[2:3]
        groups = [gs * s]
        if vectors:
            v = [part(found, 1 + c, q) for c in range(3)]
            groups.append(gv[0] * v[0] + gv[1] * v[1] + gv[2] * v[2])
        groups.append(s * along)
        d_filters.append(jnp.concatenate(groups, axis=0))
        push = part(filters_ref.at[t], wide, q) * s
        d_dirs.append([jnp.sum(push * gv[c], axis=0, keepdims=True) for c in range(3)])
    fh, fl = split(jnp.concatenate(d_filters, axis=1))
    both = hidden_ref[t]
    dro[...] += mm_nt(jnp.concatenate([fh, fl], axis=1), jnp.concatenate([both, both], axis=1))
    spread = mm(rob[...], jnp.concatenate([fh, fl], axis=0))
    d_pre = (spread[:LANES] + spread[LANES:]) * slope_ref[t]
    ph, plo = split(d_pre)
    bb = basis_ref[t]
    dri[...] += mm_nt(jnp.concatenate([ph, plo], axis=1), jnp.concatenate([bb, bb], axis=1))
    back = mm(rib[...], jnp.concatenate([ph, plo], axis=0))
    d_basis = back[:basis_count] + back[basis_count:]
    basis = bb[:basis_count].astype(F32) + bb[basis_count:].astype(F32)
    offset = centre_offsets(rows, basis_count)
    d_dist = jnp.sum(d_basis * basis * offset, axis=0, keepdims=True) * (-2.0 * sharpness(basis_count))
    return d_dirs, [d_dist[:, q * LANES : (q + 1) * LANES] for q in range(len(rows))]


def radial_grads(dro, dri, out, row_in, row_out, basis_count, groups):
    both = dri[...]
    turned = both + pltpu.roll(both, HALF, 1)
    out[row_in : row_in + basis_count] = turned.T[0:basis_count]
    for place in range(groups):
        rows = slice(place * LANES, (place + 1) * LANES)
        grad = dro[rows, 0:LANES] + dro[rows, LANES:]
        out[row_out + place * LANES : row_out + (place + 1) * LANES] = grad.T


def species_hot(row, count):
    place = lax.broadcasted_iota(jnp.int32, (count, LANES), 0).astype(F32)
    return jnp.where(place == row, 1.0, 0.0).astype(BF16)


def first_features(emb_ref, hot):
    high, rest = split(emb_ref[...])
    low = (emb_ref[...] - high.astype(F32) - rest.astype(F32)).astype(BF16)
    dims = (((0,), (0,)), ((), ()))
    terms = [
        lax.dot_general(x.astype(F32).T.astype(BF16), hot, (((1,), (0,)), ((), ())), preferred_element_type=F32)
        for x in (high, rest, low)
    ]
    return terms[0] + (terms[1] + terms[2])


def from_sides(par_ref, a_ref, b_ref):
    even = is_even(par_ref, a_ref.shape)
    a, b = a_ref[...], b_ref[...]
    return jnp.where(even, a, b), jnp.where(even, b, a)


def species_tables(own_ref, up, down, emb_ref, halo):
    lane = lane_ids(1)
    count = emb_ref.shape[0]
    beside = jnp.where(lane >= LANES - halo, down[3:4], up[3:4])
    hot_own, hot_beside = species_hot(own_ref[3:4], count), species_hot(beside, count)
    return hot_own, hot_beside


def positions(cell_ref, fractions):
    rows = [
        fractions[0:1] * cell_ref[0, 0, c] + fractions[1:2] * cell_ref[0, 1, c] + fractions[2:3] * cell_ref[0, 2, c]
        for c in range(3)
    ]
    return jnp.concatenate(rows + [fractions[3:8]], axis=0)


def prepare_kernel(rin_ref, rout_ref, *outs):
    for layer, groups in enumerate(((0, 2), (0, 1, 2))):
        ri4, ro3, rib, rob = outs[4 * layer : 4 * layer + 4]
        rin, rout = rin_ref.at[pl.ds(layer, 1)], rout_ref.at[pl.ds(layer, 1)]
        prepare_weights(rin, rout, ri4, ro3, groups)
        prepare_back(rin, rout, rib, rob, groups)


def first_kernel(
    halo, par_ref, cell_ref, own_ref, a_ref, b_ref, nb_ref, count_ref, shift_ref, emb_ref, ri4, ro3,
    sm_ref, vm_ref, vg_ref,
    geom_ref, feat_ref, agg_ref, node_ref, send_a, send_b, filters_ref, hidden_ref, basis_ref, slope_ref, found_ref,
    tab, acc,
):
    slots = nb_ref.shape[0]
    basis_count = ri4.shape[1] // 4
    pairs = slots // 2
    up, down = from_sides(par_ref, a_ref, b_ref)
    lane = lane_ids(pairs)
    low = lane < HALF

    def halves(ref, *lead):
        even = ref[(*lead, pl.ds(0, pairs, stride=2), slice(None))]
        odd = ref[(*lead, pl.ds(1, pairs, stride=2), slice(None))]
        return jnp.where(low, even, pltpu.roll(odd, HALF, 1)), jnp.where(low, pltpu.roll(even, HALF, 1), odd)

    nb = halves(nb_ref)
    shift = [halves(shift_ref, a) for a in range(3)]
    row_slot = 2 * lax.broadcasted_iota(jnp.int32, (pairs, LANES), 0) + jnp.where(low, 0, 1)
    own, up, down = [positions(cell_ref, x) for x in (own_ref[...], up, down)]
    lane8 = lane_ids(own.shape[0])
    places = (jnp.where(lane8 < LANES - halo, own, down), jnp.where(lane8 >= halo, own, up))
    for h in range(2):
        index = (nb[h] - halo) & (LANES - 1)
        near = twice(own, h)
        count = twice(count_ref[...], h)
        mask = jnp.where(row_slot < count, 1.0, 0.0).astype(F32)
        steps = [shift[a][h].astype(F32) for a in range(3)]
        r = []
        for c in range(3):
            table = jnp.broadcast_to(places[h][c : c + 1], (pairs, LANES))
            far = jnp.take_along_axis(table, index, axis=1, mode="promise_in_bounds")
            image = steps[0] * cell_ref[0, 0, c] + steps[1] * cell_ref[0, 1, c] + steps[2] * cell_ref[0, 2, c]
            r.append(far - near[c : c + 1] + image)
        dist = jnp.sqrt(r[0] * r[0] + r[1] * r[1] + r[2] * r[2] + 1.0)
        values = [x / dist for x in r] + [dist, mask, index.astype(F32)]
        for n, x in enumerate(values):
            for m in range(pairs):
                geom_ref[h * pairs + m, n : n + 1, :] = x[m : m + 1]
    hot_own, hot_beside = species_tables(own_ref, up, down, emb_ref, halo)
    s, beside = first_features(emb_ref, hot_own), first_features(emb_ref, hot_beside)
    store_tables(tab, [s], [beside], halo)
    kept = (filters_ref, hidden_ref, basis_ref, slope_ref)
    forward_edges(
        geom_ref, tab, acc, found_ref, lambda rows, t: radial(rows, t, ri4, ro3, kept, basis_count), False
    )
    agg = aggregates(acc, slots**-0.5)
    w, size, u, gate = node_forward(agg, sm_ref[0], vm_ref[0], vg_ref[0])
    features = [s + u * sigmoid(u)] + [w[c] * gate for c in range(3)]
    for n, x in enumerate(w + [size, u, gate]):
        node_ref[n] = x
    for n in range(4):
        agg_ref[n] = agg[n]
        feat_ref[n] = features[n]
    tail, head = packed(features, halo, True), packed(features, halo, False)
    even = is_even(par_ref, tail.shape)
    send_a[...] = jnp.where(even, tail, head)
    send_b[...] = jnp.where(even, head, tail)


def radial_kernel(geom_ref, ri4, ro3, filters_ref, hidden_ref, basis_ref, slope_ref):
    radial_edges(geom_ref, ri4, ro3, (filters_ref, hidden_ref, basis_ref, slope_ref), ri4.shape[1] // 4)


def second_kernel(
    halo, par_ref, geom_ref, feat_ref, a_ref, b_ref, filters_ref, sm_ref, vm_ref, vg_ref, mid_ref, out_ref,
    cot_ref, send_a, send_b, grad_ref, mid_tail, gacc, found_ref,
    tab, acc, dtab,
):
    slots = geom_ref.shape[0]
    scale = slots**-0.5
    up, down = from_sides(par_ref, a_ref, b_ref)
    lane = lane_ids(LANES)
    features = [feat_ref[n] for n in range(4)]
    besides = [
        jnp.where(lane >= LANES - halo, unpacked(down, q, halo, True), unpacked(up, q, halo, False)) for q in range(4)
    ]
    store_tables(tab, features, besides, halo)
    forward_edges(geom_ref, tab, acc, found_ref, lambda rows, t: filters_ref.at[t], True)

    @pl.when(par_ref[0] >= 0)
    def _():
        agg = aggregates(acc, scale)
        sm, vm, vg = sm_ref[0], vm_ref[0], vg_ref[0]
        w, size, u, gate = node_forward(agg, sm, vm, vg)
        s = feat_ref[0] + u * sigmoid(u)
        mid = mid_ref[...]
        hidden = mm3(mid.T, s)
        act = sigmoid(hidden)
        shown = hidden * act
        weights = jnp.broadcast_to(out_ref[...], (8, LANES))
        per_atom = mm3(weights, shown)
        send_a[LANES:] = jnp.broadcast_to(jnp.sum(per_atom, axis=1, keepdims=True), (8, LANES))
        weight_column = jnp.broadcast_to(out_ref[...], (LANES, LANES)).T
        d_hidden = weight_column * (act * (1.0 + hidden * (1.0 - act)))
        ds = mm3(mid, d_hidden)
        zero = jnp.zeros((LANES, LANES), F32)
        dv = [zero, zero, zero]
        da, g_sm, g_vm, g_vg = node_backward(agg, w, size, u, gate, sm, vm, vg, ds, dv, scale)
        for n in range(4):
            for h in range(2):
                gacc[h, n] = twice(da[n], h)
        for n, x in enumerate([ds] + dv):
            cot_ref[n] = x
        row = 0
        for grad in (g_sm, g_vm, g_vg):
            grad_ref[row : row + LANES] = grad
            row += LANES
        grad_ref[row : row + 8] = mm3_nt(jnp.ones((8, LANES), F32), shown)
        g_mid = mm3_nt(s, d_hidden)
        grad_ref[row + 8 :] = g_mid[:MID_ROWS]
        mid_tail[...] = g_mid[MID_ROWS:]

    per_half = slots // 2 // ROWS
    dtab[...] = jnp.zeros(dtab.shape, F32)

    def step(t, carry):
        h = t // per_half
        rows = edge_rows(geom_ref, t)
        gs, gv = step_derivatives(gacc, h)
        columns = source_terms(rows, filters_ref.at[t], found_ref.at[t], gs, gv, True)
        dtab[h] += scatter(columns, one_hot_of(rows))
        return carry

    for t in range(2 * per_half):
        step(t, 0)
    firsts = [dtab[0, q * LANES : (q + 1) * LANES] for q in range(4)]
    seconds = [dtab[1, q * LANES : (q + 1) * LANES] for q in range(4)]
    for q in range(4):
        cot_ref[q] += (
            jnp.where(lane < LANES - halo, firsts[q], 0.0) + jnp.where(lane >= halo, seconds[q], 0.0)
        )
    to_prev, to_next = packed(firsts, halo, True), packed(seconds, halo, False)
    even = is_even(par_ref, to_prev.shape)
    send_a[:LANES] = jnp.where(even, to_next, to_prev)
    send_b[...] = jnp.where(even, to_prev, to_next)


def radial_back_kernel(
    t, geom_ref, filters_ref, hidden_ref, basis_ref, slope_ref, found_ref, gacc, rib, rob, *rest
):
    basis_count = rib.shape[0] // 2
    last = len(rest) > 3
    if last:
        dro_first, dri_first, mixed_ref, dgeom_ref, grad_ref, dro, dri = rest
        dro[...] = dro_first[...]
        dri[...] = dri_first[...]
    else:
        dgeom_ref, dro, dri = rest
        dro[...] = jnp.zeros(dro.shape, F32)
        dri[...] = jnp.zeros(dri.shape, F32)
    kept = (filters_ref, hidden_ref, basis_ref, slope_ref)
    rows = edge_rows(geom_ref, t)
    gs, gv = step_derivatives(gacc, t // (geom_ref.shape[0] // 2 // ROWS))
    d_dirs, d_dists = filter_terms(rows, t, kept, found_ref.at[t], gs, gv, rib, rob, dro, dri, basis_count, True)
    for q in range(ROWS):
        for c in range(3):
            dgeom_ref[q, c : c + 1, :] = d_dirs[q][c]
        dgeom_ref[q, 3:4, :] = d_dists[q]
    if last:
        radial_grads(dro, dri, grad_ref, 0, basis_count, basis_count, 3)
        grad_ref[basis_count + 3 * LANES :] = mixed_ref[...]


def third_kernel(
    halo, par_ref, geom_ref, dgeom_one, dgeom_two, agg_ref, node_ref, cot_ref, a_ref, b_ref, own_ref, pa_ref, pb_ref, mid_tail,
    filters_ref, hidden_ref, basis_ref, slope_ref, found_ref, emb_ref, rib, rob, sm_ref, vm_ref, vg_ref,
    force_ref, send_ref, grad_ref,
    gacc, dro, dri, dtab, pull, virial,
):
    basis_count = rib.shape[0] // 2
    slots = geom_ref.shape[0]
    scale = slots**-0.5
    lane = lane_ids(LANES)
    up, down = from_sides(par_ref, a_ref.at[:LANES], b_ref)
    cot = []
    for q in range(4):
        cot.append(
            cot_ref[q]
            + jnp.where(lane >= LANES - halo, unpacked(up, q, halo, True), 0.0)
            + jnp.where(lane < halo, unpacked(down, q, halo, False), 0.0)
        )
    place_up, place_down = from_sides(par_ref, pa_ref, pb_ref)
    hot_own, hot_beside = species_tables(own_ref, place_up, place_down, emb_ref, halo)
    groups = (0, 2)
    count = emb_ref.shape[0]

    @pl.when(par_ref[0] >= 0)
    def _():
        agg = [agg_ref[n] for n in range(4)]
        sm, vm, vg = sm_ref[0], vm_ref[0], vg_ref[0]
        w, (size, u, gate) = [node_ref[c] for c in range(3)], [node_ref[n] for n in range(3, 6)]
        da, g_sm, g_vm, g_vg = node_backward(agg, w, size, u, gate, sm, vm, vg, cot[0], cot[1:], scale)
        for n in range(4):
            for h in range(2):
                gacc[h, n] = twice(da[n], h)
        row = count + basis_count + 2 * LANES
        for g in (g_sm, g_vm, g_vg):
            grad_ref[row : row + LANES] = g
            row += LANES

    pull[...] = jnp.zeros(pull.shape, F32)
    virial[...] = jnp.zeros(virial.shape, F32)

    def finish(row, g, d_dir, d_dist):
        more = (dgeom_one, dgeom_two)[row // ROWS][row % ROWS]
        dist = g[3:4]
        toward = [g[c : c + 1] for c in range(3)]
        turn = [d_dir[c] + more[c : c + 1] for c in range(3)]
        inner = turn[0] * toward[0] + turn[1] * toward[1] + turn[2] * toward[2]
        stretch = d_dist + more[3:4]
        inverse = 1.0 / dist
        dr = [(turn[c] - toward[c] * inner) * inverse + stretch * toward[c] for c in range(3)]
        r = [toward[c] * dist for c in range(3)]
        lines = jnp.concatenate(dr + [jnp.zeros((13, LANES), F32)], axis=0)
        products = [r[a] * dr[c] for a in range(3) for c in range(3)]
        return lines, jnp.concatenate(products + [jnp.zeros((7, LANES), F32)], axis=0)

    kept = (filters_ref, hidden_ref, basis_ref, slope_ref)
    per_half = slots // 2 // ROWS
    dro[...] = jnp.zeros(dro.shape, F32)
    dri[...] = jnp.zeros(dri.shape, F32)
    dtab[...] = jnp.zeros(dtab.shape, F32)

    def step(t, carry):
        h = t // per_half
        rows = edge_rows(geom_ref, t)
        gs, gv = step_derivatives(gacc, h)
        found = found_ref.at[t]
        d_dirs, d_dists = filter_terms(rows, t, kept, found, gs, gv, rib, rob, dro, dri, basis_count, False)
        columns = source_terms(rows, filters_ref.at[t], found, gs, gv, False)
        pairs = [finish(t * ROWS + q, g, d_dirs[q], d_dists[q]) for q, g in enumerate(rows)]
        pull[h] += sum(x for x, _ in pairs[1:]) + pairs[0][0]
        virial[...] += sum(x for _, x in pairs[1:]) + pairs[0][1]
        columns = [jnp.concatenate([x, y], axis=0) for x, (y, _) in zip(columns, pairs)]
        dtab[h] += scatter(columns, one_hot_of(rows))
        return carry

    for t in range(2 * per_half):
        step(t, 0)
    first, second = dtab[0, 0:LANES], dtab[1, 0:LANES]
    own_cot = cot[0] + jnp.where(lane < LANES - halo, first, 0.0) + jnp.where(lane >= halo, second, 0.0)
    side_cot = jnp.where(lane >= LANES - halo, first, 0.0) + jnp.where(lane < halo, second, 0.0)
    grad = 0.0
    for hot, value in ((hot_own, own_cot), (hot_beside, side_cot)):
        hi, lo = split(value)
        grad = grad + (mm_nt(hot, hi) + mm_nt(hot, lo))
    grad_ref[0:count] = grad
    row = count
    radial_grads(dro, dri, grad_ref, row, row + basis_count, basis_count, len(groups))
    row += basis_count + 5 * LANES
    grad_ref[row:] = jnp.zeros((grad_ref.shape[0] - row, LANES), F32)
    grad_ref[row + 64 : row + 64 + mid_tail.shape[0]] = mid_tail[...]
    total = jnp.broadcast_to(jnp.sum(virial[...], axis=1, keepdims=True), virial.shape)
    grad_ref[pl.ds(pl.multiple_of(row + 16 * par_ref[1], 16), 16)] = total
    lane16 = lane_ids(16)
    first, second = dtab[0, LANES:], dtab[1, LANES:]
    force_ref[...] = (
        jnp.where(lane16 < LANES - halo, first, 0.0)
        + jnp.where(lane16 >= halo, second, 0.0)
        - folded(pull[0], pull[1])
    )
    even = is_even(par_ref, first.shape)
    send_ref[0:8] = jnp.where(even, second, first)[0:8]
    send_ref[8:16] = jnp.where(even, first, second)[0:8]


def final_kernel(
    halo, par_ref, cell_ref, sum_energy, force_ref, a_ref, b_ref, mine_turned, other_turned,
    energy_ref, forces_ref, stress_ref, emb_ref, rin_ref, rout_ref, sm_ref, vm_ref, vg_ref, mid_ref, out_ref,
    mine, other,
):
    energy_ref[0, 0] = jnp.max(sum_energy[0:1])
    rows = mine.shape[0] // 4
    for c in range(4):
        turned = pl.ds(pl.multiple_of((par_ref[2] ^ c) * rows, 8), rows)
        mine[c * rows : (c + 1) * rows] = mine_turned[turned]
        other[c * rows : (c + 1) * rows] = other_turned[turned]
    lane = lane_ids(8)
    up, down = from_sides(par_ref, a_ref, b_ref.at[pl.ds(pl.multiple_of(8 * par_ref[3], 8), 8)])
    force = force_ref[0:8] + jnp.where(lane >= LANES - halo, up, 0.0) + jnp.where(lane < halo, down, 0.0)
    forces_ref[...] = -force[0:3]
    count, basis_count = emb_ref.shape[0], rin_ref.shape[1]
    m = [[cell_ref[0, a, c] for c in range(3)] for a in range(3)]
    det = (
        m[0][0] * (m[1][1] * m[2][2] - m[1][2] * m[2][1])
        - m[0][1] * (m[1][0] * m[2][2] - m[1][2] * m[2][0])
        + m[0][2] * (m[1][0] * m[2][1] - m[1][1] * m[2][0])
    )

    def write(one, two):
        emb_ref[...] = one[0:count]
        row = count
        rin_ref[0] = one[row : row + basis_count]
        rin_ref[1] = two[0:basis_count]
        row += basis_count
        rout_ref[0, :, 0:LANES] = one[row : row + LANES]
        rout_ref[0, :, LANES : 2 * LANES] = jnp.zeros((LANES, LANES), F32)
        rout_ref[0, :, 2 * LANES :] = one[row + LANES : row + 2 * LANES]
        row += 2 * LANES
        line = basis_count
        for g in range(3):
            rout_ref[1, :, g * LANES : (g + 1) * LANES] = two[line : line + LANES]
            line += LANES
        for ref in (sm_ref, vm_ref, vg_ref):
            ref[0] = one[row : row + LANES]
            ref[1] = two[line : line + LANES]
            row += LANES
            line += LANES
        out_ref[...] = two[line : line + 1]
        mid_ref[0:MID_ROWS] = two[line + 8 : line + 8 + MID_ROWS]
        mid_ref[MID_ROWS:] = one[row + 64 : row + 64 + LANES - MID_ROWS]
        virial = one[pl.ds(pl.multiple_of(row + 16 * par_ref[1], 16), 16)]
        place = lane_ids(1)
        lines = [
            jnp.where(place == 0, virial[3 * a : 3 * a + 1], jnp.where(place == 1, virial[3 * a + 1 : 3 * a + 2], virial[3 * a + 2 : 3 * a + 3]))
            for a in range(3)
        ]
        stress = jnp.concatenate(lines, axis=0) / (jnp.zeros((3, LANES), F32) + det)
        stress_ref[...] = stress[:, 0:3]

    @pl.when(par_ref[1] % 2 == 0)
    def _():
        write(other, mine)

    @pl.when(par_ref[1] % 2 == 1)
    def _():
        write(mine, other)


def side_one(x, axis):
    return lax.ppermute(x, axis, [(i, i ^ 1) for i in range(lax.axis_size(axis))])


def side_two(x, axis):
    size = lax.axis_size(axis)
    return lax.ppermute(x, axis, [(i, (i + 1) % size if i % 2 else (i - 1) % size) for i in range(size)])


def after(x, *others):
    return lax.optimization_barrier((x,) + others)[0]


def swap(x, axis, bit):
    return lax.ppermute(x, axis, [(i, i ^ bit) for i in range(lax.axis_size(axis))])


def layer_spec(x, layer):
    rest = x.shape[1:]
    return pl.BlockSpec((1,) + rest, lambda i: (layer,) + (0,) * len(rest))


def vmem():
    return pl.BlockSpec(memory_space=pltpu.VMEM)


def smem():
    return pl.BlockSpec(memory_space=pltpu.SMEM)


def whole(x):
    return pl.BlockSpec(x.shape, lambda i: (0,) * len(x.shape))


def f32(*shape):
    return jax.ShapeDtypeStruct(shape, F32)


def call(kernel, name, outs, in_specs, out_specs, scratch, flops, *args):
    return pl.pallas_call(
        kernel,
        grid=(1,),
        out_shape=outs,
        in_specs=in_specs,
        out_specs=out_specs,
        scratch_shapes=scratch,
        compiler_params=pltpu.CompilerParams(vmem_limit_bytes=VMEM_LIMIT),
        cost_estimate=pl.CostEstimate(flops=flops, bytes_accessed=flops // 500, transcendentals=0),
        name=name,
    )(*args)


def exchange(x, moves):
    groups, slabs = lax.axis_size("dp"), lax.axis_size("atom")
    route = []
    for g in range(groups):
        for p in range(slabs):
            to_g, to_p = moves(g, p)
            route.append((g * slabs + p, to_g * slabs + to_p))
    return lax.ppermute(x, ("dp", "atom"), route)


def local(
    frac, species, neighbours, counts, shifts, cell, energy_ref, embedding, radial_in, radial_out, scalar_mix,
    vector_mix, vector_gate, readout_mid, readout_out,
):
    atom_count = frac.shape[1]
    halo = atom_count // 4
    slots = neighbours.shape[0]
    basis_count = radial_in.shape[1]
    me = lax.axis_index("atom")
    group = lax.axis_index("dp")
    counts_row, out_row = counts[None], readout_out[None]
    own = jnp.concatenate([frac, species.astype(F32)[None], jnp.zeros((4, atom_count), F32)], axis=0)
    side_a, side_b = side_one(own, "atom"), side_two(own, "atom")
    plane = group // 2 * 2 + me % 2
    slabs = lax.axis_size("atom")
    levels = (slabs - 1).bit_length() - 1
    bits = [2 << n for n in range(levels)]
    opposite = jnp.where(me % 2 == 1, (me + 1) % slabs, (me + slabs - 1) % slabs)
    turned = (me ^ opposite ^ 1) >> 1
    turned = jnp.where(group % 2 == 1, (turned >> 1) | ((turned & 1) << (levels - 1)), turned)
    par = jnp.stack([me % 2, group, plane, turned]).astype(jnp.int32)
    layer = (radial_in, radial_out, scalar_mix, vector_mix, vector_gate)
    block = f32(LANES, LANES)
    edges, steps = ROWS * LANES, slots // ROWS

    def kept(groups):
        halves = tuple(jax.ShapeDtypeStruct((steps, n, edges), BF16) for n in (2 * LANES, 2 * basis_count))
        return (f32(steps, groups * LANES, edges),) + halves + (f32(steps, LANES, edges),)

    prepared = call(
        prepare_kernel,
        "prepare",
        tuple(
            jax.ShapeDtypeStruct(shape, BF16)
            for n in (2, 3)
            for shape in (
                (LANES, 4 * basis_count), (n * LANES, 3 * LANES), (2 * basis_count, 2 * LANES), (2 * LANES, 2 * n * LANES)
            )
        ),
        [vmem()] * 2,
        [vmem()] * 8,
        [],
        10**10,
        radial_in, radial_out,
    )
    geom, feat, agg, node, feat_a, feat_b, *kept_one = call(
        functools.partial(first_kernel, halo),
        "layer_one",
        (f32(slots, 8, LANES), f32(4, LANES, LANES), f32(4, LANES, LANES), f32(6, LANES, LANES), block, block) + kept(2)
        + (f32(steps, LANES, edges),),
        [smem(), smem()] + [vmem()] * 9 + [layer_spec(x, 0) for x in layer[2:]],
        [vmem()] * 11,
        [
            pltpu.VMEM((2, LANES, 2 * LANES), BF16),
            pltpu.VMEM((2, 4, LANES, LANES), F32),
        ],
        3 * 10**9,
        par, cell, own, side_a, side_b, neighbours, counts_row, shifts, embedding, *prepared[:2], *layer[2:],
    )
    feat_a, feat_b = side_one(feat_a, "atom"), side_two(feat_b, "atom")
    kept_two = call(
        radial_kernel,
        "radial_two",
        kept(3),
        [vmem()] * 3,
        [vmem()] * 4,
        [],
        3 * 10**9,
        geom, *prepared[4:6],
    )
    tail_rows = LANES - MID_ROWS
    mixed_rows = 3 * LANES + 8 + MID_ROWS
    cot, cot_a, cot_b, mixed, mid_tail, gacc, found_two = call(
        functools.partial(second_kernel, halo),
        "layer_two",
        (
            f32(4, LANES, LANES), f32(LANES + 8, LANES), block, f32(mixed_rows, LANES), f32(tail_rows, LANES),
            f32(2, 4, LANES, LANES), f32(steps, 4 * LANES, edges),
        ),
        [smem()] + [vmem()] * 5 + [layer_spec(x, 1) for x in layer[2:]] + [whole(readout_mid), whole(out_row)],
        [vmem()] * 7,
        [
            pltpu.VMEM((2, 4 * LANES, 2 * LANES), BF16),
            pltpu.VMEM((2, 4, LANES, LANES), F32),
            pltpu.VMEM((2, 4 * LANES, LANES), F32),
        ],
        5 * 10**9,
        par, geom, feat, feat_a, feat_b, kept_two[0], *layer[2:], readout_mid, out_row,
    )
    energy = cot_a[LANES:]
    cot_a = side_one(cot_a, "atom")
    back_args = (geom, *kept_two, found_two, gacc, *prepared[6:8])
    sums = (f32(3 * LANES, 2 * LANES), f32(LANES, 2 * basis_count))
    dgeom_one, dro_first, dri_first = call(
        functools.partial(radial_back_kernel, 0),
        "radial_two_back",
        (f32(ROWS, 8, LANES),) + sums,
        [vmem()] * 9,
        [vmem()] * 3,
        [],
        3 * 10**9,
        *back_args,
    )
    energy = energy + cot_a[LANES:]
    moved = swap(energy, "atom", 2)
    cot_b = side_two(after(cot_b, dri_first), "atom")
    dgeom_two, grads_two = call(
        functools.partial(radial_back_kernel, 1),
        "radial_two_back_last",
        (f32(ROWS, 8, LANES), f32(G_ROWS, LANES)),
        [vmem()] * 12,
        [vmem()] * 2,
        [pltpu.VMEM(x.shape, F32) for x in sums],
        3 * 10**9,
        *back_args, dro_first, after(dri_first, energy), mixed,
    )
    energy = after(energy + moved, dgeom_two)
    if slabs > 4:
        energy = energy + swap(energy, "atom", 4)
    force, force_sent, grads_one = call(
        functools.partial(third_kernel, halo),
        "layer_one_back",
        (f32(16, LANES), f32(16, LANES), f32(G_ROWS, LANES)),
        [smem()] + [vmem()] * 20 + [layer_spec(x, 0) for x in layer[2:]],
        [vmem()] * 3,
        [
            pltpu.VMEM((2, 4, LANES, LANES), F32),
            pltpu.VMEM((2 * LANES, 2 * LANES), F32),
            pltpu.VMEM((LANES, 2 * basis_count), F32),
            pltpu.VMEM((2, LANES + 16, LANES), F32),
            pltpu.VMEM((2, 16, LANES), F32),
            pltpu.VMEM((16, LANES), F32),
        ],
        6 * 10**9,
        par, geom, dgeom_one, dgeom_two, agg, node, cot, cot_a, cot_b, own, side_a, side_b, mid_tail, *kept_one,
        embedding, *prepared[2:4], *layer[2:],
    )
    for bit in bits[2:]:
        energy = energy + swap(energy, "atom", bit)
    cell_atoms = atom_count * slabs
    loss_scale = 2.0 * (energy[0:1] / cell_atoms - energy_ref[0]) / cell_atoms
    virial_row = embedding.shape[0] + basis_count + 5 * LANES
    line = lax.broadcasted_iota(jnp.int32, (G_ROWS, 1), 0)
    one = grads_one * jnp.where((line >= virial_row) & (line < virial_row + 64), 1.0, loss_scale)
    two = grads_two * loss_scale
    core = group % 2 == 1
    x = jnp.where(core, one, two) + swap(jnp.where(core, two, one), "dp", 1)
    quarter = G_ROWS // 4

    def piece(k):
        return lax.dynamic_slice_in_dim(x, (plane ^ k) * quarter, quarter, 0)

    def plane_move(k):
        return lambda g, p: (g ^ (2 * (k >> 1)), p ^ (k & 1))

    joined = exchange(jnp.concatenate([piece(1), force_sent]), plane_move(1))
    second, third = exchange(piece(2), plane_move(2)), exchange(piece(3), plane_move(3))
    force_a, force_b = joined[quarter : quarter + 8], joined[quarter + 8 :]
    y = piece(0) + joined[:quarter] + second + third
    for n in range(levels):
        one_bit, two_bit = bits[n], bits[(n + 1) % levels]
        joined = exchange(jnp.concatenate([y, force_b]), lambda g, p: (g, p ^ (two_bit if g % 2 else one_bit)))
        y = y + joined[:quarter]
        force_b = jnp.concatenate([force_b, joined[quarter:]])
    x = jnp.concatenate([y] + [exchange(y, plane_move(k)) for k in (1, 2, 3)])
    other = swap(x, "dp", 1)
    weights = (embedding,) + layer + (readout_mid, out_row)
    outs = (f32(1, 1), f32(3, atom_count), f32(3, 3)) + tuple(f32(*x.shape) for x in weights)
    result = call(
        functools.partial(final_kernel, halo),
        "final",
        outs,
        [smem(), smem()] + [vmem()] * 6,
        [smem()] + [whole(x) for x in outs[1:]],
        [pltpu.VMEM((G_ROWS, LANES), F32)] * 2,
        10**8,
        par, cell, energy, force, force_a, force_b, x, other,
    )
    return (result[0].reshape(1), result[1], result[2][None]) + tuple(result[3:-1]) + (result[-1].reshape(LANES),)


def solution(mesh):
    both = ("dp", "atom")
    return jax.shard_map(
        local,
        mesh=mesh,
        in_specs=(
            P(None, both), P(both), P(None, both), P(both), P(None, None, both), P("dp", None, None), P("dp"),
        ) + (P(),) * 8,
        out_specs=(P("dp"), P(None, both), P("dp", None, None)) + (P(),) * 8,
        check_vma=False,
    )
```

```python
import functools

import jax
import jax.numpy as jnp
from jax import lax
from jax.experimental import pallas as pl
from jax.experimental.pallas import tpu as pltpu
from jax.sharding import PartitionSpec as P

F32 = jnp.float32
BF16 = jnp.bfloat16
LANES = 128
HALF = 64
ROWS = 16
VMEM_LIMIT = 20 * 1024 * 1024
G_ROWS = 896
MID_ROWS = 56


def split(x):
    high = x.astype(BF16)
    return high, (x - high.astype(F32)).astype(BF16)


def mm(a, b):
    return lax.dot_general(a, b, (((1,), (0,)), ((), ())), preferred_element_type=F32)


def mm_nt(a, b):
    return lax.dot_general(a, b, (((1,), (1,)), ((), ())), preferred_element_type=F32)


def mm3(a, b):
    ah, al = split(a)
    bh, bl = split(b)
    return mm(ah, bh) + (mm(ah, bl) + mm(al, bh))


def mm3_nt(a, b):
    ah, al = split(a)
    bh, bl = split(b)
    return mm_nt(ah, bh) + (mm_nt(ah, bl) + mm_nt(al, bh))


def sigmoid(x):
    return 0.5 * jnp.tanh(0.5 * x) + 0.5


def lane_ids(rows):
    return lax.broadcasted_iota(jnp.int32, (rows, LANES), 1)


def twice(x, half):
    low = lane_ids(x.shape[0]) < HALF
    other = pltpu.roll(x, HALF, 1)
    return jnp.where(low, x, other) if half == 0 else jnp.where(low, other, x)


def folded(first, second):
    low = lane_ids(first.shape[0]) < HALF
    return jnp.where(low, first + pltpu.roll(first, HALF, 1), second + pltpu.roll(second, HALF, 1))


def windows(own, beside, halo):
    lane = lane_ids(own.shape[0])
    return jnp.where(lane < LANES - halo, own, beside), jnp.where(lane >= halo, own, beside)


def packed(parts, halo, tail):
    lane = lane_ids(parts[0].shape[0])
    out = None
    for q, x in enumerate(parts):
        turn = (halo * (q + 1) if tail else halo * q) % LANES
        x = pltpu.roll(x, turn, 1) if turn else x
        out = x if out is None else jnp.where(lane < halo * q, out, x)
    return out


def unpacked(pack, q, halo, tail):
    turn = (LANES - halo * (q + 1) if tail else LANES - halo * q) % LANES
    return pltpu.roll(pack, turn, 1) if turn else pack


def is_even(par_ref, shape):
    return (jnp.zeros(shape, jnp.int32) + par_ref[0]) == 0


def prepare_weights(rin_ref, rout_ref, ri4, ro3, groups):
    rh, rl = split(rin_ref[0])
    rows = jnp.concatenate([rh, rh, rl, rl], axis=0).astype(F32)
    ri4[...] = rows.T.astype(BF16)
    wh, wl = split(rout_ref[0])
    for place, g in enumerate(groups):
        cols = slice(g * LANES, (g + 1) * LANES)
        th = wh[:, cols].astype(F32).T.astype(BF16)
        tl = wl[:, cols].astype(F32).T.astype(BF16)
        out = slice(place * LANES, (place + 1) * LANES)
        ro3[out, 0:LANES] = th
        ro3[out, LANES : 2 * LANES] = th
        ro3[out, 2 * LANES : 3 * LANES] = tl


def prepare_back(rin_ref, rout_ref, rib, rob, groups):
    rh, rl = split(rin_ref[0])
    count = rh.shape[0]
    rib[0:count, 0:LANES] = rh
    rib[0:count, LANES:] = rh
    rib[count:, 0:LANES] = rl
    rib[count:, LANES:] = rl
    wh, wl = split(rout_ref[0])
    width = len(groups) * LANES
    for place, g in enumerate(groups):
        cols = slice(g * LANES, (g + 1) * LANES)
        for copy in range(2):
            out = slice(copy * width + place * LANES, copy * width + (place + 1) * LANES)
            rob[0:LANES, out] = wh[:, cols]
            rob[LANES:, out] = wl[:, cols]


def store_tables(tab, parts, besides, halo):
    for q, (own, beside) in enumerate(zip(parts, besides)):
        for h, table in enumerate(windows(own, beside, halo)):
            hi, lo = split(table)
            tab[h, q * LANES : (q + 1) * LANES, 0:LANES] = hi
            tab[h, q * LANES : (q + 1) * LANES, LANES:] = lo


def centre_offsets(rows, basis_count):
    place = lax.broadcasted_iota(jnp.int32, (basis_count, LANES), 0).astype(F32)
    centres = 8.0 * place / (basis_count - 1)
    return jnp.concatenate([g[3:4] - centres for g in rows], axis=1)


def sharpness(basis_count):
    return 0.5 * ((basis_count - 1) / 8.0) ** 2


def edge_rows(geom, t):
    return [geom[t * ROWS + q] for q in range(ROWS)]


def radial(rows, t, ri4, ro3, kept, basis_count):
    filters_ref, hidden_ref, basis_ref, slope_ref = kept
    offset = centre_offsets(rows, basis_count)
    bh, bl = split(jnp.exp(-sharpness(basis_count) * offset * offset))
    basis_ref[t] = jnp.concatenate([bh, bl], axis=0)
    pre = mm(ri4[...], jnp.concatenate([bh, bl, bh, bl], axis=0))
    gate = sigmoid(pre)
    mask = jnp.concatenate([g[4:5] for g in rows], axis=1)
    slope_ref[t] = mask * (gate * (1.0 + pre * (1.0 - gate)))
    hh, hl = split(pre * gate * mask)
    hidden_ref[t] = jnp.concatenate([hh, hl], axis=0)
    filters = mm(ro3[...], jnp.concatenate([hh, hl, hh], axis=0))
    filters_ref[t] = filters
    return filters


def one_hot_of(rows):
    place = lax.broadcasted_iota(jnp.int32, (LANES, LANES), 0).astype(F32)
    return jnp.concatenate(
        [jnp.where(place == g[5:6], 1.0, 0.0).astype(BF16) for g in rows], axis=1
    )


def part(x, group, q):
    return x[group * LANES : (group + 1) * LANES, q * LANES : (q + 1) * LANES]


def radial_edges(geom, ri4, ro3, kept, basis_count):
    def step(t, carry):
        radial(edge_rows(geom, t), t, ri4, ro3, kept, basis_count)
        return carry

    for t in range(geom.shape[0] // ROWS):
        step(t, 0)


def forward_edges(geom, tab, acc, found_ref, filters_of, vectors):
    per_half = geom.shape[0] // 2 // ROWS
    acc[...] = jnp.zeros(acc.shape, F32)
    wide = 2 if vectors else 1

    def step(t, carry):
        h = t // per_half
        rows = edge_rows(geom, t)
        filters = filters_of(rows, t)
        hot = one_hot_of(rows)
        found = mm(tab[h], jnp.concatenate([hot, hot], axis=0))
        found_ref[t] = found
        sums = [None] * 4
        for q, g in enumerate(rows):
            s = part(found, 0, q)
            terms = [part(filters, 0, q) * s]
            push = part(filters, wide, q) * s
            for c in range(3):
                term = push * g[c : c + 1]
                if vectors:
                    term = term + part(filters, 1, q) * part(found, 1 + c, q)
                terms.append(term)
            sums = [x if y is None else y + x for x, y in zip(terms, sums)]
        for n in range(4):
            acc[h, n] += sums[n]
        return carry

    for t in range(2 * per_half):
        step(t, 0)


def aggregates(acc, scale):
    return [folded(acc[0, n], acc[1, n]) * scale for n in range(4)]


def node_forward(agg, sm, vm, vg):
    mixed = mm3(vm.T, jnp.concatenate(agg[1:], axis=1))
    w = [mixed[:, c * LANES : (c + 1) * LANES] for c in range(3)]
    size = jnp.sqrt(w[0] * w[0] + w[1] * w[1] + w[2] * w[2] + 1.0)
    u = mm3(sm.T, agg[0]) + (size - 1.0)
    gate = sigmoid(mm3(vg.T, agg[0]))
    return w, size, u, gate


def node_backward(agg, w, size, u, gate, sm, vm, vg, ds, dv, scale):
    act = sigmoid(u)
    du = ds * (act * (1.0 + u * (1.0 - act)))
    ratio = du / size
    dw = [w[c] * ratio + dv[c] * gate for c in range(3)]
    dq = (dv[0] * w[0] + dv[1] * w[1] + dv[2] * w[2]) * gate * (1.0 - gate)
    dw_all = jnp.concatenate(dw, axis=1)
    da_s = (mm3(sm, du) + mm3(vg, dq)) * scale
    da_v = mm3(vm, dw_all) * scale
    da = [da_s] + [da_v[:, c * LANES : (c + 1) * LANES] for c in range(3)]
    g_sm = mm3_nt(agg[0], du)
    g_vg = mm3_nt(agg[0], dq)
    g_vm = mm3_nt(jnp.concatenate(agg[1:], axis=1), dw_all)
    return da, g_sm, g_vm, g_vg


def source_terms(rows, filters, found, gs, gv, vectors):
    wide = 2 if vectors else 1
    columns = []
    for q, g in enumerate(rows):
        along = gv[0] * g[0:1] + gv[1] * g[1:2] + gv[2] * g[2:3]
        sources = [part(filters, 0, q) * gs + part(filters, wide, q) * along]
        if vectors:
            f_v = part(filters, 1, q)
            sources += [f_v * gv[c] for c in range(3)]
        columns.append(jnp.concatenate(sources, axis=0))
    return columns


def scatter(columns, hot):
    sh, sl = split(jnp.concatenate(columns, axis=1))
    return mm_nt(jnp.concatenate([sh, sl], axis=1), jnp.concatenate([hot, hot], axis=1))


def step_derivatives(gacc, h):
    return gacc[h, 0], [gacc[h, 1 + c] for c in range(3)]


def filter_terms(rows, t, kept, found, gs, gv, rib, rob, dro, dri, basis_count, vectors):
    filters_ref, hidden_ref, basis_ref, slope_ref = kept
    wide = 2 if vectors else 1
    d_filters, d_dirs = [], []
    for q, g in enumerate(rows):
        s = part(found, 0, q)
        along = gv[0] * g[0:1] + gv[1] * g[1:2] + gv[2] * g[2:3]
        groups = [gs * s]
        if vectors:
            v = [part(found, 1 + c, q) for c in range(3)]
            groups.append(gv[0] * v[0] + gv[1] * v[1] + gv[2] * v[2])
        groups.append(s * along)
        d_filters.append(jnp.concatenate(groups, axis=0))
        push = part(filters_ref.at[t], wide, q) * s
        d_dirs.append([jnp.sum(push * gv[c], axis=0, keepdims=True) for c in range(3)])
    fh, fl = split(jnp.concatenate(d_filters, axis=1))
    both = hidden_ref[t]
    if vectors:
        dro[...] += mm_nt(jnp.concatenate([fh, fl], axis=1), jnp.concatenate([both, both], axis=1))
    else:
        pair = mm_nt(both, fh)
        dro[...] += pair[:LANES] + pair[LANES:] + mm_nt(both[:LANES], fl)
    spread = mm(rob[...], jnp.concatenate([fh, fl], axis=0))
    d_pre = (spread[:LANES] + spread[LANES:]) * slope_ref[t]
    ph, plo = split(d_pre)
    bb = basis_ref[t]
    dri[...] += mm_nt(jnp.concatenate([ph, plo], axis=1), jnp.concatenate([bb, bb], axis=1))
    back = mm(rib[...], jnp.concatenate([ph, plo], axis=0))
    d_basis = back[:basis_count] + back[basis_count:]
    basis = bb[:basis_count].astype(F32) + bb[basis_count:].astype(F32)
    offset = centre_offsets(rows, basis_count)
    d_dist = jnp.sum(d_basis * basis * offset, axis=0, keepdims=True) * (-2.0 * sharpness(basis_count))
    return d_dirs, [d_dist[:, q * LANES : (q + 1) * LANES] for q in range(len(rows))]


def radial_grads(dro, dri, out, row_in, row_out, basis_count, groups, turned):
    both = dri[...]
    turned_in = both + pltpu.roll(both, HALF, 1)
    out[row_in : row_in + basis_count] = turned_in.T[0:basis_count]
    for place in range(groups):
        block = slice(place * LANES, (place + 1) * LANES)
        grad = (dro[block, 0:LANES] + dro[block, LANES:]).T if turned else dro[:, block]
        out[row_out + place * LANES : row_out + (place + 1) * LANES] = grad


def species_hot(row, count):
    place = lax.broadcasted_iota(jnp.int32, (count, LANES), 0).astype(F32)
    return jnp.where(place == row, 1.0, 0.0).astype(BF16)


def first_features(emb_ref, hot):
    high, rest = split(emb_ref[...])
    low = (emb_ref[...] - high.astype(F32) - rest.astype(F32)).astype(BF16)
    dims = (((0,), (0,)), ((), ()))
    terms = [
        lax.dot_general(x.astype(F32).T.astype(BF16), hot, (((1,), (0,)), ((), ())), preferred_element_type=F32)
        for x in (high, rest, low)
    ]
    return terms[0] + (terms[1] + terms[2])


def from_sides(par_ref, a_ref, b_ref):
    even = is_even(par_ref, a_ref.shape)
    a, b = a_ref[...], b_ref[...]
    return jnp.where(even, a, b), jnp.where(even, b, a)


def species_tables(own_ref, up, down, emb_ref, halo):
    lane = lane_ids(1)
    count = emb_ref.shape[0]
    beside = jnp.where(lane >= LANES - halo, down[3:4], up[3:4])
    hot_own, hot_beside = species_hot(own_ref[3:4], count), species_hot(beside, count)
    return hot_own, hot_beside


def positions(cell_ref, fractions):
    rows = [
        fractions[0:1] * cell_ref[0, 0, c] + fractions[1:2] * cell_ref[0, 1, c] + fractions[2:3] * cell_ref[0, 2, c]
        for c in range(3)
    ]
    return jnp.concatenate(rows + [fractions[3:8]], axis=0)


def prepare_kernel(rin_ref, rout_ref, *outs):
    for layer, groups in enumerate(((0, 2), (0, 1, 2))):
        ri4, ro3, rib, rob = outs[4 * layer : 4 * layer + 4]
        rin, rout = rin_ref.at[pl.ds(layer, 1)], rout_ref.at[pl.ds(layer, 1)]
        prepare_weights(rin, rout, ri4, ro3, groups)
        prepare_back(rin, rout, rib, rob, groups)


def first_kernel(
    halo, par_ref, cell_ref, own_ref, a_ref, b_ref, nb_ref, count_ref, shift_ref, emb_ref, ri4, ro3,
    sm_ref, vm_ref, vg_ref,
    geom_ref, feat_ref, agg_ref, node_ref, send_a, send_b, filters_ref, hidden_ref, basis_ref, slope_ref, found_ref,
    tab, acc,
):
    slots = nb_ref.shape[0]
    basis_count = ri4.shape[1] // 4
    pairs = slots // 2
    up, down = from_sides(par_ref, a_ref, b_ref)
    lane = lane_ids(pairs)
    low = lane < HALF

    def halves(ref, *lead):
        even = ref[(*lead, pl.ds(0, pairs, stride=2), slice(None))]
        odd = ref[(*lead, pl.ds(1, pairs, stride=2), slice(None))]
        return jnp.where(low, even, pltpu.roll(odd, HALF, 1)), jnp.where(low, pltpu.roll(even, HALF, 1), odd)

    nb = halves(nb_ref)
    shift = [halves(shift_ref, a) for a in range(3)]
    row_slot = 2 * lax.broadcasted_iota(jnp.int32, (pairs, LANES), 0) + jnp.where(low, 0, 1)
    own, up, down = [positions(cell_ref, x) for x in (own_ref[...], up, down)]
    lane8 = lane_ids(own.shape[0])
    places = (jnp.where(lane8 < LANES - halo, own, down), jnp.where(lane8 >= halo, own, up))
    for h in range(2):
        index = (nb[h] - halo) & (LANES - 1)
        near = twice(own, h)
        count = twice(count_ref[...], h)
        mask = jnp.where(row_slot < count, 1.0, 0.0).astype(F32)
        steps = [shift[a][h].astype(F32) for a in range(3)]
        r = []
        for c in range(3):
            table = jnp.broadcast_to(places[h][c : c + 1], (pairs, LANES))
            far = jnp.take_along_axis(table, index, axis=1, mode="promise_in_bounds")
            image = steps[0] * cell_ref[0, 0, c] + steps[1] * cell_ref[0, 1, c] + steps[2] * cell_ref[0, 2, c]
            r.append(far - near[c : c + 1] + image)
        dist = jnp.sqrt(r[0] * r[0] + r[1] * r[1] + r[2] * r[2] + 1.0)
        values = [x / dist for x in r] + [dist, mask, index.astype(F32)]
        for n, x in enumerate(values):
            for m in range(pairs):
                geom_ref[h * pairs + m, n : n + 1, :] = x[m : m + 1]
    hot_own, hot_beside = species_tables(own_ref, up, down, emb_ref, halo)
    s, beside = first_features(emb_ref, hot_own), first_features(emb_ref, hot_beside)
    store_tables(tab, [s], [beside], halo)
    kept = (filters_ref, hidden_ref, basis_ref, slope_ref)
    forward_edges(
        geom_ref, tab, acc, found_ref, lambda rows, t: radial(rows, t, ri4, ro3, kept, basis_count), False
    )
    agg = aggregates(acc, slots**-0.5)
    w, size, u, gate = node_forward(agg, sm_ref[0], vm_ref[0], vg_ref[0])
    features = [s + u * sigmoid(u)] + [w[c] * gate for c in range(3)]
    for n, x in enumerate(w + [size, u, gate]):
        node_ref[n] = x
    for n in range(4):
        agg_ref[n] = agg[n]
        feat_ref[n] = features[n]
    tail, head = packed(features, halo, True), packed(features, halo, False)
    even = is_even(par_ref, tail.shape)
    send_a[...] = jnp.where(even, tail, head)
    send_b[...] = jnp.where(even, head, tail)


def radial_kernel(geom_ref, ri4, ro3, filters_ref, hidden_ref, basis_ref, slope_ref):
    radial_edges(geom_ref, ri4, ro3, (filters_ref, hidden_ref, basis_ref, slope_ref), ri4.shape[1] // 4)


def second_kernel(
    halo, par_ref, geom_ref, feat_ref, a_ref, b_ref, filters_ref, sm_ref, vm_ref, vg_ref, mid_ref, out_ref,
    cot_ref, send_a, send_b, grad_ref, mid_tail, gacc, found_ref,
    tab, acc, dtab,
):
    slots = geom_ref.shape[0]
    scale = slots**-0.5
    up, down = from_sides(par_ref, a_ref, b_ref)
    lane = lane_ids(LANES)
    features = [feat_ref[n] for n in range(4)]
    besides = [
        jnp.where(lane >= LANES - halo, unpacked(down, q, halo, True), unpacked(up, q, halo, False)) for q in range(4)
    ]
    store_tables(tab, features, besides, halo)
    forward_edges(geom_ref, tab, acc, found_ref, lambda rows, t: filters_ref.at[t], True)

    @pl.when(par_ref[0] >= 0)
    def _():
        agg = aggregates(acc, scale)
        sm, vm, vg = sm_ref[0], vm_ref[0], vg_ref[0]
        w, size, u, gate = node_forward(agg, sm, vm, vg)
        s = feat_ref[0] + u * sigmoid(u)
        mid = mid_ref[...]
        hidden = mm3(mid.T, s)
        act = sigmoid(hidden)
        shown = hidden * act
        weights = jnp.broadcast_to(out_ref[...], (8, LANES))
        per_atom = mm3(weights, shown)
        send_a[LANES:] = jnp.broadcast_to(jnp.sum(per_atom, axis=1, keepdims=True), (8, LANES))
        weight_column = jnp.broadcast_to(out_ref[...], (LANES, LANES)).T
        d_hidden = weight_column * (act * (1.0 + hidden * (1.0 - act)))
        ds = mm3(mid, d_hidden)
        zero = jnp.zeros((LANES, LANES), F32)
        dv = [zero, zero, zero]
        da, g_sm, g_vm, g_vg = node_backward(agg, w, size, u, gate, sm, vm, vg, ds, dv, scale)
        for n in range(4):
            for h in range(2):
                gacc[h, n] = twice(da[n], h)
        for n, x in enumerate([ds] + dv):
            cot_ref[n] = x
        row = 0
        for grad in (g_sm, g_vm, g_vg):
            grad_ref[row : row + LANES] = grad
            row += LANES
        grad_ref[row : row + 8] = mm3_nt(jnp.ones((8, LANES), F32), shown)
        g_mid = mm3_nt(s, d_hidden)
        grad_ref[row + 8 :] = g_mid[:MID_ROWS]
        mid_tail[...] = g_mid[MID_ROWS:]

    per_half = slots // 2 // ROWS
    dtab[...] = jnp.zeros(dtab.shape, F32)

    def step(t, carry):
        h = t // per_half
        rows = edge_rows(geom_ref, t)
        gs, gv = step_derivatives(gacc, h)
        columns = source_terms(rows, filters_ref.at[t], found_ref.at[t], gs, gv, True)
        dtab[h] += scatter(columns, one_hot_of(rows))
        return carry

    for t in range(2 * per_half):
        step(t, 0)
    firsts = [dtab[0, q * LANES : (q + 1) * LANES] for q in range(4)]
    seconds = [dtab[1, q * LANES : (q + 1) * LANES] for q in range(4)]
    for q in range(4):
        cot_ref[q] += (
            jnp.where(lane < LANES - halo, firsts[q], 0.0) + jnp.where(lane >= halo, seconds[q], 0.0)
        )
    to_prev, to_next = packed(firsts, halo, True), packed(seconds, halo, False)
    even = is_even(par_ref, to_prev.shape)
    send_a[:LANES] = jnp.where(even, to_next, to_prev)
    send_b[...] = jnp.where(even, to_prev, to_next)


def radial_back_kernel(
    t, geom_ref, filters_ref, hidden_ref, basis_ref, slope_ref, found_ref, gacc, rib, rob, *rest
):
    basis_count = rib.shape[0] // 2
    last = len(rest) > 3
    if last:
        dro_first, dri_first, mixed_ref, dgeom_ref, grad_ref, dro, dri = rest
        dro[...] = dro_first[...]
        dri[...] = dri_first[...]
    else:
        dgeom_ref, dro, dri = rest
        dro[...] = jnp.zeros(dro.shape, F32)
        dri[...] = jnp.zeros(dri.shape, F32)
    kept = (filters_ref, hidden_ref, basis_ref, slope_ref)
    rows = edge_rows(geom_ref, t)
    gs, gv = step_derivatives(gacc, t // (geom_ref.shape[0] // 2 // ROWS))
    d_dirs, d_dists = filter_terms(rows, t, kept, found_ref.at[t], gs, gv, rib, rob, dro, dri, basis_count, True)
    for q in range(ROWS):
        for c in range(3):
            dgeom_ref[q, c : c + 1, :] = d_dirs[q][c]
        dgeom_ref[q, 3:4, :] = d_dists[q]
    if last:
        radial_grads(dro, dri, grad_ref, 0, basis_count, basis_count, 3, True)
        grad_ref[basis_count + 3 * LANES :] = mixed_ref[...]


def third_kernel(
    halo, par_ref, geom_ref, dgeom_one, dgeom_two, agg_ref, node_ref, cot_ref, a_ref, b_ref, own_ref, pa_ref, pb_ref, mid_tail,
    filters_ref, hidden_ref, basis_ref, slope_ref, found_ref, emb_ref, rib, rob, sm_ref, vm_ref, vg_ref,
    force_ref, send_ref, grad_ref,
    gacc, dro, dri, dtab, pull, virial,
):
    basis_count = rib.shape[0] // 2
    slots = geom_ref.shape[0]
    scale = slots**-0.5
    lane = lane_ids(LANES)
    up, down = from_sides(par_ref, a_ref.at[:LANES], b_ref)
    cot = []
    for q in range(4):
        cot.append(
            cot_ref[q]
            + jnp.where(lane >= LANES - halo, unpacked(up, q, halo, True), 0.0)
            + jnp.where(lane < halo, unpacked(down, q, halo, False), 0.0)
        )
    place_up, place_down = from_sides(par_ref, pa_ref, pb_ref)
    hot_own, hot_beside = species_tables(own_ref, place_up, place_down, emb_ref, halo)
    count = emb_ref.shape[0]

    @pl.when(par_ref[0] >= 0)
    def _():
        agg = [agg_ref[n] for n in range(4)]
        sm, vm, vg = sm_ref[0], vm_ref[0], vg_ref[0]
        w, (size, u, gate) = [node_ref[c] for c in range(3)], [node_ref[n] for n in range(3, 6)]
        da, g_sm, g_vm, g_vg = node_backward(agg, w, size, u, gate, sm, vm, vg, cot[0], cot[1:], scale)
        for n in range(4):
            for h in range(2):
                gacc[h, n] = twice(da[n], h)
        row = count + basis_count + 2 * LANES
        for g in (g_sm, g_vm, g_vg):
            grad_ref[row : row + LANES] = g
            row += LANES

    pull[...] = jnp.zeros(pull.shape, F32)
    virial[...] = jnp.zeros(virial.shape, F32)

    def finish(row, g, d_dir, d_dist):
        more = (dgeom_one, dgeom_two)[row // ROWS][row % ROWS]
        dist = g[3:4]
        toward = [g[c : c + 1] for c in range(3)]
        turn = [d_dir[c] + more[c : c + 1] for c in range(3)]
        inner = turn[0] * toward[0] + turn[1] * toward[1] + turn[2] * toward[2]
        stretch = d_dist + more[3:4]
        inverse = 1.0 / dist
        dr = [(turn[c] - toward[c] * inner) * inverse + stretch * toward[c] for c in range(3)]
        r = [toward[c] * dist for c in range(3)]
        lines = jnp.concatenate(dr + [jnp.zeros((13, LANES), F32)], axis=0)
        products = [r[a] * dr[c] for a in range(3) for c in range(3)]
        return lines, jnp.concatenate(products + [jnp.zeros((7, LANES), F32)], axis=0)

    kept = (filters_ref, hidden_ref, basis_ref, slope_ref)
    per_half = slots // 2 // ROWS
    dro[...] = jnp.zeros(dro.shape, F32)
    dri[...] = jnp.zeros(dri.shape, F32)
    dtab[...] = jnp.zeros(dtab.shape, F32)

    def step(t, carry):
        h = t // per_half
        rows = edge_rows(geom_ref, t)
        gs, gv = step_derivatives(gacc, h)
        found = found_ref.at[t]
        d_dirs, d_dists = filter_terms(rows, t, kept, found, gs, gv, rib, rob, dro, dri, basis_count, False)
        columns = source_terms(rows, filters_ref.at[t], found, gs, gv, False)
        pairs = [finish(t * ROWS + q, g, d_dirs[q], d_dists[q]) for q, g in enumerate(rows)]
        pull[h] += sum(x for x, _ in pairs[1:]) + pairs[0][0]
        virial[...] += sum(x for _, x in pairs[1:]) + pairs[0][1]
        columns = [jnp.concatenate([x, y], axis=0) for x, (y, _) in zip(columns, pairs)]
        dtab[h] += scatter(columns, one_hot_of(rows))
        return carry

    for t in range(2 * per_half):
        step(t, 0)
    first, second = dtab[0, 0:LANES], dtab[1, 0:LANES]
    own_cot = cot[0] + jnp.where(lane < LANES - halo, first, 0.0) + jnp.where(lane >= halo, second, 0.0)
    side_cot = jnp.where(lane >= LANES - halo, first, 0.0) + jnp.where(lane < halo, second, 0.0)
    grad = 0.0
    for hot, value in ((hot_own, own_cot), (hot_beside, side_cot)):
        hi, lo = split(value)
        grad = grad + (mm_nt(hot, hi) + mm_nt(hot, lo))
    grad_ref[0:count] = grad
    row = count
    radial_grads(dro, dri, grad_ref, row, row + basis_count, basis_count, 2, False)
    row += basis_count + 5 * LANES
    grad_ref[row:] = jnp.zeros((grad_ref.shape[0] - row, LANES), F32)
    grad_ref[row + 8 : row + 8 + mid_tail.shape[0]] = mid_tail[...]
    sublane = lax.broadcasted_iota(jnp.int32, (16, LANES), 0)
    total = jnp.broadcast_to(jnp.sum(virial[...], axis=1, keepdims=True), virial.shape)
    nine = jnp.sum(jnp.where(lane_ids(16) == sublane, total, 0.0), axis=0, keepdims=True)
    mine = (sublane[:8] - par_ref[1]) == 0
    grad_ref[row : row + 8] = jnp.where(mine, nine, 0.0)
    lane16 = lane_ids(16)
    first, second = dtab[0, LANES:], dtab[1, LANES:]
    force_ref[...] = (
        jnp.where(lane16 < LANES - halo, first, 0.0)
        + jnp.where(lane16 >= halo, second, 0.0)
        - folded(pull[0], pull[1])
    )
    even = is_even(par_ref, first.shape)
    send_ref[0:8] = jnp.where(even, second, first)[0:8]
    send_ref[8:16] = jnp.where(even, first, second)[0:8]


def final_kernel(
    halo, par_ref, cell_ref, sum_energy, force_ref, a_ref, b_ref, mine_turned, other_turned,
    energy_ref, forces_ref, stress_ref, emb_ref, rin_ref, rout_ref, sm_ref, vm_ref, vg_ref, mid_ref, out_ref,
    mine, other,
):
    energy_ref[0, 0] = jnp.max(sum_energy[0:1])
    rows = mine.shape[0] // 4
    for c in range(4):
        turned = pl.ds(pl.multiple_of((par_ref[2] ^ c) * rows, 8), rows)
        mine[c * rows : (c + 1) * rows] = mine_turned[turned]
        other[c * rows : (c + 1) * rows] = other_turned[turned]
    lane = lane_ids(8)
    up, down = from_sides(par_ref, a_ref, b_ref.at[pl.ds(pl.multiple_of(8 * par_ref[3], 8), 8)])
    force = force_ref[0:8] + jnp.where(lane >= LANES - halo, up, 0.0) + jnp.where(lane < halo, down, 0.0)
    forces_ref[...] = -force[0:3]
    count, basis_count = emb_ref.shape[0], rin_ref.shape[1]
    m = [[cell_ref[0, a, c] for c in range(3)] for a in range(3)]
    det = (
        m[0][0] * (m[1][1] * m[2][2] - m[1][2] * m[2][1])
        - m[0][1] * (m[1][0] * m[2][2] - m[1][2] * m[2][0])
        + m[0][2] * (m[1][0] * m[2][1] - m[1][1] * m[2][0])
    )

    def write(one, two):
        emb_ref[...] = one[0:count]
        row = count
        rin_ref[0] = one[row : row + basis_count]
        rin_ref[1] = two[0:basis_count]
        row += basis_count
        rout_ref[0, :, 0:LANES] = one[row : row + LANES]
        rout_ref[0, :, LANES : 2 * LANES] = jnp.zeros((LANES, LANES), F32)
        rout_ref[0, :, 2 * LANES :] = one[row + LANES : row + 2 * LANES]
        row += 2 * LANES
        line = basis_count
        for g in range(3):
            rout_ref[1, :, g * LANES : (g + 1) * LANES] = two[line : line + LANES]
            line += LANES
        for ref in (sm_ref, vm_ref, vg_ref):
            ref[0] = one[row : row + LANES]
            ref[1] = two[line : line + LANES]
            row += LANES
            line += LANES
        out_ref[...] = two[line : line + 1]
        mid_ref[0:MID_ROWS] = two[line + 8 : line + 8 + MID_ROWS]
        mid_ref[MID_ROWS:] = one[row + 8 : row + 8 + LANES - MID_ROWS]
        wanted = (lax.broadcasted_iota(jnp.int32, (8, LANES), 0) - par_ref[1]) == 0
        nine = jnp.sum(jnp.where(wanted, one[row : row + 8], 0.0), axis=0, keepdims=True)
        stress = jnp.broadcast_to(nine, (8, LANES)) / (jnp.zeros((8, LANES), F32) + det)
        lines = [stress] + [pltpu.roll(stress, LANES - 3 * a, 1) for a in (1, 2)]
        for a in range(3):
            stress_ref[a] = lines[a][0:1, 0:3]

    @pl.when(par_ref[1] % 2 == 0)
    def _():
        write(other, mine)

    @pl.when(par_ref[1] % 2 == 1)
    def _():
        write(mine, other)


def side_one(x, axis):
    return lax.ppermute(x, axis, [(i, i ^ 1) for i in range(lax.axis_size(axis))])


def side_two(x, axis):
    size = lax.axis_size(axis)
    return lax.ppermute(x, axis, [(i, (i + 1) % size if i % 2 else (i - 1) % size) for i in range(size)])


def after(x, *others):
    return lax.optimization_barrier((x,) + others)[0]


def swap(x, axis, bit):
    return lax.ppermute(x, axis, [(i, i ^ bit) for i in range(lax.axis_size(axis))])


def layer_spec(x, layer):
    rest = x.shape[1:]
    return pl.BlockSpec((1,) + rest, lambda i: (layer,) + (0,) * len(rest))


def vmem():
    return pl.BlockSpec(memory_space=pltpu.VMEM)


def smem():
    return pl.BlockSpec(memory_space=pltpu.SMEM)


def whole(x):
    return pl.BlockSpec(x.shape, lambda i: (0,) * len(x.shape))


def f32(*shape):
    return jax.ShapeDtypeStruct(shape, F32)


def call(kernel, name, outs, in_specs, out_specs, scratch, flops, *args):
    return pl.pallas_call(
        kernel,
        grid=(1,),
        out_shape=outs,
        in_specs=in_specs,
        out_specs=out_specs,
        scratch_shapes=scratch,
        compiler_params=pltpu.CompilerParams(vmem_limit_bytes=VMEM_LIMIT),
        cost_estimate=pl.CostEstimate(flops=flops, bytes_accessed=flops // 500, transcendentals=0),
        name=name,
    )(*args)


def exchange(x, moves):
    groups, slabs = lax.axis_size("dp"), lax.axis_size("atom")
    route = []
    for g in range(groups):
        for p in range(slabs):
            to_g, to_p = moves(g, p)
            route.append((g * slabs + p, to_g * slabs + to_p))
    return lax.ppermute(x, ("dp", "atom"), route)


def local(
    frac, species, neighbours, counts, shifts, cell, energy_ref, embedding, radial_in, radial_out, scalar_mix,
    vector_mix, vector_gate, readout_mid, readout_out,
):
    atom_count = frac.shape[1]
    halo = atom_count // 4
    slots = neighbours.shape[0]
    basis_count = radial_in.shape[1]
    me = lax.axis_index("atom")
    group = lax.axis_index("dp")
    counts_row, out_row = counts[None], readout_out[None]
    own_row = lax.broadcasted_iota(jnp.int32, (8, 1), 0)
    own = jnp.pad(frac, ((0, 5), (0, 0))) + jnp.where(own_row == 3, species[None], 0).astype(F32)
    side_a, side_b = side_one(own, "atom"), side_two(own, "atom")
    plane = group // 2 * 2 + me % 2
    slabs = lax.axis_size("atom")
    levels = (slabs - 1).bit_length() - 1
    bits = [2 << n for n in range(levels)]
    opposite = jnp.where(me % 2 == 1, (me + 1) % slabs, (me + slabs - 1) % slabs)
    turned = (me ^ opposite ^ 1) >> 1
    turned = jnp.where(group % 2 == 1, (turned >> 1) | ((turned & 1) << (levels - 1)), turned)
    par = jnp.stack([me % 2, group, plane, turned]).astype(jnp.int32)
    layer = (radial_in, radial_out, scalar_mix, vector_mix, vector_gate)
    block = f32(LANES, LANES)
    edges, steps = ROWS * LANES, slots // ROWS

    def kept(groups):
        halves = tuple(jax.ShapeDtypeStruct((steps, n, edges), BF16) for n in (2 * LANES, 2 * basis_count))
        return (f32(steps, groups * LANES, edges),) + halves + (f32(steps, LANES, edges),)

    prepared = call(
        prepare_kernel,
        "prepare",
        tuple(
            jax.ShapeDtypeStruct(shape, BF16)
            for n in (2, 3)
            for shape in (
                (LANES, 4 * basis_count), (n * LANES, 3 * LANES), (2 * basis_count, 2 * LANES), (2 * LANES, 2 * n * LANES)
            )
        ),
        [vmem()] * 2,
        [vmem()] * 8,
        [],
        10**10,
        radial_in, radial_out,
    )
    geom, feat, agg, node, feat_a, feat_b, *kept_one = call(
        functools.partial(first_kernel, halo),
        "layer_one",
        (f32(slots, 8, LANES), f32(4, LANES, LANES), f32(4, LANES, LANES), f32(6, LANES, LANES), block, block) + kept(2)
        + (f32(steps, LANES, edges),),
        [smem(), smem()] + [vmem()] * 9 + [layer_spec(x, 0) for x in layer[2:]],
        [vmem()] * 11,
        [
            pltpu.VMEM((2, LANES, 2 * LANES), BF16),
            pltpu.VMEM((2, 4, LANES, LANES), F32),
        ],
        3 * 10**9,
        par, cell, own, side_a, side_b, neighbours, counts_row, shifts, embedding, *prepared[:2], *layer[2:],
    )
    feat_a, feat_b = side_one(feat_a, "atom"), side_two(feat_b, "atom")
    kept_two = call(
        radial_kernel,
        "radial_two",
        kept(3),
        [vmem()] * 3,
        [vmem()] * 4,
        [],
        3 * 10**9,
        geom, *prepared[4:6],
    )
    tail_rows = LANES - MID_ROWS
    mixed_rows = 3 * LANES + 8 + MID_ROWS
    cot, cot_a, cot_b, mixed, mid_tail, gacc, found_two = call(
        functools.partial(second_kernel, halo),
        "layer_two",
        (
            f32(4, LANES, LANES), f32(LANES + 8, LANES), block, f32(mixed_rows, LANES), f32(tail_rows, LANES),
            f32(2, 4, LANES, LANES), f32(steps, 4 * LANES, edges),
        ),
        [smem()] + [vmem()] * 5 + [layer_spec(x, 1) for x in layer[2:]] + [whole(readout_mid), whole(out_row)],
        [vmem()] * 7,
        [
            pltpu.VMEM((2, 4 * LANES, 2 * LANES), BF16),
            pltpu.VMEM((2, 4, LANES, LANES), F32),
            pltpu.VMEM((2, 4 * LANES, LANES), F32),
        ],
        5 * 10**9,
        par, geom, feat, feat_a, feat_b, kept_two[0], *layer[2:], readout_mid, out_row,
    )
    energy = cot_a[LANES:]
    cot_a = side_one(cot_a, "atom")
    back_args = (geom, *kept_two, found_two, gacc, *prepared[6:8])
    sums = (f32(3 * LANES, 2 * LANES), f32(LANES, 2 * basis_count))
    dgeom_one, dro_first, dri_first = call(
        functools.partial(radial_back_kernel, 0),
        "radial_two_back",
        (f32(ROWS, 8, LANES),) + sums,
        [vmem()] * 9,
        [vmem()] * 3,
        [],
        3 * 10**9,
        *back_args,
    )
    energy = energy + cot_a[LANES:]
    moved = swap(energy, "atom", 2)
    cot_b = side_two(after(cot_b, dri_first), "atom")
    dgeom_two, grads_two = call(
        functools.partial(radial_back_kernel, 1),
        "radial_two_back_last",
        (f32(ROWS, 8, LANES), f32(G_ROWS, LANES)),
        [vmem()] * 12,
        [vmem()] * 2,
        [pltpu.VMEM(x.shape, F32) for x in sums],
        3 * 10**9,
        *back_args, dro_first, after(dri_first, energy), mixed,
    )
    energy = after(energy + moved, dgeom_two)
    if slabs > 4:
        energy = energy + swap(energy, "atom", 4)
    force, force_sent, grads_one = call(
        functools.partial(third_kernel, halo),
        "layer_one_back",
        (f32(16, LANES), f32(16, LANES), f32(G_ROWS, LANES)),
        [smem()] + [vmem()] * 20 + [layer_spec(x, 0) for x in layer[2:]],
        [vmem()] * 3,
        [
            pltpu.VMEM((2, 4, LANES, LANES), F32),
            pltpu.VMEM((LANES, 2 * LANES), F32),
            pltpu.VMEM((LANES, 2 * basis_count), F32),
            pltpu.VMEM((2, LANES + 16, LANES), F32),
            pltpu.VMEM((2, 16, LANES), F32),
            pltpu.VMEM((16, LANES), F32),
        ],
        6 * 10**9,
        par, geom, dgeom_one, dgeom_two, agg, node, cot, cot_a, cot_b, own, side_a, side_b, mid_tail, *kept_one,
        embedding, *prepared[2:4], *layer[2:],
    )
    for bit in bits[2:]:
        energy = energy + swap(energy, "atom", bit)
    cell_atoms = atom_count * slabs
    loss_scale = 2.0 * (energy[0:1] / cell_atoms - energy_ref[0]) / cell_atoms
    virial_row = embedding.shape[0] + basis_count + 5 * LANES
    line = lax.broadcasted_iota(jnp.int32, (G_ROWS, 1), 0)
    one = grads_one * jnp.where((line >= virial_row) & (line < virial_row + 8), 1.0, loss_scale)
    two = grads_two * loss_scale
    core = group % 2 == 1
    x = jnp.where(core, one, two) + swap(jnp.where(core, two, one), "dp", 1)
    quarter = G_ROWS // 4

    def piece(k):
        return lax.dynamic_slice_in_dim(x, (plane ^ k) * quarter, quarter, 0)

    def plane_move(k):
        return lambda g, p: (g ^ (2 * (k >> 1)), p ^ (k & 1))

    joined = exchange(jnp.concatenate([piece(1), force_sent]), plane_move(1))
    second, third = exchange(piece(2), plane_move(2)), exchange(piece(3), plane_move(3))
    force_a, force_b = joined[quarter : quarter + 8], joined[quarter + 8 :]
    y = piece(0) + joined[:quarter] + second + third
    for n in range(levels):
        one_bit, two_bit = bits[n], bits[(n + 1) % levels]
        joined = exchange(jnp.concatenate([y, force_b]), lambda g, p: (g, p ^ (two_bit if g % 2 else one_bit)))
        y = y + joined[:quarter]
        force_b = jnp.concatenate([force_b, joined[quarter:]])
    x = jnp.concatenate([y] + [exchange(y, plane_move(k)) for k in (1, 2, 3)])
    other = swap(x, "dp", 1)
    weights = (embedding,) + layer + (readout_mid, out_row)
    outs = (f32(1, 1), f32(3, atom_count), f32(3, 1, 3)) + tuple(f32(*x.shape) for x in weights)
    result = call(
        functools.partial(final_kernel, halo),
        "final",
        outs,
        [smem(), smem()] + [vmem()] * 6,
        [smem()] + [whole(x) for x in outs[1:]],
        [pltpu.VMEM((G_ROWS, LANES), F32)] * 2,
        10**8,
        par, cell, energy, force, force_a, force_b, x, other,
    )
    return (result[0].reshape(1), result[1], result[2].transpose(1, 0, 2)) + tuple(result[3:-1]) + (result[-1].reshape(LANES),)


def solution(mesh):
    both = ("dp", "atom")
    return jax.shard_map(
        local,
        mesh=mesh,
        in_specs=(
            P(None, both), P(both), P(None, both), P(both), P(None, None, both), P("dp", None, None), P("dp"),
        ) + (P(),) * 8,
        out_specs=(P("dp"), P(None, both), P("dp", None, None)) + (P(),) * 8,
        check_vma=False,
    )
```

```python
import functools

import jax
import jax.numpy as jnp
from jax import lax
from jax.experimental import pallas as pl
from jax.experimental.pallas import tpu as pltpu
from jax.sharding import PartitionSpec as P

F32 = jnp.float32
BF16 = jnp.bfloat16
LANES = 128
HALF = 64
ROWS = 16
VMEM_LIMIT = 20 * 1024 * 1024
G_ROWS = 896
MID_ROWS = 56


def split(x):
    high = x.astype(BF16)
    return high, (x - high.astype(F32)).astype(BF16)


def mm(a, b):
    return lax.dot_general(a, b, (((1,), (0,)), ((), ())), preferred_element_type=F32)


def mm_nt(a, b):
    return lax.dot_general(a, b, (((1,), (1,)), ((), ())), preferred_element_type=F32)


def mm3(a, b):
    ah, al = split(a)
    bh, bl = split(b)
    return mm(ah, bh) + (mm(ah, bl) + mm(al, bh))


def mm3_nt(a, b):
    ah, al = split(a)
    bh, bl = split(b)
    return mm_nt(ah, bh) + (mm_nt(ah, bl) + mm_nt(al, bh))


def sigmoid(x):
    return 0.5 * jnp.tanh(0.5 * x) + 0.5


def lane_ids(rows):
    return lax.broadcasted_iota(jnp.int32, (rows, LANES), 1)


def twice(x, half):
    low = lane_ids(x.shape[0]) < HALF
    other = pltpu.roll(x, HALF, 1)
    return jnp.where(low, x, other) if half == 0 else jnp.where(low, other, x)


def folded(first, second):
    low = lane_ids(first.shape[0]) < HALF
    return jnp.where(low, first + pltpu.roll(first, HALF, 1), second + pltpu.roll(second, HALF, 1))


def windows(own, beside, halo):
    lane = lane_ids(own.shape[0])
    return jnp.where(lane < LANES - halo, own, beside), jnp.where(lane >= halo, own, beside)


def packed(parts, halo, tail):
    lane = lane_ids(parts[0].shape[0])
    out = None
    for q, x in enumerate(parts):
        turn = (halo * (q + 1) if tail else halo * q) % LANES
        x = pltpu.roll(x, turn, 1) if turn else x
        out = x if out is None else jnp.where(lane < halo * q, out, x)
    return out


def unpacked(pack, q, halo, tail):
    turn = (LANES - halo * (q + 1) if tail else LANES - halo * q) % LANES
    return pltpu.roll(pack, turn, 1) if turn else pack


def is_even(par_ref, shape):
    return (jnp.zeros(shape, jnp.int32) + par_ref[0]) == 0


def prepare_weights(rin_ref, rout_ref, ri4, ro3, groups):
    rh, rl = split(rin_ref[0])
    rows = jnp.concatenate([rh, rh, rl, rl], axis=0).astype(F32)
    ri4[...] = rows.T.astype(BF16)
    wh, wl = split(rout_ref[0])
    for place, g in enumerate(groups):
        cols = slice(g * LANES, (g + 1) * LANES)
        th = wh[:, cols].astype(F32).T.astype(BF16)
        tl = wl[:, cols].astype(F32).T.astype(BF16)
        out = slice(place * LANES, (place + 1) * LANES)
        ro3[out, 0:LANES] = th
        ro3[out, LANES : 2 * LANES] = th
        ro3[out, 2 * LANES : 3 * LANES] = tl


def prepare_back(rin_ref, rout_ref, rib, rob, groups):
    rh, rl = split(rin_ref[0])
    count = rh.shape[0]
    rib[0:count, 0:LANES] = rh
    rib[0:count, LANES:] = rh
    rib[count:, 0:LANES] = rl
    rib[count:, LANES:] = rl
    wh, wl = split(rout_ref[0])
    width = len(groups) * LANES
    for place, g in enumerate(groups):
        cols = slice(g * LANES, (g + 1) * LANES)
        for copy in range(2):
            out = slice(copy * width + place * LANES, copy * width + (place + 1) * LANES)
            rob[0:LANES, out] = wh[:, cols]
            rob[LANES:, out] = wl[:, cols]


def store_tables(tab, parts, besides, halo):
    for q, (own, beside) in enumerate(zip(parts, besides)):
        for h, table in enumerate(windows(own, beside, halo)):
            hi, lo = split(table)
            tab[h, q * LANES : (q + 1) * LANES, 0:LANES] = hi
            tab[h, q * LANES : (q + 1) * LANES, LANES:] = lo


def centre_offsets(rows, basis_count):
    place = lax.broadcasted_iota(jnp.int32, (basis_count, LANES), 0).astype(F32)
    centres = 8.0 * place / (basis_count - 1)
    return jnp.concatenate([g[3:4] - centres for g in rows], axis=1)


def sharpness(basis_count):
    return 0.5 * ((basis_count - 1) / 8.0) ** 2


def edge_rows(geom, t):
    return [geom[t * ROWS + q] for q in range(ROWS)]


def radial(rows, t, ri4, ro3, kept, basis_count):
    filters_ref, hidden_ref, basis_ref, slope_ref = kept
    offset = centre_offsets(rows, basis_count)
    bh, bl = split(jnp.exp(-sharpness(basis_count) * offset * offset))
    basis_ref[t] = jnp.concatenate([bh, bl], axis=0)
    pre = mm(ri4[...], jnp.concatenate([bh, bl, bh, bl], axis=0))
    gate = sigmoid(pre)
    mask = jnp.concatenate([g[4:5] for g in rows], axis=1)
    slope_ref[t] = mask * (gate * (1.0 + pre * (1.0 - gate)))
    hh, hl = split(pre * gate * mask)
    hidden_ref[t] = jnp.concatenate([hh, hl], axis=0)
    filters = mm(ro3[...], jnp.concatenate([hh, hl, hh], axis=0))
    filters_ref[t] = filters
    return filters


def one_hot_of(rows):
    place = lax.broadcasted_iota(jnp.int32, (LANES, LANES), 0).astype(F32)
    return jnp.concatenate(
        [jnp.where(place == g[5:6], 1.0, 0.0).astype(BF16) for g in rows], axis=1
    )


def part(x, group, q):
    return x[group * LANES : (group + 1) * LANES, q * LANES : (q + 1) * LANES]


def radial_edges(geom, ri4, ro3, kept, basis_count):
    def step(t, carry):
        radial(edge_rows(geom, t), t, ri4, ro3, kept, basis_count)
        return carry

    for t in range(geom.shape[0] // ROWS):
        step(t, 0)


def forward_edges(geom, tab, acc, found_ref, filters_of, vectors):
    per_half = geom.shape[0] // 2 // ROWS
    acc[...] = jnp.zeros(acc.shape, F32)
    wide = 2 if vectors else 1

    def step(t, carry):
        h = t // per_half
        rows = edge_rows(geom, t)
        filters = filters_of(rows, t)
        hot = one_hot_of(rows)
        found = mm(tab[h], jnp.concatenate([hot, hot], axis=0))
        found_ref[t] = found
        sums = [None] * 4
        for q, g in enumerate(rows):
            s = part(found, 0, q)
            terms = [part(filters, 0, q) * s]
            push = part(filters, wide, q) * s
            for c in range(3):
                term = push * g[c : c + 1]
                if vectors:
                    term = term + part(filters, 1, q) * part(found, 1 + c, q)
                terms.append(term)
            sums = [x if y is None else y + x for x, y in zip(terms, sums)]
        for n in range(4):
            acc[h, n] += sums[n]
        return carry

    for t in range(2 * per_half):
        step(t, 0)


def aggregates(acc, scale):
    return [folded(acc[0, n], acc[1, n]) * scale for n in range(4)]


def node_forward(agg, sm, vm, vg):
    mixed = mm3(vm.T, jnp.concatenate(agg[1:], axis=1))
    w = [mixed[:, c * LANES : (c + 1) * LANES] for c in range(3)]
    size = jnp.sqrt(w[0] * w[0] + w[1] * w[1] + w[2] * w[2] + 1.0)
    u = mm3(sm.T, agg[0]) + (size - 1.0)
    gate = sigmoid(mm3(vg.T, agg[0]))
    return w, size, u, gate


def node_backward(agg, w, size, u, gate, sm, vm, vg, ds, dv, scale):
    act = sigmoid(u)
    du = ds * (act * (1.0 + u * (1.0 - act)))
    ratio = du / size
    dw = [w[c] * ratio + dv[c] * gate for c in range(3)]
    dq = (dv[0] * w[0] + dv[1] * w[1] + dv[2] * w[2]) * gate * (1.0 - gate)
    dw_all = jnp.concatenate(dw, axis=1)
    da_s = (mm3(sm, du) + mm3(vg, dq)) * scale
    da_v = mm3(vm, dw_all) * scale
    da = [da_s] + [da_v[:, c * LANES : (c + 1) * LANES] for c in range(3)]
    g_sm = mm3_nt(agg[0], du)
    g_vg = mm3_nt(agg[0], dq)
    g_vm = mm3_nt(jnp.concatenate(agg[1:], axis=1), dw_all)
    return da, g_sm, g_vm, g_vg


def source_terms(rows, filters, found, gs, gv, vectors):
    wide = 2 if vectors else 1
    columns = []
    for q, g in enumerate(rows):
        along = gv[0] * g[0:1] + gv[1] * g[1:2] + gv[2] * g[2:3]
        sources = [part(filters, 0, q) * gs + part(filters, wide, q) * along]
        if vectors:
            f_v = part(filters, 1, q)
            sources += [f_v * gv[c] for c in range(3)]
        columns.append(jnp.concatenate(sources, axis=0))
    return columns


def scatter(columns, hot):
    sh, sl = split(jnp.concatenate(columns, axis=1))
    return mm_nt(jnp.concatenate([sh, sl], axis=1), jnp.concatenate([hot, hot], axis=1))


def step_derivatives(gacc, h):
    return gacc[h, 0], [gacc[h, 1 + c] for c in range(3)]


def filter_terms(rows, t, kept, found, gs, gv, rib, rob, dro, dri, basis_count, vectors):
    filters_ref, hidden_ref, basis_ref, slope_ref = kept
    wide = 2 if vectors else 1
    d_filters, d_dirs = [], []
    for q, g in enumerate(rows):
        s = part(found, 0, q)
        along = gv[0] * g[0:1] + gv[1] * g[1:2] + gv[2] * g[2:3]
        groups = [gs * s]
        if vectors:
            v = [part(found, 1 + c, q) for c in range(3)]
            groups.append(gv[0] * v[0] + gv[1] * v[1] + gv[2] * v[2])
        groups.append(s * along)
        d_filters.append(jnp.concatenate(groups, axis=0))
        push = part(filters_ref.at[t], wide, q) * s
        d_dirs.append([jnp.sum(push * gv[c], axis=0, keepdims=True) for c in range(3)])
    fh, fl = split(jnp.concatenate(d_filters, axis=1))
    both = hidden_ref[t]
    if vectors:
        dro[...] += mm_nt(jnp.concatenate([fh, fl], axis=1), jnp.concatenate([both, both], axis=1))
    else:
        pair = mm_nt(both, fh)
        dro[...] += pair[:LANES] + pair[LANES:] + mm_nt(both[:LANES], fl)
    spread = mm(rob[...], jnp.concatenate([fh, fl], axis=0))
    d_pre = (spread[:LANES] + spread[LANES:]) * slope_ref[t]
    ph, plo = split(d_pre)
    bb = basis_ref[t]
    dri[...] += mm_nt(jnp.concatenate([ph, plo], axis=1), jnp.concatenate([bb, bb], axis=1))
    back = mm(rib[...], jnp.concatenate([ph, plo], axis=0))
    d_basis = back[:basis_count] + back[basis_count:]
    basis = bb[:basis_count].astype(F32) + bb[basis_count:].astype(F32)
    offset = centre_offsets(rows, basis_count)
    d_dist = jnp.sum(d_basis * basis * offset, axis=0, keepdims=True) * (-2.0 * sharpness(basis_count))
    return d_dirs, [d_dist[:, q * LANES : (q + 1) * LANES] for q in range(len(rows))]


def radial_grads(dro, dri, out, row_in, row_out, basis_count, groups, turned):
    both = dri[...]
    turned_in = both + pltpu.roll(both, HALF, 1)
    out[row_in : row_in + basis_count] = turned_in.T[0:basis_count]
    for place in range(groups):
        block = slice(place * LANES, (place + 1) * LANES)
        grad = (dro[block, 0:LANES] + dro[block, LANES:]).T if turned else dro[:, block]
        out[row_out + place * LANES : row_out + (place + 1) * LANES] = grad


def species_hot(row, count):
    place = lax.broadcasted_iota(jnp.int32, (count, LANES), 0).astype(F32)
    return jnp.where(place == row, 1.0, 0.0).astype(BF16)


def first_features(emb_ref, hot):
    high, rest = split(emb_ref[...])
    low = (emb_ref[...] - high.astype(F32) - rest.astype(F32)).astype(BF16)
    dims = (((0,), (0,)), ((), ()))
    terms = [
        lax.dot_general(x.astype(F32).T.astype(BF16), hot, (((1,), (0,)), ((), ())), preferred_element_type=F32)
        for x in (high, rest, low)
    ]
    return terms[0] + (terms[1] + terms[2])


def from_sides(par_ref, a_ref, b_ref):
    even = is_even(par_ref, a_ref.shape)
    a, b = a_ref[...], b_ref[...]
    return jnp.where(even, a, b), jnp.where(even, b, a)


def species_tables(own_ref, up, down, emb_ref, halo):
    lane = lane_ids(1)
    count = emb_ref.shape[0]
    beside = jnp.where(lane >= LANES - halo, down[3:4], up[3:4])
    hot_own, hot_beside = species_hot(own_ref[3:4], count), species_hot(beside, count)
    return hot_own, hot_beside


def positions(cell_ref, fractions):
    rows = [
        fractions[0:1] * cell_ref[0, 0, c] + fractions[1:2] * cell_ref[1, 0, c] + fractions[2:3] * cell_ref[2, 0, c]
        for c in range(3)
    ]
    return jnp.concatenate(rows + [fractions[3:8]], axis=0)


def prepare_kernel(rin_ref, rout_ref, *outs):
    for layer, groups in enumerate(((0, 2), (0, 1, 2))):
        ri4, ro3, rib, rob = outs[4 * layer : 4 * layer + 4]
        rin, rout = rin_ref.at[pl.ds(layer, 1)], rout_ref.at[pl.ds(layer, 1)]
        prepare_weights(rin, rout, ri4, ro3, groups)
        prepare_back(rin, rout, rib, rob, groups)


def first_kernel(
    halo, par_ref, cell_ref, own_ref, a_ref, b_ref, nb_ref, count_ref, shift_ref, emb_ref, ri4, ro3,
    sm_ref, vm_ref, vg_ref,
    geom_ref, feat_ref, agg_ref, node_ref, send_a, send_b, filters_ref, hidden_ref, basis_ref, slope_ref, found_ref,
    tab, acc,
):
    slots = nb_ref.shape[0]
    basis_count = ri4.shape[1] // 4
    pairs = slots // 2
    up, down = from_sides(par_ref, a_ref, b_ref)
    lane = lane_ids(pairs)
    low = lane < HALF

    def halves(ref, *lead):
        even = ref[(*lead, pl.ds(0, pairs, stride=2), slice(None))]
        odd = ref[(*lead, pl.ds(1, pairs, stride=2), slice(None))]
        return jnp.where(low, even, pltpu.roll(odd, HALF, 1)), jnp.where(low, pltpu.roll(even, HALF, 1), odd)

    nb = halves(nb_ref)
    shift = [halves(shift_ref, a) for a in range(3)]
    row_slot = 2 * lax.broadcasted_iota(jnp.int32, (pairs, LANES), 0) + jnp.where(low, 0, 1)
    own, up, down = [positions(cell_ref, x) for x in (own_ref[...], up, down)]
    lane8 = lane_ids(own.shape[0])
    places = (jnp.where(lane8 < LANES - halo, own, down), jnp.where(lane8 >= halo, own, up))
    for h in range(2):
        index = (nb[h] - halo) & (LANES - 1)
        near = twice(own, h)
        count = twice(count_ref[...], h)
        mask = jnp.where(row_slot < count, 1.0, 0.0).astype(F32)
        steps = [shift[a][h].astype(F32) for a in range(3)]
        r = []
        for c in range(3):
            table = jnp.broadcast_to(places[h][c : c + 1], (pairs, LANES))
            far = jnp.take_along_axis(table, index, axis=1, mode="promise_in_bounds")
            image = steps[0] * cell_ref[0, 0, c] + steps[1] * cell_ref[1, 0, c] + steps[2] * cell_ref[2, 0, c]
            r.append(far - near[c : c + 1] + image)
        dist = jnp.sqrt(r[0] * r[0] + r[1] * r[1] + r[2] * r[2] + 1.0)
        values = [x / dist for x in r] + [dist, mask, index.astype(F32)]
        for n, x in enumerate(values):
            for m in range(pairs):
                geom_ref[h * pairs + m, n : n + 1, :] = x[m : m + 1]
    hot_own, hot_beside = species_tables(own_ref, up, down, emb_ref, halo)
    s, beside = first_features(emb_ref, hot_own), first_features(emb_ref, hot_beside)
    store_tables(tab, [s], [beside], halo)
    kept = (filters_ref, hidden_ref, basis_ref, slope_ref)
    forward_edges(
        geom_ref, tab, acc, found_ref, lambda rows, t: radial(rows, t, ri4, ro3, kept, basis_count), False
    )
    agg = aggregates(acc, slots**-0.5)
    w, size, u, gate = node_forward(agg, sm_ref[0], vm_ref[0], vg_ref[0])
    features = [s + u * sigmoid(u)] + [w[c] * gate for c in range(3)]
    for n, x in enumerate(w + [size, u, gate]):
        node_ref[n] = x
    for n in range(4):
        agg_ref[n] = agg[n]
        feat_ref[n] = features[n]
    tail, head = packed(features, halo, True), packed(features, halo, False)
    even = is_even(par_ref, tail.shape)
    send_a[...] = jnp.where(even, tail, head)
    send_b[...] = jnp.where(even, head, tail)


def radial_kernel(geom_ref, ri4, ro3, filters_ref, hidden_ref, basis_ref, slope_ref):
    radial_edges(geom_ref, ri4, ro3, (filters_ref, hidden_ref, basis_ref, slope_ref), ri4.shape[1] // 4)


def second_kernel(
    halo, par_ref, geom_ref, feat_ref, a_ref, b_ref, filters_ref, sm_ref, vm_ref, vg_ref, mid_ref, out_ref,
    cot_ref, send_a, send_b, grad_ref, mid_tail, gacc, found_ref,
    tab, acc, dtab,
):
    slots = geom_ref.shape[0]
    scale = slots**-0.5
    up, down = from_sides(par_ref, a_ref, b_ref)
    lane = lane_ids(LANES)
    features = [feat_ref[n] for n in range(4)]
    besides = [
        jnp.where(lane >= LANES - halo, unpacked(down, q, halo, True), unpacked(up, q, halo, False)) for q in range(4)
    ]
    store_tables(tab, features, besides, halo)
    forward_edges(geom_ref, tab, acc, found_ref, lambda rows, t: filters_ref.at[t], True)

    @pl.when(par_ref[0] >= 0)
    def _():
        agg = aggregates(acc, scale)
        sm, vm, vg = sm_ref[0], vm_ref[0], vg_ref[0]
        w, size, u, gate = node_forward(agg, sm, vm, vg)
        s = feat_ref[0] + u * sigmoid(u)
        mid = mid_ref[...]
        hidden = mm3(mid.T, s)
        act = sigmoid(hidden)
        shown = hidden * act
        weights = jnp.broadcast_to(out_ref[...], (8, LANES))
        per_atom = mm3(weights, shown)
        send_a[LANES:] = jnp.broadcast_to(jnp.sum(per_atom, axis=1, keepdims=True), (8, LANES))
        weight_column = jnp.broadcast_to(out_ref[...], (LANES, LANES)).T
        d_hidden = weight_column * (act * (1.0 + hidden * (1.0 - act)))
        ds = mm3(mid, d_hidden)
        zero = jnp.zeros((LANES, LANES), F32)
        dv = [zero, zero, zero]
        da, g_sm, g_vm, g_vg = node_backward(agg, w, size, u, gate, sm, vm, vg, ds, dv, scale)
        for n in range(4):
            for h in range(2):
                gacc[h, n] = twice(da[n], h)
        for n, x in enumerate([ds] + dv):
            cot_ref[n] = x
        row = 0
        for grad in (g_sm, g_vm, g_vg):
            grad_ref[row : row + LANES] = grad
            row += LANES
        grad_ref[row : row + 8] = mm3_nt(jnp.ones((8, LANES), F32), shown)
        g_mid = mm3_nt(s, d_hidden)
        grad_ref[row + 8 :] = g_mid[:MID_ROWS]
        mid_tail[...] = g_mid[MID_ROWS:]

    per_half = slots // 2 // ROWS
    dtab[...] = jnp.zeros(dtab.shape, F32)

    def step(t, carry):
        h = t // per_half
        rows = edge_rows(geom_ref, t)
        gs, gv = step_derivatives(gacc, h)
        columns = source_terms(rows, filters_ref.at[t], found_ref.at[t], gs, gv, True)
        dtab[h] += scatter(columns, one_hot_of(rows))
        return carry

    for t in range(2 * per_half):
        step(t, 0)
    firsts = [dtab[0, q * LANES : (q + 1) * LANES] for q in range(4)]
    seconds = [dtab[1, q * LANES : (q + 1) * LANES] for q in range(4)]
    for q in range(4):
        cot_ref[q] += (
            jnp.where(lane < LANES - halo, firsts[q], 0.0) + jnp.where(lane >= halo, seconds[q], 0.0)
        )
    to_prev, to_next = packed(firsts, halo, True), packed(seconds, halo, False)
    even = is_even(par_ref, to_prev.shape)
    send_a[:LANES] = jnp.where(even, to_next, to_prev)
    send_b[...] = jnp.where(even, to_prev, to_next)


def radial_back_kernel(
    t, geom_ref, filters_ref, hidden_ref, basis_ref, slope_ref, found_ref, gacc, rib, rob, *rest
):
    basis_count = rib.shape[0] // 2
    last = len(rest) > 3
    if last:
        dro_first, dri_first, mixed_ref, dgeom_ref, grad_ref, dro, dri = rest
        dro[...] = dro_first[...]
        dri[...] = dri_first[...]
    else:
        dgeom_ref, dro, dri = rest
        dro[...] = jnp.zeros(dro.shape, F32)
        dri[...] = jnp.zeros(dri.shape, F32)
    kept = (filters_ref, hidden_ref, basis_ref, slope_ref)
    rows = edge_rows(geom_ref, t)
    gs, gv = step_derivatives(gacc, t // (geom_ref.shape[0] // 2 // ROWS))
    d_dirs, d_dists = filter_terms(rows, t, kept, found_ref.at[t], gs, gv, rib, rob, dro, dri, basis_count, True)
    for q in range(ROWS):
        for c in range(3):
            dgeom_ref[q, c : c + 1, :] = d_dirs[q][c]
        dgeom_ref[q, 3:4, :] = d_dists[q]
    if last:
        radial_grads(dro, dri, grad_ref, 0, basis_count, basis_count, 3, True)
        grad_ref[basis_count + 3 * LANES :] = mixed_ref[...]


def third_kernel(
    halo, par_ref, geom_ref, dgeom_one, dgeom_two, agg_ref, node_ref, cot_ref, a_ref, b_ref, own_ref, pa_ref, pb_ref, mid_tail,
    filters_ref, hidden_ref, basis_ref, slope_ref, found_ref, emb_ref, rib, rob, sm_ref, vm_ref, vg_ref,
    force_ref, send_ref, grad_ref,
    gacc, dro, dri, dtab, pull, virial,
):
    basis_count = rib.shape[0] // 2
    slots = geom_ref.shape[0]
    scale = slots**-0.5
    lane = lane_ids(LANES)
    up, down = from_sides(par_ref, a_ref.at[:LANES], b_ref)
    cot = []
    for q in range(4):
        cot.append(
            cot_ref[q]
            + jnp.where(lane >= LANES - halo, unpacked(up, q, halo, True), 0.0)
            + jnp.where(lane < halo, unpacked(down, q, halo, False), 0.0)
        )
    place_up, place_down = from_sides(par_ref, pa_ref, pb_ref)
    hot_own, hot_beside = species_tables(own_ref, place_up, place_down, emb_ref, halo)
    count = emb_ref.shape[0]

    @pl.when(par_ref[0] >= 0)
    def _():
        agg = [agg_ref[n] for n in range(4)]
        sm, vm, vg = sm_ref[0], vm_ref[0], vg_ref[0]
        w, (size, u, gate) = [node_ref[c] for c in range(3)], [node_ref[n] for n in range(3, 6)]
        da, g_sm, g_vm, g_vg = node_backward(agg, w, size, u, gate, sm, vm, vg, cot[0], cot[1:], scale)
        for n in range(4):
            for h in range(2):
                gacc[h, n] = twice(da[n], h)
        row = count + basis_count + 2 * LANES
        for g in (g_sm, g_vm, g_vg):
            grad_ref[row : row + LANES] = g
            row += LANES

    pull[...] = jnp.zeros(pull.shape, F32)
    virial[...] = jnp.zeros(virial.shape, F32)

    def finish(row, g, d_dir, d_dist):
        more = (dgeom_one, dgeom_two)[row // ROWS][row % ROWS]
        dist = g[3:4]
        toward = [g[c : c + 1] for c in range(3)]
        turn = [d_dir[c] + more[c : c + 1] for c in range(3)]
        inner = turn[0] * toward[0] + turn[1] * toward[1] + turn[2] * toward[2]
        stretch = d_dist + more[3:4]
        inverse = 1.0 / dist
        dr = [(turn[c] - toward[c] * inner) * inverse + stretch * toward[c] for c in range(3)]
        r = [toward[c] * dist for c in range(3)]
        lines = jnp.concatenate(dr + [jnp.zeros((13, LANES), F32)], axis=0)
        products = [r[a] * dr[c] for a in range(3) for c in range(3)]
        return lines, jnp.concatenate(products + [jnp.zeros((7, LANES), F32)], axis=0)

    kept = (filters_ref, hidden_ref, basis_ref, slope_ref)
    per_half = slots // 2 // ROWS
    dro[...] = jnp.zeros(dro.shape, F32)
    dri[...] = jnp.zeros(dri.shape, F32)
    dtab[...] = jnp.zeros(dtab.shape, F32)

    def step(t, carry):
        h = t // per_half
        rows = edge_rows(geom_ref, t)
        gs, gv = step_derivatives(gacc, h)
        found = found_ref.at[t]
        d_dirs, d_dists = filter_terms(rows, t, kept, found, gs, gv, rib, rob, dro, dri, basis_count, False)
        columns = source_terms(rows, filters_ref.at[t], found, gs, gv, False)
        pairs = [finish(t * ROWS + q, g, d_dirs[q], d_dists[q]) for q, g in enumerate(rows)]
        pull[h] += sum(x for x, _ in pairs[1:]) + pairs[0][0]
        virial[...] += sum(x for _, x in pairs[1:]) + pairs[0][1]
        columns = [jnp.concatenate([x, y], axis=0) for x, (y, _) in zip(columns, pairs)]
        dtab[h] += scatter(columns, one_hot_of(rows))
        return carry

    for t in range(2 * per_half):
        step(t, 0)
    first, second = dtab[0, 0:LANES], dtab[1, 0:LANES]
    own_cot = cot[0] + jnp.where(lane < LANES - halo, first, 0.0) + jnp.where(lane >= halo, second, 0.0)
    side_cot = jnp.where(lane >= LANES - halo, first, 0.0) + jnp.where(lane < halo, second, 0.0)
    grad = 0.0
    for hot, value in ((hot_own, own_cot), (hot_beside, side_cot)):
        hi, lo = split(value)
        grad = grad + (mm_nt(hot, hi) + mm_nt(hot, lo))
    grad_ref[0:count] = grad
    row = count
    radial_grads(dro, dri, grad_ref, row, row + basis_count, basis_count, 2, False)
    row += basis_count + 5 * LANES
    grad_ref[row:] = jnp.zeros((grad_ref.shape[0] - row, LANES), F32)
    grad_ref[row + 8 : row + 8 + mid_tail.shape[0]] = mid_tail[...]
    sublane = lax.broadcasted_iota(jnp.int32, (16, LANES), 0)
    total = jnp.broadcast_to(jnp.sum(virial[...], axis=1, keepdims=True), virial.shape)
    nine = jnp.sum(jnp.where(lane_ids(16) == sublane, total, 0.0), axis=0, keepdims=True)
    mine = (sublane[:8] - par_ref[1]) == 0
    grad_ref[row : row + 8] = jnp.where(mine, nine, 0.0)
    lane16 = lane_ids(16)
    first, second = dtab[0, LANES:], dtab[1, LANES:]
    force_ref[...] = (
        jnp.where(lane16 < LANES - halo, first, 0.0)
        + jnp.where(lane16 >= halo, second, 0.0)
        - folded(pull[0], pull[1])
    )
    even = is_even(par_ref, first.shape)
    send_ref[0:8] = jnp.where(even, second, first)[0:8]
    send_ref[8:16] = jnp.where(even, first, second)[0:8]


def final_kernel(
    halo, par_ref, cell_ref, sum_energy, force_ref, a_ref, b_ref, mine_turned, other_turned,
    energy_ref, forces_ref, stress_ref, emb_ref, rin_ref, rout_ref, sm_ref, vm_ref, vg_ref, mid_ref, out_ref,
    mine, other,
):
    energy_ref[0, 0] = jnp.max(sum_energy[0:1])
    rows = mine.shape[0] // 4
    for c in range(4):
        turned = pl.ds(pl.multiple_of((par_ref[2] ^ c) * rows, 8), rows)
        mine[c * rows : (c + 1) * rows] = mine_turned[turned]
        other[c * rows : (c + 1) * rows] = other_turned[turned]
    lane = lane_ids(8)
    up, down = from_sides(par_ref, a_ref, b_ref.at[pl.ds(pl.multiple_of(8 * par_ref[3], 8), 8)])
    force = force_ref[0:8] + jnp.where(lane >= LANES - halo, up, 0.0) + jnp.where(lane < halo, down, 0.0)
    forces_ref[...] = -force[0:3]
    count, basis_count = emb_ref.shape[0], rin_ref.shape[1]
    m = [[cell_ref[a, 0, c] for c in range(3)] for a in range(3)]
    det = (
        m[0][0] * (m[1][1] * m[2][2] - m[1][2] * m[2][1])
        - m[0][1] * (m[1][0] * m[2][2] - m[1][2] * m[2][0])
        + m[0][2] * (m[1][0] * m[2][1] - m[1][1] * m[2][0])
    )

    def write(one, two):
        emb_ref[...] = one[0:count]
        row = count
        rin_ref[0] = one[row : row + basis_count]
        rin_ref[1] = two[0:basis_count]
        row += basis_count
        rout_ref[0, :, 0:LANES] = one[row : row + LANES]
        rout_ref[0, :, LANES : 2 * LANES] = jnp.zeros((LANES, LANES), F32)
        rout_ref[0, :, 2 * LANES :] = one[row + LANES : row + 2 * LANES]
        row += 2 * LANES
        line = basis_count
        for g in range(3):
            rout_ref[1, :, g * LANES : (g + 1) * LANES] = two[line : line + LANES]
            line += LANES
        for ref in (sm_ref, vm_ref, vg_ref):
            ref[0] = one[row : row + LANES]
            ref[1] = two[line : line + LANES]
            row += LANES
            line += LANES
        out_ref[...] = two[line : line + 1]
        mid_ref[0:MID_ROWS] = two[line + 8 : line + 8 + MID_ROWS]
        mid_ref[MID_ROWS:] = one[row + 8 : row + 8 + LANES - MID_ROWS]
        wanted = (lax.broadcasted_iota(jnp.int32, (8, LANES), 0) - par_ref[1]) == 0
        nine = jnp.sum(jnp.where(wanted, one[row : row + 8], 0.0), axis=0, keepdims=True)
        stress = jnp.broadcast_to(nine, (8, LANES)) / (jnp.zeros((8, LANES), F32) + det)
        lines = [stress] + [pltpu.roll(stress, LANES - 3 * a, 1) for a in (1, 2)]
        for a in range(3):
            stress_ref[a] = lines[a][0:1, 0:3]

    @pl.when(par_ref[1] % 2 == 0)
    def _():
        write(other, mine)

    @pl.when(par_ref[1] % 2 == 1)
    def _():
        write(mine, other)


def side_one(x, axis):
    return lax.ppermute(x, axis, [(i, i ^ 1) for i in range(lax.axis_size(axis))])


def side_two(x, axis):
    size = lax.axis_size(axis)
    return lax.ppermute(x, axis, [(i, (i + 1) % size if i % 2 else (i - 1) % size) for i in range(size)])


def after(x, *others):
    return lax.optimization_barrier((x,) + others)[0]


def swap(x, axis, bit):
    return lax.ppermute(x, axis, [(i, i ^ bit) for i in range(lax.axis_size(axis))])


def layer_spec(x, layer):
    rest = x.shape[1:]
    return pl.BlockSpec((1,) + rest, lambda i: (layer,) + (0,) * len(rest))


def vmem():
    return pl.BlockSpec(memory_space=pltpu.VMEM)


def smem():
    return pl.BlockSpec(memory_space=pltpu.SMEM)


def whole(x):
    return pl.BlockSpec(x.shape, lambda i: (0,) * len(x.shape))


def f32(*shape):
    return jax.ShapeDtypeStruct(shape, F32)


def call(kernel, name, outs, in_specs, out_specs, scratch, flops, *args):
    return pl.pallas_call(
        kernel,
        grid=(1,),
        out_shape=outs,
        in_specs=in_specs,
        out_specs=out_specs,
        scratch_shapes=scratch,
        compiler_params=pltpu.CompilerParams(vmem_limit_bytes=VMEM_LIMIT),
        cost_estimate=pl.CostEstimate(flops=flops, bytes_accessed=flops // 500, transcendentals=0),
        name=name,
    )(*args)


def exchange(x, moves):
    groups, slabs = lax.axis_size("dp"), lax.axis_size("atom")
    route = []
    for g in range(groups):
        for p in range(slabs):
            to_g, to_p = moves(g, p)
            route.append((g * slabs + p, to_g * slabs + to_p))
    return lax.ppermute(x, ("dp", "atom"), route)


def local(
    frac, species, neighbours, counts, shifts, cell, energy_ref, embedding, radial_in, radial_out, scalar_mix,
    vector_mix, vector_gate, readout_mid, readout_out,
):
    atom_count = frac.shape[1]
    halo = atom_count // 4
    slots = neighbours.shape[0]
    basis_count = radial_in.shape[1]
    me = lax.axis_index("atom")
    group = lax.axis_index("dp")
    counts_row, out_row = counts[None], readout_out[None]
    lattice = cell.transpose(1, 0, 2)
    own_row = lax.broadcasted_iota(jnp.int32, (8, 1), 0)
    own = jnp.pad(frac, ((0, 5), (0, 0))) + jnp.where(own_row == 3, species[None], 0).astype(F32)
    side_a, side_b = side_one(own, "atom"), side_two(own, "atom")
    plane = group // 2 * 2 + me % 2
    slabs = lax.axis_size("atom")
    levels = (slabs - 1).bit_length() - 1
    bits = [2 << n for n in range(levels)]
    opposite = jnp.where(me % 2 == 1, (me + 1) % slabs, (me + slabs - 1) % slabs)
    turned = (me ^ opposite ^ 1) >> 1
    turned = jnp.where(group % 2 == 1, (turned >> 1) | ((turned & 1) << (levels - 1)), turned)
    par = jnp.stack([me % 2, group, plane, turned]).astype(jnp.int32)
    layer = (radial_in, radial_out, scalar_mix, vector_mix, vector_gate)
    block = f32(LANES, LANES)
    edges, steps = ROWS * LANES, slots // ROWS

    def kept(groups):
        halves = tuple(jax.ShapeDtypeStruct((steps, n, edges), BF16) for n in (2 * LANES, 2 * basis_count))
        return (f32(steps, groups * LANES, edges),) + halves + (f32(steps, LANES, edges),)

    prepared = call(
        prepare_kernel,
        "prepare",
        tuple(
            jax.ShapeDtypeStruct(shape, BF16)
            for n in (2, 3)
            for shape in (
                (LANES, 4 * basis_count), (n * LANES, 3 * LANES), (2 * basis_count, 2 * LANES), (2 * LANES, 2 * n * LANES)
            )
        ),
        [vmem()] * 2,
        [vmem()] * 8,
        [],
        10**10,
        radial_in, radial_out,
    )
    geom, feat, agg, node, feat_a, feat_b, *kept_one = call(
        functools.partial(first_kernel, halo),
        "layer_one",
        (f32(slots, 8, LANES), f32(4, LANES, LANES), f32(4, LANES, LANES), f32(6, LANES, LANES), block, block) + kept(2)
        + (f32(steps, LANES, edges),),
        [smem(), smem()] + [vmem()] * 9 + [layer_spec(x, 0) for x in layer[2:]],
        [vmem()] * 11,
        [
            pltpu.VMEM((2, LANES, 2 * LANES), BF16),
            pltpu.VMEM((2, 4, LANES, LANES), F32),
        ],
        3 * 10**9,
        par, lattice, own, side_a, side_b, neighbours, counts_row, shifts, embedding, *prepared[:2], *layer[2:],
    )
    feat_a, feat_b = side_one(feat_a, "atom"), side_two(feat_b, "atom")
    kept_two = call(
        radial_kernel,
        "radial_two",
        kept(3),
        [vmem()] * 3,
        [vmem()] * 4,
        [],
        3 * 10**9,
        geom, *prepared[4:6],
    )
    tail_rows = LANES - MID_ROWS
    mixed_rows = 3 * LANES + 8 + MID_ROWS
    cot, cot_a, cot_b, mixed, mid_tail, gacc, found_two = call(
        functools.partial(second_kernel, halo),
        "layer_two",
        (
            f32(4, LANES, LANES), f32(LANES + 8, LANES), block, f32(mixed_rows, LANES), f32(tail_rows, LANES),
            f32(2, 4, LANES, LANES), f32(steps, 4 * LANES, edges),
        ),
        [smem()] + [vmem()] * 5 + [layer_spec(x, 1) for x in layer[2:]] + [whole(readout_mid), whole(out_row)],
        [vmem()] * 7,
        [
            pltpu.VMEM((2, 4 * LANES, 2 * LANES), BF16),
            pltpu.VMEM((2, 4, LANES, LANES), F32),
            pltpu.VMEM((2, 4 * LANES, LANES), F32),
        ],
        5 * 10**9,
        par, geom, feat, feat_a, feat_b, kept_two[0], *layer[2:], readout_mid, out_row,
    )
    energy = cot_a[LANES:]
    cot_a = side_one(cot_a, "atom")
    back_args = (geom, *kept_two, found_two, gacc, *prepared[6:8])
    sums = (f32(3 * LANES, 2 * LANES), f32(LANES, 2 * basis_count))
    dgeom_one, dro_first, dri_first = call(
        functools.partial(radial_back_kernel, 0),
        "radial_two_back",
        (f32(ROWS, 8, LANES),) + sums,
        [vmem()] * 9,
        [vmem()] * 3,
        [],
        3 * 10**9,
        *back_args,
    )
    energy = energy + cot_a[LANES:]
    moved = swap(energy, "atom", 2)
    cot_b = side_two(after(cot_b, dri_first), "atom")
    dgeom_two, grads_two = call(
        functools.partial(radial_back_kernel, 1),
        "radial_two_back_last",
        (f32(ROWS, 8, LANES), f32(G_ROWS, LANES)),
        [vmem()] * 12,
        [vmem()] * 2,
        [pltpu.VMEM(x.shape, F32) for x in sums],
        3 * 10**9,
        *back_args, dro_first, after(dri_first, energy), mixed,
    )
    energy = after(energy + moved, dgeom_two)
    if slabs > 4:
        energy = energy + swap(energy, "atom", 4)
    force, force_sent, grads_one = call(
        functools.partial(third_kernel, halo),
        "layer_one_back",
        (f32(16, LANES), f32(16, LANES), f32(G_ROWS, LANES)),
        [smem()] + [vmem()] * 20 + [layer_spec(x, 0) for x in layer[2:]],
        [vmem()] * 3,
        [
            pltpu.VMEM((2, 4, LANES, LANES), F32),
            pltpu.VMEM((LANES, 2 * LANES), F32),
            pltpu.VMEM((LANES, 2 * basis_count), F32),
            pltpu.VMEM((2, LANES + 16, LANES), F32),
            pltpu.VMEM((2, 16, LANES), F32),
            pltpu.VMEM((16, LANES), F32),
        ],
        6 * 10**9,
        par, geom, dgeom_one, dgeom_two, agg, node, cot, cot_a, cot_b, own, side_a, side_b, mid_tail, *kept_one,
        embedding, *prepared[2:4], *layer[2:],
    )
    for bit in bits[2:]:
        energy = energy + swap(energy, "atom", bit)
    cell_atoms = atom_count * slabs
    loss_scale = 2.0 * (energy[0:1] / cell_atoms - energy_ref[0]) / cell_atoms
    virial_row = embedding.shape[0] + basis_count + 5 * LANES
    line = lax.broadcasted_iota(jnp.int32, (G_ROWS, 1), 0)
    one = grads_one * jnp.where((line >= virial_row) & (line < virial_row + 8), 1.0, loss_scale)
    two = grads_two * loss_scale
    core = group % 2 == 1
    x = jnp.where(core, one, two) + swap(jnp.where(core, two, one), "dp", 1)
    quarter = G_ROWS // 4

    def piece(k):
        return lax.dynamic_slice_in_dim(x, (plane ^ k) * quarter, quarter, 0)

    def plane_move(k):
        return lambda g, p: (g ^ (2 * (k >> 1)), p ^ (k & 1))

    link_a, link_b = jnp.where(core, 2, 1), jnp.where(core, 1, 2)

    def move_a(g, p):
        return plane_move(2 if g % 2 else 1)(g, p)

    def move_b(g, p):
        return plane_move(1 if g % 2 else 2)(g, p)

    got_a = exchange(jnp.concatenate([piece(link_a), force_sent]), move_a)
    got_b = exchange(jnp.concatenate([piece(link_b), force_sent]), move_b)
    got_c = exchange(piece(3), plane_move(3))
    joined = jnp.where(core, got_b, got_a)[quarter:]
    force_a, force_b = joined[:8], joined[8:]
    y = piece(0) + got_a[:quarter] + got_b[:quarter] + got_c
    for n in range(levels):
        one_bit, two_bit = bits[n], bits[(n + 1) % levels]
        joined = exchange(jnp.concatenate([y, force_b]), lambda g, p: (g, p ^ (two_bit if g % 2 else one_bit)))
        y = y + joined[:quarter]
        force_b = jnp.concatenate([force_b, joined[quarter:]])
    all_a, all_b = exchange(y, move_a), exchange(y, move_b)
    all_c = exchange(y, plane_move(3))
    x = jnp.concatenate([y, jnp.where(core, all_b, all_a), jnp.where(core, all_a, all_b), all_c])
    other = swap(x, "dp", 1)
    weights = (embedding,) + layer + (readout_mid, out_row)
    outs = (f32(1, 1), f32(3, atom_count), f32(3, 1, 3)) + tuple(f32(*x.shape) for x in weights)
    result = call(
        functools.partial(final_kernel, halo),
        "final",
        outs,
        [smem(), smem()] + [vmem()] * 6,
        [smem()] + [whole(x) for x in outs[1:]],
        [pltpu.VMEM((G_ROWS, LANES), F32)] * 2,
        10**8,
        par, lattice, energy, force, force_a, force_b, x, other,
    )
    return (result[0].reshape(1), result[1], result[2].transpose(1, 0, 2)) + tuple(result[3:-1]) + (result[-1].reshape(LANES),)


def solution(mesh):
    both = ("dp", "atom")
    return jax.shard_map(
        local,
        mesh=mesh,
        in_specs=(
            P(None, both), P(both), P(None, both), P(both), P(None, None, both), P("dp", None, None), P("dp"),
        ) + (P(),) * 8,
        out_specs=(P("dp"), P(None, both), P("dp", None, None)) + (P(),) * 8,
        check_vma=False,
    )
```

```python
import functools

import jax
import jax.numpy as jnp
from jax import lax
from jax.experimental import pallas as pl
from jax.experimental.pallas import tpu as pltpu
from jax.sharding import PartitionSpec as P

F32 = jnp.float32
BF16 = jnp.bfloat16
LANES = 128
HALF = 64
ROWS = 16
VMEM_LIMIT = 20 * 1024 * 1024
G_ROWS = 896
MID_ROWS = 56


def split(x):
    high = x.astype(BF16)
    return high, (x - high.astype(F32)).astype(BF16)


def mm(a, b):
    return lax.dot_general(a, b, (((1,), (0,)), ((), ())), preferred_element_type=F32)


def mm_nt(a, b):
    return lax.dot_general(a, b, (((1,), (1,)), ((), ())), preferred_element_type=F32)


def mm3(a, b):
    ah, al = split(a)
    bh, bl = split(b)
    return mm(ah, bh) + (mm(ah, bl) + mm(al, bh))


def mm3_nt(a, b):
    ah, al = split(a)
    bh, bl = split(b)
    return mm_nt(ah, bh) + (mm_nt(ah, bl) + mm_nt(al, bh))


def sigmoid(x):
    return 0.5 * jnp.tanh(0.5 * x) + 0.5


def lane_ids(rows):
    return lax.broadcasted_iota(jnp.int32, (rows, LANES), 1)


def twice(x, half):
    low = lane_ids(x.shape[0]) < HALF
    other = pltpu.roll(x, HALF, 1)
    return jnp.where(low, x, other) if half == 0 else jnp.where(low, other, x)


def folded(first, second):
    low = lane_ids(first.shape[0]) < HALF
    return jnp.where(low, first + pltpu.roll(first, HALF, 1), second + pltpu.roll(second, HALF, 1))


def windows(own, beside, halo):
    lane = lane_ids(own.shape[0])
    return jnp.where(lane < LANES - halo, own, beside), jnp.where(lane >= halo, own, beside)


def packed(parts, halo, tail):
    lane = lane_ids(parts[0].shape[0])
    out = None
    for q, x in enumerate(parts):
        turn = (halo * (q + 1) if tail else halo * q) % LANES
        x = pltpu.roll(x, turn, 1) if turn else x
        out = x if out is None else jnp.where(lane < halo * q, out, x)
    return out


def unpacked(pack, q, halo, tail):
    turn = (LANES - halo * (q + 1) if tail else LANES - halo * q) % LANES
    return pltpu.roll(pack, turn, 1) if turn else pack


def is_even(par_ref, shape):
    return (jnp.zeros(shape, jnp.int32) + par_ref[0]) == 0


def prepare_weights(rin_ref, rout_ref, ri4, ro3, groups):
    rh, rl = split(rin_ref[0])
    rows = jnp.concatenate([rh, rh, rl, rl], axis=0).astype(F32)
    ri4[...] = rows.T.astype(BF16)
    wh, wl = split(rout_ref[0])
    for place, g in enumerate(groups):
        cols = slice(g * LANES, (g + 1) * LANES)
        th = wh[:, cols].astype(F32).T.astype(BF16)
        tl = wl[:, cols].astype(F32).T.astype(BF16)
        out = slice(place * LANES, (place + 1) * LANES)
        ro3[out, 0:LANES] = th
        ro3[out, LANES : 2 * LANES] = th
        ro3[out, 2 * LANES : 3 * LANES] = tl


def prepare_back(rin_ref, rout_ref, rib, rob, groups):
    rh, rl = split(rin_ref[0])
    count = rh.shape[0]
    rib[0:count, 0:LANES] = rh
    rib[0:count, LANES:] = rh
    rib[count:, 0:LANES] = rl
    rib[count:, LANES:] = rl
    wh, wl = split(rout_ref[0])
    width = len(groups) * LANES
    for place, g in enumerate(groups):
        cols = slice(g * LANES, (g + 1) * LANES)
        for copy in range(2):
            out = slice(copy * width + place * LANES, copy * width + (place + 1) * LANES)
            rob[0:LANES, out] = wh[:, cols]
            rob[LANES:, out] = wl[:, cols]


def store_tables(tab, parts, besides, halo):
    for q, (own, beside) in enumerate(zip(parts, besides)):
        for h, table in enumerate(windows(own, beside, halo)):
            hi, lo = split(table)
            tab[h, q * LANES : (q + 1) * LANES, 0:LANES] = hi
            tab[h, q * LANES : (q + 1) * LANES, LANES:] = lo


def centre_offsets(rows, basis_count):
    place = lax.broadcasted_iota(jnp.int32, (basis_count, LANES), 0).astype(F32)
    centres = 8.0 * place / (basis_count - 1)
    return jnp.concatenate([g[3:4] - centres for g in rows], axis=1)


def sharpness(basis_count):
    return 0.5 * ((basis_count - 1) / 8.0) ** 2


def edge_rows(geom, t):
    return [geom[t * ROWS + q] for q in range(ROWS)]


def radial(rows, t, ri4, ro3, kept, basis_count):
    filters_ref, hidden_ref, basis_ref, slope_ref = kept
    offset = centre_offsets(rows, basis_count)
    bh, bl = split(jnp.exp(-sharpness(basis_count) * offset * offset))
    basis_ref[t] = jnp.concatenate([bh, bl], axis=0)
    pre = mm(ri4[...], jnp.concatenate([bh, bl, bh, bl], axis=0))
    gate = sigmoid(pre)
    mask = jnp.concatenate([g[4:5] for g in rows], axis=1)
    slope_ref[t] = mask * (gate * (1.0 + pre * (1.0 - gate)))
    hh, hl = split(pre * gate * mask)
    hidden_ref[t] = jnp.concatenate([hh, hl], axis=0)
    filters = mm(ro3[...], jnp.concatenate([hh, hl, hh], axis=0))
    filters_ref[t] = filters
    return filters


def one_hot_of(rows):
    place = lax.broadcasted_iota(jnp.int32, (LANES, LANES), 0).astype(F32)
    return jnp.concatenate(
        [jnp.where(place == g[5:6], 1.0, 0.0).astype(BF16) for g in rows], axis=1
    )


def part(x, group, q):
    return x[group * LANES : (group + 1) * LANES, q * LANES : (q + 1) * LANES]


def radial_edges(geom, ri4, ro3, kept, basis_count):
    def step(t, carry):
        radial(edge_rows(geom, t), t, ri4, ro3, kept, basis_count)
        return carry

    for t in range(geom.shape[0] // ROWS):
        step(t, 0)


def forward_edges(geom, tab, acc, found_ref, filters_of, vectors):
    per_half = geom.shape[0] // 2 // ROWS
    acc[...] = jnp.zeros(acc.shape, F32)
    wide = 2 if vectors else 1

    def step(t, carry):
        h = t // per_half
        rows = edge_rows(geom, t)
        filters = filters_of(rows, t)
        hot = one_hot_of(rows)
        found = mm(tab[h], jnp.concatenate([hot, hot], axis=0))
        found_ref[t] = found
        sums = [None] * 4
        for q, g in enumerate(rows):
            s = part(found, 0, q)
            terms = [part(filters, 0, q) * s]
            push = part(filters, wide, q) * s
            for c in range(3):
                term = push * g[c : c + 1]
                if vectors:
                    term = term + part(filters, 1, q) * part(found, 1 + c, q)
                terms.append(term)
            sums = [x if y is None else y + x for x, y in zip(terms, sums)]
        for n in range(4):
            acc[h, n] += sums[n]
        return carry

    for t in range(2 * per_half):
        step(t, 0)


def aggregates(acc, scale):
    return [folded(acc[0, n], acc[1, n]) * scale for n in range(4)]


def node_forward(agg, sm, vm, vg):
    mixed = mm3(vm.T, jnp.concatenate(agg[1:], axis=1))
    w = [mixed[:, c * LANES : (c + 1) * LANES] for c in range(3)]
    size = jnp.sqrt(w[0] * w[0] + w[1] * w[1] + w[2] * w[2] + 1.0)
    u = mm3(sm.T, agg[0]) + (size - 1.0)
    gate = sigmoid(mm3(vg.T, agg[0]))
    return w, size, u, gate


def node_backward(agg, w, size, u, gate, sm, vm, vg, ds, dv, scale):
    act = sigmoid(u)
    du = ds * (act * (1.0 + u * (1.0 - act)))
    ratio = du / size
    dw = [w[c] * ratio + dv[c] * gate for c in range(3)]
    dq = (dv[0] * w[0] + dv[1] * w[1] + dv[2] * w[2]) * gate * (1.0 - gate)
    dw_all = jnp.concatenate(dw, axis=1)
    da_s = (mm3(sm, du) + mm3(vg, dq)) * scale
    da_v = mm3(vm, dw_all) * scale
    da = [da_s] + [da_v[:, c * LANES : (c + 1) * LANES] for c in range(3)]
    g_sm = mm3_nt(agg[0], du)
    g_vg = mm3_nt(agg[0], dq)
    g_vm = mm3_nt(jnp.concatenate(agg[1:], axis=1), dw_all)
    return da, g_sm, g_vm, g_vg


def source_terms(rows, filters, found, gs, gv, vectors):
    wide = 2 if vectors else 1
    columns = []
    for q, g in enumerate(rows):
        along = gv[0] * g[0:1] + gv[1] * g[1:2] + gv[2] * g[2:3]
        sources = [part(filters, 0, q) * gs + part(filters, wide, q) * along]
        if vectors:
            f_v = part(filters, 1, q)
            sources += [f_v * gv[c] for c in range(3)]
        columns.append(jnp.concatenate(sources, axis=0))
    return columns


def scatter(columns, hot):
    sh, sl = split(jnp.concatenate(columns, axis=1))
    return mm_nt(jnp.concatenate([sh, sl], axis=1), jnp.concatenate([hot, hot], axis=1))


def step_derivatives(gacc, h):
    return gacc[h, 0], [gacc[h, 1 + c] for c in range(3)]


def filter_terms(rows, t, kept, found, gs, gv, rib, rob, dro, dri, basis_count, vectors):
    filters_ref, hidden_ref, basis_ref, slope_ref = kept
    wide = 2 if vectors else 1
    d_filters, d_dirs = [], []
    for q, g in enumerate(rows):
        s = part(found, 0, q)
        along = gv[0] * g[0:1] + gv[1] * g[1:2] + gv[2] * g[2:3]
        groups = [gs * s]
        if vectors:
            v = [part(found, 1 + c, q) for c in range(3)]
            groups.append(gv[0] * v[0] + gv[1] * v[1] + gv[2] * v[2])
        groups.append(s * along)
        d_filters.append(jnp.concatenate(groups, axis=0))
        push = part(filters_ref.at[t], wide, q) * s
        d_dirs.append([jnp.sum(push * gv[c], axis=0, keepdims=True) for c in range(3)])
    fh, fl = split(jnp.concatenate(d_filters, axis=1))
    both = hidden_ref[t]
    if vectors:
        dro[...] += mm_nt(jnp.concatenate([fh, fl], axis=1), jnp.concatenate([both, both], axis=1))
    else:
        pair = mm_nt(both, fh)
        dro[...] += pair[:LANES] + pair[LANES:] + mm_nt(both[:LANES], fl)
    spread = mm(rob[...], jnp.concatenate([fh, fl], axis=0))
    d_pre = (spread[:LANES] + spread[LANES:]) * slope_ref[t]
    ph, plo = split(d_pre)
    bb = basis_ref[t]
    dri[...] += mm_nt(jnp.concatenate([ph, plo], axis=1), jnp.concatenate([bb, bb], axis=1))
    back = mm(rib[...], jnp.concatenate([ph, plo], axis=0))
    d_basis = back[:basis_count] + back[basis_count:]
    basis = bb[:basis_count].astype(F32) + bb[basis_count:].astype(F32)
    offset = centre_offsets(rows, basis_count)
    d_dist = jnp.sum(d_basis * basis * offset, axis=0, keepdims=True) * (-2.0 * sharpness(basis_count))
    return d_dirs, [d_dist[:, q * LANES : (q + 1) * LANES] for q in range(len(rows))]


def radial_grads(dro, dri, out, row_in, row_out, basis_count, groups, turned):
    both = dri[...]
    turned_in = both + pltpu.roll(both, HALF, 1)
    out[row_in : row_in + basis_count] = turned_in.T[0:basis_count]
    for place in range(groups):
        block = slice(place * LANES, (place + 1) * LANES)
        grad = (dro[block, 0:LANES] + dro[block, LANES:]).T if turned else dro[:, block]
        out[row_out + place * LANES : row_out + (place + 1) * LANES] = grad


def species_hot(row, count):
    place = lax.broadcasted_iota(jnp.int32, (count, LANES), 0).astype(F32)
    return jnp.where(place == row, 1.0, 0.0).astype(BF16)


def first_features(emb_ref, hot):
    high, rest = split(emb_ref[...])
    low = (emb_ref[...] - high.astype(F32) - rest.astype(F32)).astype(BF16)
    dims = (((0,), (0,)), ((), ()))
    terms = [
        lax.dot_general(x.astype(F32).T.astype(BF16), hot, (((1,), (0,)), ((), ())), preferred_element_type=F32)
        for x in (high, rest, low)
    ]
    return terms[0] + (terms[1] + terms[2])


def from_sides(par_ref, a_ref, b_ref):
    even = is_even(par_ref, a_ref.shape)
    a, b = a_ref[...], b_ref[...]
    return jnp.where(even, a, b), jnp.where(even, b, a)


def species_tables(own_ref, up, down, emb_ref, halo):
    lane = lane_ids(1)
    count = emb_ref.shape[0]
    beside = jnp.where(lane >= LANES - halo, down[3:4], up[3:4])
    hot_own, hot_beside = species_hot(own_ref[3:4], count), species_hot(beside, count)
    return hot_own, hot_beside


def positions(cell_ref, fractions):
    rows = [
        fractions[0:1] * cell_ref[0, 0, c] + fractions[1:2] * cell_ref[1, 0, c] + fractions[2:3] * cell_ref[2, 0, c]
        for c in range(3)
    ]
    return jnp.concatenate(rows + [fractions[3:8]], axis=0)


def prepare_kernel(rin_ref, rout_ref, *outs):
    for layer, groups in enumerate(((0, 2), (0, 1, 2))):
        ri4, ro3, rib, rob = outs[4 * layer : 4 * layer + 4]
        rin, rout = rin_ref.at[pl.ds(layer, 1)], rout_ref.at[pl.ds(layer, 1)]
        prepare_weights(rin, rout, ri4, ro3, groups)
        prepare_back(rin, rout, rib, rob, groups)


def first_kernel(
    halo, par_ref, cell_ref, own_ref, a_ref, b_ref, nb_ref, count_ref, shift_ref, emb_ref, ri4, ro3,
    sm_ref, vm_ref, vg_ref,
    geom_ref, feat_ref, agg_ref, node_ref, send_a, send_b, filters_ref, hidden_ref, basis_ref, slope_ref, found_ref,
    tab, acc,
):
    slots = nb_ref.shape[0]
    basis_count = ri4.shape[1] // 4
    pairs = slots // 2
    up, down = from_sides(par_ref, a_ref, b_ref)
    lane = lane_ids(pairs)
    low = lane < HALF

    def halves(ref, *lead):
        even = ref[(*lead, pl.ds(0, pairs, stride=2), slice(None))]
        odd = ref[(*lead, pl.ds(1, pairs, stride=2), slice(None))]
        return jnp.where(low, even, pltpu.roll(odd, HALF, 1)), jnp.where(low, pltpu.roll(even, HALF, 1), odd)

    nb = halves(nb_ref)
    shift = [halves(shift_ref, a) for a in range(3)]
    row_slot = 2 * lax.broadcasted_iota(jnp.int32, (pairs, LANES), 0) + jnp.where(low, 0, 1)
    own, up, down = [positions(cell_ref, x) for x in (own_ref[...], up, down)]
    lane8 = lane_ids(own.shape[0])
    places = (jnp.where(lane8 < LANES - halo, own, down), jnp.where(lane8 >= halo, own, up))
    for h in range(2):
        index = (nb[h] - halo) & (LANES - 1)
        near = twice(own, h)
        count = twice(count_ref[...], h)
        mask = jnp.where(row_slot < count, 1.0, 0.0).astype(F32)
        steps = [shift[a][h].astype(F32) for a in range(3)]
        r = []
        for c in range(3):
            table = jnp.broadcast_to(places[h][c : c + 1], (pairs, LANES))
            far = jnp.take_along_axis(table, index, axis=1, mode="promise_in_bounds")
            image = steps[0] * cell_ref[0, 0, c] + steps[1] * cell_ref[1, 0, c] + steps[2] * cell_ref[2, 0, c]
            r.append(far - near[c : c + 1] + image)
        dist = jnp.sqrt(r[0] * r[0] + r[1] * r[1] + r[2] * r[2] + 1.0)
        values = [x / dist for x in r] + [dist, mask, index.astype(F32)]
        for n, x in enumerate(values):
            for m in range(pairs):
                geom_ref[h * pairs + m, n : n + 1, :] = x[m : m + 1]
    hot_own, hot_beside = species_tables(own_ref, up, down, emb_ref, halo)
    s, beside = first_features(emb_ref, hot_own), first_features(emb_ref, hot_beside)
    store_tables(tab, [s], [beside], halo)
    kept = (filters_ref, hidden_ref, basis_ref, slope_ref)
    forward_edges(
        geom_ref, tab, acc, found_ref, lambda rows, t: radial(rows, t, ri4, ro3, kept, basis_count), False
    )
    agg = aggregates(acc, slots**-0.5)
    w, size, u, gate = node_forward(agg, sm_ref[0], vm_ref[0], vg_ref[0])
    features = [s + u * sigmoid(u)] + [w[c] * gate for c in range(3)]
    for n, x in enumerate(w + [size, u, gate]):
        node_ref[n] = x
    for n in range(4):
        agg_ref[n] = agg[n]
        feat_ref[n] = features[n]
    tail, head = packed(features, halo, True), packed(features, halo, False)
    even = is_even(par_ref, tail.shape)
    send_a[...] = jnp.where(even, tail, head)
    send_b[...] = jnp.where(even, head, tail)


def radial_kernel(geom_ref, ri4, ro3, filters_ref, hidden_ref, basis_ref, slope_ref):
    radial_edges(geom_ref, ri4, ro3, (filters_ref, hidden_ref, basis_ref, slope_ref), ri4.shape[1] // 4)


def second_kernel(
    halo, par_ref, geom_ref, feat_ref, a_ref, b_ref, filters_ref, sm_ref, vm_ref, vg_ref, mid_ref, out_ref,
    cot_ref, send_a, send_b, grad_ref, mid_tail, gacc, found_ref,
    tab, acc, dtab,
):
    slots = geom_ref.shape[0]
    scale = slots**-0.5
    up, down = from_sides(par_ref, a_ref, b_ref)
    lane = lane_ids(LANES)
    features = [feat_ref[n] for n in range(4)]
    besides = [
        jnp.where(lane >= LANES - halo, unpacked(down, q, halo, True), unpacked(up, q, halo, False)) for q in range(4)
    ]
    store_tables(tab, features, besides, halo)
    forward_edges(geom_ref, tab, acc, found_ref, lambda rows, t: filters_ref.at[t], True)

    @pl.when(par_ref[0] >= 0)
    def _():
        agg = aggregates(acc, scale)
        sm, vm, vg = sm_ref[0], vm_ref[0], vg_ref[0]
        w, size, u, gate = node_forward(agg, sm, vm, vg)
        s = feat_ref[0] + u * sigmoid(u)
        mid = mid_ref[...]
        hidden = mm3(mid.T, s)
        act = sigmoid(hidden)
        shown = hidden * act
        weights = jnp.broadcast_to(out_ref[...], (8, LANES))
        per_atom = mm3(weights, shown)
        send_a[LANES:] = jnp.broadcast_to(jnp.sum(per_atom, axis=1, keepdims=True), (8, LANES))
        weight_column = jnp.broadcast_to(out_ref[...], (LANES, LANES)).T
        d_hidden = weight_column * (act * (1.0 + hidden * (1.0 - act)))
        ds = mm3(mid, d_hidden)
        zero = jnp.zeros((LANES, LANES), F32)
        dv = [zero, zero, zero]
        da, g_sm, g_vm, g_vg = node_backward(agg, w, size, u, gate, sm, vm, vg, ds, dv, scale)
        for n in range(4):
            for h in range(2):
                gacc[h, n] = twice(da[n], h)
        for n, x in enumerate([ds] + dv):
            cot_ref[n] = x
        row = 0
        for grad in (g_sm, g_vm, g_vg):
            grad_ref[row : row + LANES] = grad
            row += LANES
        grad_ref[row : row + 8] = mm3_nt(jnp.ones((8, LANES), F32), shown)
        g_mid = mm3_nt(s, d_hidden)
        grad_ref[row + 8 :] = g_mid[:MID_ROWS]
        mid_tail[...] = g_mid[MID_ROWS:]

    per_half = slots // 2 // ROWS
    dtab[...] = jnp.zeros(dtab.shape, F32)

    def step(t, carry):
        h = t // per_half
        rows = edge_rows(geom_ref, t)
        gs, gv = step_derivatives(gacc, h)
        columns = source_terms(rows, filters_ref.at[t], found_ref.at[t], gs, gv, True)
        dtab[h] += scatter(columns, one_hot_of(rows))
        return carry

    for t in range(2 * per_half):
        step(t, 0)
    firsts = [dtab[0, q * LANES : (q + 1) * LANES] for q in range(4)]
    seconds = [dtab[1, q * LANES : (q + 1) * LANES] for q in range(4)]
    for q in range(4):
        cot_ref[q] += (
            jnp.where(lane < LANES - halo, firsts[q], 0.0) + jnp.where(lane >= halo, seconds[q], 0.0)
        )
    to_prev, to_next = packed(firsts, halo, True), packed(seconds, halo, False)
    even = is_even(par_ref, to_prev.shape)
    send_a[:LANES] = jnp.where(even, to_next, to_prev)
    send_b[...] = jnp.where(even, to_prev, to_next)


def radial_back_kernel(
    t, geom_ref, filters_ref, hidden_ref, basis_ref, slope_ref, found_ref, gacc, rib, rob, *rest
):
    basis_count = rib.shape[0] // 2
    last = len(rest) > 3
    if last:
        dro_first, dri_first, mixed_ref, dgeom_ref, grad_ref, dro, dri = rest
        dro[...] = dro_first[...]
        dri[...] = dri_first[...]
    else:
        dgeom_ref, dro, dri = rest
        dro[...] = jnp.zeros(dro.shape, F32)
        dri[...] = jnp.zeros(dri.shape, F32)
    kept = (filters_ref, hidden_ref, basis_ref, slope_ref)
    rows = edge_rows(geom_ref, t)
    gs, gv = step_derivatives(gacc, t // (geom_ref.shape[0] // 2 // ROWS))
    d_dirs, d_dists = filter_terms(rows, t, kept, found_ref.at[t], gs, gv, rib, rob, dro, dri, basis_count, True)
    for q in range(ROWS):
        for c in range(3):
            dgeom_ref[q, c : c + 1, :] = d_dirs[q][c]
        dgeom_ref[q, 3:4, :] = d_dists[q]
    if last:
        radial_grads(dro, dri, grad_ref, 0, basis_count, basis_count, 3, True)
        grad_ref[basis_count + 3 * LANES :] = mixed_ref[...]


def third_kernel(
    halo, par_ref, geom_ref, dgeom_one, dgeom_two, agg_ref, node_ref, cot_ref, a_ref, b_ref, own_ref, pa_ref, pb_ref, mid_tail,
    filters_ref, hidden_ref, basis_ref, slope_ref, found_ref, emb_ref, rib, rob, sm_ref, vm_ref, vg_ref,
    force_ref, send_ref, grad_ref,
    gacc, dro, dri, dtab, pull, virial,
):
    basis_count = rib.shape[0] // 2
    slots = geom_ref.shape[0]
    scale = slots**-0.5
    lane = lane_ids(LANES)
    up, down = from_sides(par_ref, a_ref.at[:LANES], b_ref)
    cot = []
    for q in range(4):
        cot.append(
            cot_ref[q]
            + jnp.where(lane >= LANES - halo, unpacked(up, q, halo, True), 0.0)
            + jnp.where(lane < halo, unpacked(down, q, halo, False), 0.0)
        )
    place_up, place_down = from_sides(par_ref, pa_ref, pb_ref)
    hot_own, hot_beside = species_tables(own_ref, place_up, place_down, emb_ref, halo)
    count = emb_ref.shape[0]

    @pl.when(par_ref[0] >= 0)
    def _():
        agg = [agg_ref[n] for n in range(4)]
        sm, vm, vg = sm_ref[0], vm_ref[0], vg_ref[0]
        w, (size, u, gate) = [node_ref[c] for c in range(3)], [node_ref[n] for n in range(3, 6)]
        da, g_sm, g_vm, g_vg = node_backward(agg, w, size, u, gate, sm, vm, vg, cot[0], cot[1:], scale)
        for n in range(4):
            for h in range(2):
                gacc[h, n] = twice(da[n], h)
        row = count + basis_count + 2 * LANES
        for g in (g_sm, g_vm, g_vg):
            grad_ref[row : row + LANES] = g
            row += LANES

    pull[...] = jnp.zeros(pull.shape, F32)
    virial[...] = jnp.zeros(virial.shape, F32)

    def finish(row, g, d_dir, d_dist):
        more = (dgeom_one, dgeom_two)[row // ROWS][row % ROWS]
        dist = g[3:4]
        toward = [g[c : c + 1] for c in range(3)]
        turn = [d_dir[c] + more[c : c + 1] for c in range(3)]
        inner = turn[0] * toward[0] + turn[1] * toward[1] + turn[2] * toward[2]
        stretch = d_dist + more[3:4]
        inverse = 1.0 / dist
        dr = [(turn[c] - toward[c] * inner) * inverse + stretch * toward[c] for c in range(3)]
        r = [toward[c] * dist for c in range(3)]
        lines = jnp.concatenate(dr + [jnp.zeros((13, LANES), F32)], axis=0)
        products = [r[a] * dr[c] for a in range(3) for c in range(3)]
        return lines, jnp.concatenate(products + [jnp.zeros((7, LANES), F32)], axis=0)

    kept = (filters_ref, hidden_ref, basis_ref, slope_ref)
    per_half = slots // 2 // ROWS
    dro[...] = jnp.zeros(dro.shape, F32)
    dri[...] = jnp.zeros(dri.shape, F32)
    dtab[...] = jnp.zeros(dtab.shape, F32)

    def step(t, carry):
        h = t // per_half
        rows = edge_rows(geom_ref, t)
        gs, gv = step_derivatives(gacc, h)
        found = found_ref.at[t]
        d_dirs, d_dists = filter_terms(rows, t, kept, found, gs, gv, rib, rob, dro, dri, basis_count, False)
        columns = source_terms(rows, filters_ref.at[t], found, gs, gv, False)
        pairs = [finish(t * ROWS + q, g, d_dirs[q], d_dists[q]) for q, g in enumerate(rows)]
        pull[h] += sum(x for x, _ in pairs[1:]) + pairs[0][0]
        virial[...] += sum(x for _, x in pairs[1:]) + pairs[0][1]
        columns = [jnp.concatenate([x, y], axis=0) for x, (y, _) in zip(columns, pairs)]
        dtab[h] += scatter(columns, one_hot_of(rows))
        return carry

    for t in range(2 * per_half):
        step(t, 0)
    first, second = dtab[0, 0:LANES], dtab[1, 0:LANES]
    own_cot = cot[0] + jnp.where(lane < LANES - halo, first, 0.0) + jnp.where(lane >= halo, second, 0.0)
    side_cot = jnp.where(lane >= LANES - halo, first, 0.0) + jnp.where(lane < halo, second, 0.0)
    grad = 0.0
    for hot, value in ((hot_own, own_cot), (hot_beside, side_cot)):
        hi, lo = split(value)
        grad = grad + (mm_nt(hot, hi) + mm_nt(hot, lo))
    grad_ref[0:count] = grad
    row = count
    radial_grads(dro, dri, grad_ref, row, row + basis_count, basis_count, 2, False)
    row += basis_count + 5 * LANES
    grad_ref[row:] = jnp.zeros((grad_ref.shape[0] - row, LANES), F32)
    grad_ref[row + 8 : row + 8 + mid_tail.shape[0]] = mid_tail[...]
    sublane = lax.broadcasted_iota(jnp.int32, (16, LANES), 0)
    total = jnp.broadcast_to(jnp.sum(virial[...], axis=1, keepdims=True), virial.shape)
    nine = jnp.sum(jnp.where(lane_ids(16) == sublane, total, 0.0), axis=0, keepdims=True)
    mine = (sublane[:8] - par_ref[1]) == 0
    grad_ref[row : row + 8] = jnp.where(mine, nine, 0.0)
    lane16 = lane_ids(16)
    first, second = dtab[0, LANES:], dtab[1, LANES:]
    force_ref[...] = (
        jnp.where(lane16 < LANES - halo, first, 0.0)
        + jnp.where(lane16 >= halo, second, 0.0)
        - folded(pull[0], pull[1])
    )
    even = is_even(par_ref, first.shape)
    send_ref[0:8] = jnp.where(even, second, first)[0:8]
    send_ref[8:16] = jnp.where(even, first, second)[0:8]


def final_kernel(
    halo, par_ref, cell_ref, sum_energy, force_ref, a_ref, b_ref, mine_turned, other_turned,
    energy_ref, forces_ref, stress_ref, emb_ref, rin_ref, rout_ref, sm_ref, vm_ref, vg_ref, mid_ref, out_ref,
    mine, other,
):
    energy_ref[0, 0] = jnp.max(sum_energy[0:1])
    rows = mine.shape[0] // 4
    for c in range(4):
        turned = pl.ds(pl.multiple_of((par_ref[2] ^ c) * rows, 8), rows)
        mine[c * rows : (c + 1) * rows] = mine_turned[turned]
        other[c * rows : (c + 1) * rows] = other_turned[turned]
    lane = lane_ids(8)
    up, down = from_sides(par_ref, a_ref, b_ref.at[pl.ds(pl.multiple_of(8 * par_ref[3], 8), 8)])
    force = force_ref[0:8] + jnp.where(lane >= LANES - halo, up, 0.0) + jnp.where(lane < halo, down, 0.0)
    forces_ref[...] = -force[0:3]
    count, basis_count = emb_ref.shape[0], rin_ref.shape[1]
    m = [[cell_ref[a, 0, c] for c in range(3)] for a in range(3)]
    det = (
        m[0][0] * (m[1][1] * m[2][2] - m[1][2] * m[2][1])
        - m[0][1] * (m[1][0] * m[2][2] - m[1][2] * m[2][0])
        + m[0][2] * (m[1][0] * m[2][1] - m[1][1] * m[2][0])
    )

    def write(one, two):
        emb_ref[...] = one[0:count]
        row = count
        rin_ref[0] = one[row : row + basis_count]
        rin_ref[1] = two[0:basis_count]
        row += basis_count
        rout_ref[0, :, 0:LANES] = one[row : row + LANES]
        rout_ref[0, :, LANES : 2 * LANES] = jnp.zeros((LANES, LANES), F32)
        rout_ref[0, :, 2 * LANES :] = one[row + LANES : row + 2 * LANES]
        row += 2 * LANES
        line = basis_count
        for g in range(3):
            rout_ref[1, :, g * LANES : (g + 1) * LANES] = two[line : line + LANES]
            line += LANES
        for ref in (sm_ref, vm_ref, vg_ref):
            ref[0] = one[row : row + LANES]
            ref[1] = two[line : line + LANES]
            row += LANES
            line += LANES
        out_ref[...] = two[line : line + 1]
        mid_ref[0:MID_ROWS] = two[line + 8 : line + 8 + MID_ROWS]
        mid_ref[MID_ROWS:] = one[row + 8 : row + 8 + LANES - MID_ROWS]
        wanted = (lax.broadcasted_iota(jnp.int32, (8, LANES), 0) - par_ref[1]) == 0
        nine = jnp.sum(jnp.where(wanted, one[row : row + 8], 0.0), axis=0, keepdims=True)
        stress = jnp.broadcast_to(nine, (8, LANES)) / (jnp.zeros((8, LANES), F32) + det)
        lines = [stress] + [pltpu.roll(stress, LANES - 3 * a, 1) for a in (1, 2)]
        for a in range(3):
            stress_ref[a] = lines[a][0:1, 0:3]

    @pl.when(par_ref[1] % 2 == 0)
    def _():
        write(other, mine)

    @pl.when(par_ref[1] % 2 == 1)
    def _():
        write(mine, other)


def side_one(x, axis):
    return lax.ppermute(x, axis, [(i, i ^ 1) for i in range(lax.axis_size(axis))])


def side_two(x, axis):
    size = lax.axis_size(axis)
    return lax.ppermute(x, axis, [(i, (i + 1) % size if i % 2 else (i - 1) % size) for i in range(size)])


def after(x, *others):
    return lax.optimization_barrier((x,) + others)[0]


def swap(x, axis, bit):
    return lax.ppermute(x, axis, [(i, i ^ bit) for i in range(lax.axis_size(axis))])


def layer_spec(x, layer):
    rest = x.shape[1:]
    return pl.BlockSpec((1,) + rest, lambda i: (layer,) + (0,) * len(rest))


def vmem():
    return pl.BlockSpec(memory_space=pltpu.VMEM)


def smem():
    return pl.BlockSpec(memory_space=pltpu.SMEM)


def whole(x):
    return pl.BlockSpec(x.shape, lambda i: (0,) * len(x.shape))


def f32(*shape):
    return jax.ShapeDtypeStruct(shape, F32)


def call(kernel, name, outs, in_specs, out_specs, scratch, flops, *args):
    return pl.pallas_call(
        kernel,
        grid=(1,),
        out_shape=outs,
        in_specs=in_specs,
        out_specs=out_specs,
        scratch_shapes=scratch,
        compiler_params=pltpu.CompilerParams(vmem_limit_bytes=VMEM_LIMIT),
        cost_estimate=pl.CostEstimate(flops=flops, bytes_accessed=flops // 500, transcendentals=0),
        name=name,
    )(*args)


def exchange(x, moves):
    groups, slabs = lax.axis_size("dp"), lax.axis_size("atom")
    route = []
    for g in range(groups):
        for p in range(slabs):
            to_g, to_p = moves(g, p)
            route.append((g * slabs + p, to_g * slabs + to_p))
    return lax.ppermute(x, ("dp", "atom"), route)


def local(
    frac, species, neighbours, counts, shifts, cell, energy_ref, embedding, radial_in, radial_out, scalar_mix,
    vector_mix, vector_gate, readout_mid, readout_out,
):
    atom_count = frac.shape[1]
    halo = atom_count // 4
    slots = neighbours.shape[0]
    basis_count = radial_in.shape[1]
    me = lax.axis_index("atom")
    group = lax.axis_index("dp")
    counts_row, out_row = counts[None], readout_out[None]
    lattice = cell.transpose(1, 0, 2)
    own_row = lax.broadcasted_iota(jnp.int32, (8, 1), 0)
    own = jnp.pad(frac, ((0, 5), (0, 0))) + jnp.where(own_row == 3, species[None], 0).astype(F32)
    side_a, side_b = side_one(own, "atom"), side_two(own, "atom")
    plane = group // 2 * 2 + me % 2
    slabs = lax.axis_size("atom")
    levels = (slabs - 1).bit_length() - 1
    bits = [2 << n for n in range(levels)]
    opposite = jnp.where(me % 2 == 1, (me + 1) % slabs, (me + slabs - 1) % slabs)
    turned = (me ^ opposite ^ 1) >> 1
    par = jnp.stack([me % 2, group, plane, turned]).astype(jnp.int32)
    layer = (radial_in, radial_out, scalar_mix, vector_mix, vector_gate)
    block = f32(LANES, LANES)
    edges, steps = ROWS * LANES, slots // ROWS

    def kept(groups):
        halves = tuple(jax.ShapeDtypeStruct((steps, n, edges), BF16) for n in (2 * LANES, 2 * basis_count))
        return (f32(steps, groups * LANES, edges),) + halves + (f32(steps, LANES, edges),)

    prepared = call(
        prepare_kernel,
        "prepare",
        tuple(
            jax.ShapeDtypeStruct(shape, BF16)
            for n in (2, 3)
            for shape in (
                (LANES, 4 * basis_count), (n * LANES, 3 * LANES), (2 * basis_count, 2 * LANES), (2 * LANES, 2 * n * LANES)
            )
        ),
        [vmem()] * 2,
        [vmem()] * 8,
        [],
        10**10,
        radial_in, radial_out,
    )
    geom, feat, agg, node, feat_a, feat_b, *kept_one = call(
        functools.partial(first_kernel, halo),
        "layer_one",
        (f32(slots, 8, LANES), f32(4, LANES, LANES), f32(4, LANES, LANES), f32(6, LANES, LANES), block, block) + kept(2)
        + (f32(steps, LANES, edges),),
        [smem(), smem()] + [vmem()] * 9 + [layer_spec(x, 0) for x in layer[2:]],
        [vmem()] * 11,
        [
            pltpu.VMEM((2, LANES, 2 * LANES), BF16),
            pltpu.VMEM((2, 4, LANES, LANES), F32),
        ],
        3 * 10**9,
        par, lattice, own, side_a, side_b, neighbours, counts_row, shifts, embedding, *prepared[:2], *layer[2:],
    )
    feat_a, feat_b = side_one(feat_a, "atom"), side_two(feat_b, "atom")
    kept_two = call(
        radial_kernel,
        "radial_two",
        kept(3),
        [vmem()] * 3,
        [vmem()] * 4,
        [],
        3 * 10**9,
        geom, *prepared[4:6],
    )
    tail_rows = LANES - MID_ROWS
    mixed_rows = 3 * LANES + 8 + MID_ROWS
    cot, cot_a, cot_b, mixed, mid_tail, gacc, found_two = call(
        functools.partial(second_kernel, halo),
        "layer_two",
        (
            f32(4, LANES, LANES), f32(LANES + 8, LANES), block, f32(mixed_rows, LANES), f32(tail_rows, LANES),
            f32(2, 4, LANES, LANES), f32(steps, 4 * LANES, edges),
        ),
        [smem()] + [vmem()] * 5 + [layer_spec(x, 1) for x in layer[2:]] + [whole(readout_mid), whole(out_row)],
        [vmem()] * 7,
        [
            pltpu.VMEM((2, 4 * LANES, 2 * LANES), BF16),
            pltpu.VMEM((2, 4, LANES, LANES), F32),
            pltpu.VMEM((2, 4 * LANES, LANES), F32),
        ],
        5 * 10**9,
        par, geom, feat, feat_a, feat_b, kept_two[0], *layer[2:], readout_mid, out_row,
    )
    energy = cot_a[LANES:]
    cot_a = side_one(cot_a, "atom")
    back_args = (geom, *kept_two, found_two, gacc, *prepared[6:8])
    sums = (f32(3 * LANES, 2 * LANES), f32(LANES, 2 * basis_count))
    dgeom_one, dro_first, dri_first = call(
        functools.partial(radial_back_kernel, 0),
        "radial_two_back",
        (f32(ROWS, 8, LANES),) + sums,
        [vmem()] * 9,
        [vmem()] * 3,
        [],
        3 * 10**9,
        *back_args,
    )
    energy = energy + cot_a[LANES:]
    moved = swap(energy, "atom", 2)
    cot_b = side_two(after(cot_b, dri_first), "atom")
    dgeom_two, grads_two = call(
        functools.partial(radial_back_kernel, 1),
        "radial_two_back_last",
        (f32(ROWS, 8, LANES), f32(G_ROWS, LANES)),
        [vmem()] * 12,
        [vmem()] * 2,
        [pltpu.VMEM(x.shape, F32) for x in sums],
        3 * 10**9,
        *back_args, dro_first, after(dri_first, energy), mixed,
    )
    energy = after(energy + moved, dgeom_two)
    if slabs > 4:
        energy = energy + swap(energy, "atom", 4)
    force, force_sent, grads_one = call(
        functools.partial(third_kernel, halo),
        "layer_one_back",
        (f32(16, LANES), f32(16, LANES), f32(G_ROWS, LANES)),
        [smem()] + [vmem()] * 20 + [layer_spec(x, 0) for x in layer[2:]],
        [vmem()] * 3,
        [
            pltpu.VMEM((2, 4, LANES, LANES), F32),
            pltpu.VMEM((LANES, 2 * LANES), F32),
            pltpu.VMEM((LANES, 2 * basis_count), F32),
            pltpu.VMEM((2, LANES + 16, LANES), F32),
            pltpu.VMEM((2, 16, LANES), F32),
            pltpu.VMEM((16, LANES), F32),
        ],
        6 * 10**9,
        par, geom, dgeom_one, dgeom_two, agg, node, cot, cot_a, cot_b, own, side_a, side_b, mid_tail, *kept_one,
        embedding, *prepared[2:4], *layer[2:],
    )
    for bit in bits[2:]:
        energy = energy + swap(energy, "atom", bit)
    cell_atoms = atom_count * slabs
    loss_scale = 2.0 * (energy[0:1] / cell_atoms - energy_ref[0]) / cell_atoms
    virial_row = embedding.shape[0] + basis_count + 5 * LANES
    line = lax.broadcasted_iota(jnp.int32, (G_ROWS, 1), 0)
    one = grads_one * jnp.where((line >= virial_row) & (line < virial_row + 8), 1.0, loss_scale)
    two = grads_two * loss_scale
    core = group % 2 == 1
    x = jnp.where(core, one, two) + swap(jnp.where(core, two, one), "dp", 1)
    quarter = G_ROWS // 4

    def piece(k):
        return lax.dynamic_slice_in_dim(x, (plane ^ k) * quarter, quarter, 0)

    def plane_move(k):
        return lambda g, p: (g ^ (2 * (k >> 1)), p ^ (k & 1))

    link_a, link_b = jnp.where(core, 2, 1), jnp.where(core, 1, 2)

    def move_a(g, p):
        return plane_move(2 if g % 2 else 1)(g, p)

    def move_b(g, p):
        return plane_move(1 if g % 2 else 2)(g, p)

    got_a = exchange(jnp.concatenate([piece(link_a), force_sent]), move_a)
    got_b = exchange(jnp.concatenate([piece(link_b), force_sent]), move_b)
    got_c = exchange(piece(3), plane_move(3))
    joined = jnp.where(core, got_b, got_a)[quarter:]
    force_a, force_b = joined[:8], joined[8:]
    y = piece(0) + got_a[:quarter] + got_b[:quarter] + got_c
    for n in range(levels):
        one_bit = bits[n]
        joined = exchange(jnp.concatenate([y, force_b]), lambda g, p: (g, p ^ one_bit))
        y = y + joined[:quarter]
        force_b = jnp.concatenate([force_b, joined[quarter:]])
    all_a, all_b = exchange(y, move_a), exchange(y, move_b)
    all_c = exchange(y, plane_move(3))
    x = jnp.concatenate([y, jnp.where(core, all_b, all_a), jnp.where(core, all_a, all_b), all_c])
    other = swap(x, "dp", 1)
    weights = (embedding,) + layer + (readout_mid, out_row)
    outs = (f32(1, 1), f32(3, atom_count), f32(3, 1, 3)) + tuple(f32(*x.shape) for x in weights)
    result = call(
        functools.partial(final_kernel, halo),
        "final",
        outs,
        [smem(), smem()] + [vmem()] * 6,
        [smem()] + [whole(x) for x in outs[1:]],
        [pltpu.VMEM((G_ROWS, LANES), F32)] * 2,
        10**8,
        par, lattice, energy, force, force_a, force_b, x, other,
    )
    return (result[0].reshape(1), result[1], result[2].transpose(1, 0, 2)) + tuple(result[3:-1]) + (result[-1].reshape(LANES),)


def solution(mesh):
    both = ("dp", "atom")
    return jax.shard_map(
        local,
        mesh=mesh,
        in_specs=(
            P(None, both), P(both), P(None, both), P(both), P(None, None, both), P("dp", None, None), P("dp"),
        ) + (P(),) * 8,
        out_specs=(P("dp"), P(None, both), P("dp", None, None)) + (P(),) * 8,
        check_vma=False,
    )
```
